256 devices in a mesh: pairs: 64 (over z, x, core), mp: 4 (over y).
Axes of the slice: x: 4, y: 4, z: 8, core: 2. Of those that a mesh axis runs over, the one named last changes fastest.
Arguments:
- embeddings: bfloat16 [128, 128, 5120], P('pairs', None, 'mp'), may hold values from -12 to 12
- cotangent: bfloat16 [128, 128, 5120], P('pairs', None, 'mp'), may hold values from -6 to 6
- w_qk: bfloat16 [5120, 512], P('mp'), may hold values from -0.078125 to 0.078125
- w_value: bfloat16 [5120, 512], P('mp'), may hold values from -0.078125 to 0.078125
- w_out: bfloat16 [512, 5120], P(None, 'mp'), may hold values from -0.25 to 0.25
- lengths: int32 [128], replicated, may hold values from 16 to 128
- pair_list: int32 [1024, 2], replicated, may hold values from 0 to 127, as said below
Outputs:
- attended: bfloat16 [128, 128, 5120], P('pairs', None, 'mp')
- grad_qk: float32 [5120, 512], P('mp', 'pairs')
- grad_value: float32 [5120, 512], P('mp', 'pairs')
The draws below stay inside these ranges and needn't reach their ends.
Inputs may be any that keep to these rules, and one draw needn't show every extreme that they name: `pair_list`: protein p belongs to owner p // 2. The pairs in rows w * 16 to (w + 1) * 16 - 1 go to worker w; the 32 proteins named in one worker's pairs belong to 32 different owners.
All inputs are finite; a program needn't handle non-finite values.
Results may differ from the reference program's by a relative error of at most 0.024.
The reference program's roundings to bfloat16 on the way (of `keys`, `values`, `hidden` and `hidden_grad`) count: a program that leaves them out, or rounds other values in their place, can miss the bound.
Values may be sent and summed in bfloat16 or wider, within the bound.
A program may use at most 128 MiB of HBM per device.

```python
import jax
import jax.numpy as jnp
from jax import lax

D = 5120
HEADS = 8
HDIM = 64
CROP = 128
PROT_DEV = 2
PAIR_DEV = 16
PROTEINS = 128
PAIRS = 1024


def draw_embeddings(key, part):
    key = jax.random.fold_in(key, 7)
    first_key = jax.random.fold_in(key, 0)
    shape = (PROTEINS, CROP, D)
    return jnp.clip(jax.random.normal(first_key, shape, jnp.float32), -4.0, 4.0).astype(jnp.bfloat16)


def draw_lengths(key, part):
    key = jax.random.fold_in(key, 5)
    first_key, second_key = jax.random.split(key)
    base = jax.random.randint(first_key, (PROTEINS,), CROP // 8, CROP + 1)
    longest = jax.random.randint(second_key, (), 0, PROTEINS)
    places = jnp.arange(PROTEINS, dtype=jnp.int32)
    return jnp.where(places == longest, CROP, base).astype(jnp.int32)


def draw_pair_list(key, part):
    key = jax.random.fold_in(key, 11)
    owners = PROTEINS // PROT_DEV
    score_key, hub_key, pick_key = jax.random.split(key, 3)
    scores = jax.random.randint(score_key, (owners, owners), 0, 1 << 20) * owners
    scores = scores + jnp.arange(owners, dtype=jnp.int32)[None, :]
    chosen = jnp.argsort(scores, axis=1)[:, :2 * PAIR_DEV].astype(jnp.int32)
    hubs = jax.random.randint(hub_key, (owners,), 0, PROT_DEV)
    picks = jax.random.randint(pick_key, (owners, 2 * PAIR_DEV), 0, 2 * PROT_DEV)
    local = jnp.where(picks < PROT_DEV, picks, hubs[chosen])
    proteins = chosen * PROT_DEV + local
    return proteins.reshape(PAIRS, 2).astype(jnp.int32)


def shard_levels(rng, extent, cuts, smallest, top_value):
    def one(position, blocks):
        draws = jax.random.uniform(jax.random.fold_in(jax.random.fold_in(rng, 6), position), (blocks,), jnp.float32, smallest / len(cuts), top_value / len(cuts))
        return jnp.repeat(jnp.exp(draws), extent[position] // blocks).reshape((-1,) + (1,) * (len(extent) - position - 1))

    loudness = one(*cuts[0])
    for cut in cuts[1:]:
        loudness = loudness * one(*cut)
    return loudness


def centred(stream_key, dims, scale, limit, cuts=(), kind=jnp.bfloat16):
    array = jax.random.normal(stream_key, dims, jnp.float32) * scale
    if len(cuts) > 0:
        array = shard_levels(stream_key, dims, cuts, -0.22, 0.18) * array
    return jnp.clip(array, min=-limit, max=limit).astype(kind)


def setup_inputs(seed: int = 0) -> dict:
    key_list = jax.random.split(jax.random.key(seed), 8)
    return {
        "embeddings": draw_embeddings(jax.random.fold_in(key_list[7], 71), 0),
        "cotangent": centred(key_list[1], (PROTEINS, CROP, D), 1.0, 6.0, ((0, 64), (2, 4))),
        "w_qk": centred(key_list[2], (D, HEADS * HDIM), D ** -0.5, 0.078125, ((0, 4),)),
        "w_value": centred(key_list[3], (D, HEADS * HDIM), D ** -0.5, 0.078125, ((0, 4),)),
        "w_out": centred(key_list[4], (HEADS * HDIM, D), (HEADS * HDIM) ** -0.5, 0.25, ((1, 4),)),
        "lengths": draw_lengths(jax.random.fold_in(key_list[7], 71), 0),
        "pair_list": draw_pair_list(jax.random.fold_in(key_list[7], 71), 0),
    }


def pair_attend(key_a, key_b, value_a, value_b, length_a, length_b):
    crop = key_a.shape[0]
    width = key_a.shape[1]
    heads = width // HDIM
    qa = key_a.reshape(crop, heads, HDIM)
    qb = key_b.reshape(crop, heads, HDIM)
    va = value_a.reshape(crop, heads, HDIM)
    vb = value_b.reshape(crop, heads, HDIM)
    scores = jnp.einsum('rhd,chd->hrc', qa, qb, precision=lax.Precision.HIGHEST) * HDIM ** (-0.5)
    places = jnp.arange(crop, dtype=jnp.int32)
    column_ok = places[None, None, :] < length_b
    row_ok = places[None, :, None] < length_a
    by_rows = jax.nn.softmax(jnp.where(column_ok, scores, -1000000000.0), axis=2)
    by_columns = jax.nn.softmax(jnp.where(row_ok, scores, -1000000000.0), axis=1)
    out_a = jnp.einsum('hrc,chd->rhd', by_rows, vb, precision=lax.Precision.HIGHEST).reshape(crop, width)
    out_b = jnp.einsum('hrc,rhd->chd', by_columns, va, precision=lax.Precision.HIGHEST).reshape(crop, width)
    return (out_a, out_b)

def reference(embeddings, cotangent, w_qk, w_value, w_out, lengths, pair_list):
    count, crop, width = embeddings.shape
    inner = w_qk.shape[1]
    flat = embeddings.reshape(count * crop, width)
    keys = jnp.dot(flat, w_qk, preferred_element_type=jnp.float32).astype(jnp.bfloat16).reshape(count, crop, inner)
    values = jnp.dot(flat, w_value, preferred_element_type=jnp.float32).astype(jnp.bfloat16).reshape(count, crop, inner)
    rows_ok = (jnp.arange(crop, dtype=jnp.int32)[None, :] < lengths[:, None]).astype(jnp.float32)[:, :, None]
    first = pair_list[:, 0]
    second = pair_list[:, 1]

    def forward_one(index):
        a = first[index]
        b = second[index]
        return pair_attend(keys[a].astype(jnp.float32), keys[b].astype(jnp.float32), values[a].astype(jnp.float32), values[b].astype(jnp.float32), lengths[a], lengths[b])
    out_a, out_b = lax.map(forward_one, jnp.arange(pair_list.shape[0], dtype=jnp.int32))
    summed = jnp.zeros((count, crop, inner), jnp.float32).at[first].add(out_a).at[second].add(out_b)
    hidden = (summed * rows_ok).astype(jnp.bfloat16)
    attended = jnp.dot(hidden.reshape(count * crop, inner), w_out, preferred_element_type=jnp.float32)
    attended = attended.astype(jnp.bfloat16).reshape(count, crop, width)
    back = jnp.dot(cotangent.reshape(count * crop, width), w_out.T, preferred_element_type=jnp.float32)
    hidden_grad = (back.reshape(count, crop, inner) * rows_ok).astype(jnp.bfloat16)

    def backward_one(index):
        a = first[index]
        b = second[index]
        la = lengths[a]
        lb = lengths[b]

        def local(ka, kb, va, vb):
            return pair_attend(ka, kb, va, vb, la, lb)
        primal, pull = jax.vjp(local, keys[a].astype(jnp.float32), keys[b].astype(jnp.float32), values[a].astype(jnp.float32), values[b].astype(jnp.float32))
        return pull((hidden_grad[a].astype(jnp.float32), hidden_grad[b].astype(jnp.float32)))
    dka, dkb, dva, dvb = lax.map(backward_one, jnp.arange(pair_list.shape[0], dtype=jnp.int32))
    zeros = jnp.zeros((count, crop, inner), jnp.float32)
    key_grad = zeros.at[first].add(dka).at[second].add(dkb).astype(jnp.bfloat16)
    value_grad = zeros.at[first].add(dva).at[second].add(dvb).astype(jnp.bfloat16)
    grad_qk = jnp.dot(flat.T, key_grad.reshape(count * crop, inner), preferred_element_type=jnp.float32)
    grad_value = jnp.dot(flat.T, value_grad.reshape(count * crop, inner), preferred_element_type=jnp.float32)
    return (attended, grad_qk, grad_value)
```

```python
import functools, math
import jax, jax.numpy as jnp
from jax import lax
from jax.sharding import PartitionSpec as P
from jax.experimental import pallas as pl
from jax.experimental.pallas import tpu as pltpu
HDIM=64
CROP=128
SCALE=HDIM**-0.5*math.log2(math.e)
NT=(((1,),(1,)),((),()))

def pair_kernel(locals_, heads, group, codes_ref, len_ref, first_ref, table_ref, hid_ref, grad_ref, list_ref, count_ref, out_acc, dk_acc, dv_acc):
    slots = codes_ref.shape[0]
    for l in range(locals_ + 1):
        count_ref[l] = 0

    def place(i, carry):
        code = codes_ref[i]
        local = jnp.where(code > 0, (code - 1) // 128, locals_)
        at = count_ref[local]
        list_ref[local, at] = jnp.maximum(code - 1, 0) % 128
        count_ref[local] = at + 1
        return carry

    lax.fori_loop(0, slots, place, 0)
    rows = lax.broadcasted_iota(jnp.int32, (CROP, CROP), 0)
    columns = lax.broadcasted_iota(jnp.int32, (1, CROP), 1)
    for l in range(locals_):
        me = first_ref[0] + l
        row_bias = jnp.where(rows < len_ref[me], 0.0, -1e30)
        count = count_ref[l]
        for extra in range(group):
            list_ref[l, count + extra] = 0
        for h in range(heads):
            own = table_ref[me * heads + h].astype(jnp.float32)
            kp = own[:HDIM].T.astype(jnp.bfloat16)
            vp = own[HDIM:2 * HDIM].T.astype(jnp.bfloat16)
            gp = own[2 * HDIM:].T.astype(jnp.bfloat16)
            out_acc[...] = jnp.zeros_like(out_acc)
            dk_acc[...] = jnp.zeros_like(dk_acc)
            dv_acc[...] = jnp.zeros_like(dv_acc)

            def step(i, carry):
                blocks, lens, live = [], [], []
                for j in range(group):
                    q = list_ref[l, i * group + j]
                    blocks.append(table_ref[q * heads + h])
                    lens.append(len_ref[q])
                    live.append(jnp.where(i * group + j < count, 1.0, 0.0))
                many = jnp.concatenate(blocks, axis=1)
                kq, vq, gq = many[:HDIM], many[HDIM:2 * HDIM], many[2 * HDIM:]
                scores = jnp.dot(kp, kq, preferred_element_type=jnp.float32)
                d_rows = jnp.dot(gp, vq, preferred_element_type=jnp.float32)
                d_cols = jnp.dot(vp, gq, preferred_element_type=jnp.float32)
                a_parts, b_parts, ds_parts = [], [], []
                for j in range(group):
                    part = slice(j * CROP, (j + 1) * CROP)
                    s = scores[:, part] * SCALE
                    sa = s + jnp.where(columns < lens[j], 0.0, -1e30)
                    ea = jnp.exp2(sa - jnp.max(sa, axis=1, keepdims=True))
                    a = ea * (live[j] / jnp.sum(ea, axis=1, keepdims=True))
                    sb = s + row_bias
                    eb = jnp.exp2(sb - jnp.max(sb, axis=0, keepdims=True))
                    b = eb * (live[j] / jnp.sum(eb, axis=0, keepdims=True))
                    da = d_rows[:, part]
                    db = d_cols[:, part]
                    ta = a * da
                    tb = b * db
                    ds = (ta - a * jnp.sum(ta, axis=1, keepdims=True)) + (tb - b * jnp.sum(tb, axis=0, keepdims=True))
                    a_parts.append(a.astype(jnp.bfloat16))
                    b_parts.append(b.astype(jnp.bfloat16))
                    ds_parts.append(ds.astype(jnp.bfloat16))
                cat = lambda x: jnp.concatenate(x, axis=1)
                out_acc[...] += lax.dot_general(cat(a_parts), vq, NT, preferred_element_type=jnp.float32)
                dv_acc[...] += lax.dot_general(cat(b_parts), gq, NT, preferred_element_type=jnp.float32)
                dk_acc[...] += lax.dot_general(cat(ds_parts), kq, NT, preferred_element_type=jnp.float32)
                return carry

            lax.fori_loop(0, (count + group - 1) // group, step, 0)
            ok = rows[:, :HDIM] < len_ref[me]
            hid_ref[l * heads + h] = jnp.where(ok, out_acc[...], 0.0).astype(jnp.bfloat16)
            grad_ref[l * heads + h] = jnp.concatenate([dk_acc[...] * HDIM ** -0.5, dv_acc[...]], axis=1).astype(jnp.bfloat16)

def pairs_call(codes, lengths, first, table, locals_, heads, group=2):
    units = locals_ * heads
    smem = pl.BlockSpec(memory_space=pltpu.SMEM)
    vmem = pl.BlockSpec(memory_space=pltpu.VMEM)
    return pl.pallas_call(
        functools.partial(pair_kernel, locals_, heads, group),
        out_shape=(jax.ShapeDtypeStruct((units, CROP, HDIM), jnp.bfloat16),
                   jax.ShapeDtypeStruct((units, CROP, 2 * HDIM), jnp.bfloat16)),
        in_specs=[smem, smem, smem, vmem],
        out_specs=(vmem, vmem),
        scratch_shapes=[pltpu.SMEM((locals_ + 1, 128 + 8), jnp.int32), pltpu.SMEM((locals_ + 1,), jnp.int32),
                        pltpu.VMEM((CROP, HDIM), jnp.float32), pltpu.VMEM((CROP, HDIM), jnp.float32), pltpu.VMEM((CROP, HDIM), jnp.float32)],
        compiler_params=pltpu.CompilerParams(vmem_limit_bytes=48 * 1024 * 1024),
    )(codes, lengths, first, table)


def on_device(embeddings, cotangent, w_qk, w_value, w_out, lengths, pair_list):
    owned, crop, width = embeddings.shape
    inner = w_qk.shape[1]
    groups = lax.axis_size("mp")
    group_cols = inner // groups
    heads = group_cols // HDIM
    rows = owned * crop
    flat = embeddings.reshape(rows, width)
    stacked = jnp.stack(
        (w_qk.reshape(width, groups, group_cols), w_value.reshape(width, groups, group_cols)),
        axis=2,
    )
    stacked = stacked.reshape(width, 2 * inner)
    partial_kv = jnp.dot(flat, stacked, preferred_element_type=jnp.float32)
    key_value = lax.psum_scatter(partial_kv, "mp", scatter_dimension=1, tiled=True).astype(jnp.bfloat16)
    me = lax.axis_index("pairs")
    workers = lax.axis_size("pairs")
    my_lengths = lax.dynamic_slice_in_dim(lengths, me * owned, owned, 0)
    rows_ok = (jnp.arange(crop, dtype=jnp.int32)[None, :] < my_lengths[:, None]).astype(jnp.float32)[:, :, None]
    partial_back = lax.dot_general(
        cotangent.reshape(rows, width), w_out, (((1,), (1,)), ((), ())), preferred_element_type=jnp.float32
    )
    head_back = (
        lax.psum_scatter(partial_back.astype(jnp.bfloat16), "mp", scatter_dimension=1, tiled=True)
        .astype(jnp.float32)
        .reshape(owned, crop, group_cols)
    )
    hidden_grad = (head_back * rows_ok).astype(jnp.bfloat16)
    both = jnp.concatenate(
        [key_value.reshape(owned, crop, 2, heads, HDIM), hidden_grad.reshape(owned, crop, 1, heads, HDIM)], axis=2
    )
    block = both.transpose(0, 3, 2, 4, 1).reshape(owned * heads, 3 * HDIM, crop)
    table = lax.all_gather(block, "pairs", axis=0, tiled=True)
    named = pair_list.reshape(workers, -1)
    partner = pair_list[:, ::-1].reshape(workers, -1)
    codes = jnp.sum(jnp.where(named // owned == me, 1 + (named % owned) * 128 + partner, 0), axis=1).astype(jnp.int32)
    hidden, grads = pairs_call(codes, lengths, (me * owned).reshape(1), table, owned, heads, 4)
    hidden = hidden.reshape(owned, heads, crop, HDIM).transpose(0, 2, 1, 3).reshape(owned, crop, group_cols)
    all_heads = lax.all_gather(hidden, "mp", axis=2, tiled=True)
    attended = jnp.dot(all_heads.reshape(rows, inner), w_out, preferred_element_type=jnp.float32)
    attended = attended.astype(jnp.bfloat16).reshape(owned, crop, width)
    grads = grads.reshape(owned, heads, crop, 2, HDIM).transpose(0, 2, 3, 1, 4).reshape(owned, crop, 2 * group_cols)
    all_grads = lax.all_gather(grads, "mp", axis=2, tiled=True).reshape(rows, 2 * inner)
    terms = lax.dot_general(all_grads, flat, (((0,), (0,)), ((), ())), preferred_element_type=jnp.float32)
    terms = terms.reshape(groups, 2, group_cols, width).transpose(1, 0, 2, 3).reshape(2, workers, inner // workers, width)
    terms = terms.transpose(1, 0, 2, 3).astype(jnp.bfloat16)
    arrived = lax.all_to_all(terms, "pairs", split_axis=0, concat_axis=0, tiled=True)
    total = jnp.sum(arrived.astype(jnp.float32), axis=0)
    return (attended, total[0].T, total[1].T)


def solution(mesh):
    in_specs = (
        P("pairs", None, "mp"),
        P("pairs", None, "mp"),
        P("mp", None),
        P("mp", None),
        P(None, "mp"),
        P(),
        P(),
    )
    out_specs = (P("pairs", None, "mp"), P("mp", "pairs"), P("mp", "pairs"))
    return jax.shard_map(on_device, mesh=mesh, in_specs=in_specs, out_specs=out_specs, check_vma=False)
```

```python
import functools
import math

import jax
import jax.numpy as jnp
from jax import lax
from jax.experimental import pallas as pl
from jax.experimental.pallas import tpu as pltpu
from jax.sharding import PartitionSpec as P

HDIM = 64
CROP = 128
SCALE = HDIM**-0.5 * math.log2(math.e)
NT = (((1,), (1,)), ((), ()))
NZ, NX, NY = 8, 4, 4
CHIPS = NZ * NX
LOCALS = 4
GROUP = 4
MESH = pl.DeviceIdType.MESH
VMEM_LIMIT = 56 * 1024 * 1024


def place():
    me = lax.axis_index("pairs")
    chip = me // 2
    return chip // NX, chip % NX, me % 2, lax.axis_index("mp")


def device(z, x, c, y):
    return ((z * NX + x) * 2 + c, y)


def remote(src, dst, send, recv, to):
    return pltpu.make_async_remote_copy(
        src_ref=src, dst_ref=dst, send_sem=send, recv_sem=recv, device_id=to, device_id_type=MESH
    )


def greet(others):
    barrier = pltpu.get_barrier_semaphore()
    for other in others:
        pl.semaphore_signal(barrier, inc=1, device_id=other, device_id_type=MESH)
    pl.semaphore_wait(barrier, len(others))


def swap_halves(value):
    return pltpu.roll(value, HDIM, 1)


def gather_kernel(
    len_ref, emb_ref, cot_ref, wq_ref, wv_ref, wo_ref, table_ref, sib_ref,
    kv_send, kv_recv, g_send, g_recv, block, kv_ssem, kv_rsem, g_ssem, g_rsem, ssem, rsem, lsem,
):
    z, x, c, y = place()
    chip = z * NX + x
    mine = y * 2 + c
    column = [device(z, x, cd, (y + d) % NY) for d in (1, 2, 3) for cd in (0, 1)]
    sibling = device(z, x, 1 - c, y)
    up, down = (z + 1) % NZ, (z + NZ - 1) % NZ
    east, west = (x + 1) % NX, (x + NX - 1) % NX
    ring = [device(up, x, c, y), device(down, x, c, y), device(z, east, c, y), device(z, west, c, y)]
    greet(column + [sibling] + ring)

    share = remote(emb_ref, sib_ref, lsem.at[1], lsem.at[2], sibling)
    share.start()

    low = lax.broadcasted_iota(jnp.int32, (2 * CROP, 2 * HDIM), 1) < HDIM

    def pieces(yd):
        at = pl.ds(pl.multiple_of(yd * 2 * HDIM, 2 * HDIM), 2 * HDIM)
        k = jnp.dot(emb_ref[...], wq_ref[:, at], preferred_element_type=jnp.float32)
        v = jnp.dot(emb_ref[...], wv_ref[:, at], preferred_element_type=jnp.float32)
        g = lax.dot_general(cot_ref[...], wo_ref[at, :], NT, preferred_element_type=jnp.float32)
        first, second = g[:CROP], g[CROP:]
        half = low[:CROP]
        kv = (jnp.where(low, k, swap_halves(v)), jnp.where(low, swap_halves(k), v))
        gg = (
            jnp.where(half, first, swap_halves(second)).astype(jnp.bfloat16),
            jnp.where(half, swap_halves(first), second).astype(jnp.bfloat16),
        )
        return kv, gg

    def kv_copy(slot, to):
        return remote(kv_send.at[slot], kv_recv.at[mine], kv_ssem.at[slot], kv_rsem.at[mine], to)

    def g_copy(slot, to):
        return remote(g_send.at[slot], g_recv.at[mine], g_ssem.at[slot], g_rsem.at[mine], to)

    def away(step, carry):
        d = jnp.where(step == 0, 2, jnp.where(step == 1, 1, 3))
        yd = (y + d) % NY
        kv, gg = pieces(yd)
        for cd in (0, 1):
            slot = yd * 2 + cd
            kv_send[slot] = kv[cd]
            g_send[slot] = gg[cd]
            kv_copy(slot, device(z, x, cd, yd)).start()
            g_copy(slot, device(z, x, cd, yd)).start()
        return carry

    lax.fori_loop(0, 3, away, 0)
    kv, gg = pieces(y)
    other = y * 2 + 1 - c
    kv_send[other] = jnp.where(c == 0, kv[1], kv[0])
    g_send[other] = jnp.where(c == 0, gg[1], gg[0])
    kv_copy(other, sibling).start()
    g_copy(other, sibling).start()
    kv_recv[mine] = jnp.where(c == 0, kv[0], kv[1])
    g_recv[mine] = jnp.where(c == 0, gg[0], gg[1])

    def arrive(step, carry):
        slot = (mine + step) % (2 * NY)
        remote(kv_send.at[slot], kv_recv.at[slot], kv_ssem.at[slot], kv_rsem.at[slot], sibling).wait_recv()
        remote(g_send.at[slot], g_recv.at[slot], g_ssem.at[slot], g_rsem.at[slot], sibling).wait_recv()
        return carry

    lax.fori_loop(1, 2 * NY, arrive, 0)
    lanes = lax.broadcasted_iota(jnp.int32, (HDIM, CROP), 1)
    for cs in (0, 1):
        kv_sum = (kv_recv[cs] + kv_recv[2 + cs]) + (kv_recv[4 + cs] + kv_recv[6 + cs])
        g_sum = (g_recv[cs].astype(jnp.float32) + g_recv[2 + cs].astype(jnp.float32)) + (
            g_recv[4 + cs].astype(jnp.float32) + g_recv[6 + cs].astype(jnp.float32)
        )
        g_turned = g_sum.T
        for j in (0, 1):
            p = cs * 2 + j
            block[p, : 2 * HDIM] = kv_sum[j * CROP : (j + 1) * CROP].T.astype(jnp.bfloat16)
            ok = lanes < len_ref[chip * LOCALS + p]
            block[p, 2 * HDIM :] = jnp.where(ok, g_turned[j * HDIM : (j + 1) * HDIM], 0.0).astype(jnp.bfloat16)

    keep = pltpu.make_async_copy(block, table_ref.at[pl.ds(chip * LOCALS, LOCALS)], lsem.at[0])
    keep.start()
    sent = []

    def part(bz, bx, half):
        at = (bz * NX + bx) * LOCALS
        if half is None:
            return table_ref.at[pl.ds(at, LOCALS)]
        return table_ref.at[pl.ds(at + half * (LOCALS // 2), LOCALS // 2)]

    def push(bz, bx, half, to, own=False):
        sem = rsem.at[bz * NX + bx, half or 0]
        src = block if own else part(bz, bx, half)
        copy = remote(src, part(bz, bx, half), ssem.at[len(sent)], sem, device(to[0], to[1], c, y))
        copy.start()
        sent.append(copy)

    def landed(bz, bx, half=None):
        ref = part(bz, bx, half)
        remote(ref, ref, ssem.at[0], rsem.at[bz * NX + bx, half or 0], device(up, x, c, y)).wait_recv()

    def cross(bz):
        landed(bz, west)
        push(bz, west, 0, (z, east))
        landed(bz, east)
        push(bz, east, 1, (z, west))

    @pl.when(c == 0)
    def _():
        sent.clear()
        for to in ((z, east), (z, west), (up, x), (down, x)):
            push(z, x, None, to, own=True)
        ready = [z]
        for s in range(1, NZ // 2 + 1):
            lo, hi = (z + NZ - s) % NZ, (z + s) % NZ
            fresh = [lo, hi]
            if s < NZ // 2:
                for bz, to, half in ((lo, up, 0), (hi, down, 1)):
                    landed(bz, x)
                    push(bz, x, None if s < NZ // 2 - 1 else half, (to, x))
                    push(bz, x, None, (z, east))
                    push(bz, x, None, (z, west))
            else:
                fresh = [lo]
                landed(lo, x, 0)
                landed(lo, x, 1)
                push(lo, x, None, (z, east))
                push(lo, x, None, (z, west))
            for bz in ready:
                cross(bz)
            ready = fresh
        for bz in ready:
            cross(bz)
        for bz in range(NZ):
            landed(bz, (x + 2) % NX, 0)
            landed(bz, (x + 2) % NX, 1)
        for copy in sent:
            copy.wait_send()

    @pl.when(c == 1)
    def _():
        sent.clear()
        for to in ((up, x), (down, x), (z, east), (z, west)):
            push(z, x, None, to, own=True)
        for bx, to, half in ((west, east, 0), (east, west, 1)):
            landed(z, bx)
            push(z, bx, half, (z, to))
            push(z, bx, None, (up, x))
            push(z, bx, None, (down, x))
        far = (x + 2) % NX
        landed(z, far, 0)
        landed(z, far, 1)
        push(z, far, None, (up, x))
        push(z, far, None, (down, x))
        for s in range(1, NZ // 2 + 1):
            lo, hi = (z + NZ - s) % NZ, (z + s) % NZ
            for bx in (x, west, east, far):
                if s < NZ // 2:
                    last = s == NZ // 2 - 1
                    landed(lo, bx)
                    push(lo, bx, 0 if last else None, (up, x))
                    landed(hi, bx)
                    push(hi, bx, 1 if last else None, (down, x))
                else:
                    landed(lo, bx, 0)
                    landed(lo, bx, 1)
        for copy in sent:
            copy.wait_send()

    def leave(step, carry):
        slot = (mine + step) % (2 * NY)
        kv_copy(slot, sibling).wait_send()
        g_copy(slot, sibling).wait_send()
        return carry

    lax.fori_loop(1, 2 * NY, leave, 0)
    keep.wait()
    share.wait()


def gather_call(lengths, emb, cot, w_qk, w_value, w_out):
    rows, width = emb.shape
    smem = pl.BlockSpec(memory_space=pltpu.SMEM)
    vmem = pl.BlockSpec(memory_space=pltpu.VMEM)
    hbm = pl.BlockSpec(memory_space=pl.ANY)
    dma = pltpu.SemaphoreType.DMA
    return pl.pallas_call(
        gather_kernel,
        out_shape=(
            jax.ShapeDtypeStruct((CHIPS * LOCALS, 3 * HDIM, CROP), jnp.bfloat16),
            jax.ShapeDtypeStruct((rows, width), jnp.bfloat16),
        ),
        in_specs=[smem] + [vmem] * 5,
        out_specs=(hbm, hbm),
        scratch_shapes=[
            pltpu.VMEM((2 * NY, rows, 2 * HDIM), jnp.float32),
            pltpu.VMEM((2 * NY, rows, 2 * HDIM), jnp.float32),
            pltpu.VMEM((2 * NY, CROP, 2 * HDIM), jnp.bfloat16),
            pltpu.VMEM((2 * NY, CROP, 2 * HDIM), jnp.bfloat16),
            pltpu.VMEM((LOCALS, 3 * HDIM, CROP), jnp.bfloat16),
            dma((2 * NY,)),
            dma((2 * NY,)),
            dma((2 * NY,)),
            dma((2 * NY,)),
            dma((48,)),
            dma((CHIPS, 2)),
            dma((3,)),
        ],
        compiler_params=pltpu.CompilerParams(
            collective_id=0, has_side_effects=True, vmem_limit_bytes=VMEM_LIMIT
        ),
    )(lengths, emb, cot, w_qk, w_value, w_out)


def pair_kernel(codes_ref, len_ref, first_ref, table_ref, hid_ref, grad_ref, list_ref, count_ref, out_acc, dk_acc, dv_acc):
    for l in range(LOCALS + 1):
        count_ref[l] = 0

    def sort(i, carry):
        code = codes_ref[i]
        local = jnp.where(code > 0, (code - 1) // CROP, LOCALS)
        at = count_ref[local]
        list_ref[local, at] = jnp.maximum(code - 1, 0) % CROP
        count_ref[local] = at + 1
        return carry

    lax.fori_loop(0, codes_ref.shape[0], sort, 0)
    rows = lax.broadcasted_iota(jnp.int32, (CROP, CROP), 0)
    columns = lax.broadcasted_iota(jnp.int32, (1, CROP), 1)
    for l in range(LOCALS):
        me = first_ref[0] + l
        row_bias = jnp.where(rows < len_ref[me], 0.0, -1e30)
        count = count_ref[l]
        for extra in range(GROUP):
            list_ref[l, count + extra] = 0
        own = table_ref[me].astype(jnp.float32)
        kp = own[:HDIM].T.astype(jnp.bfloat16)
        vp = own[HDIM : 2 * HDIM].T.astype(jnp.bfloat16)
        gp = own[2 * HDIM :].T.astype(jnp.bfloat16)
        out_acc[...] = jnp.zeros_like(out_acc)
        dk_acc[...] = jnp.zeros_like(dk_acc)
        dv_acc[...] = jnp.zeros_like(dv_acc)

        def step(i, carry):
            blocks, lens, live = [], [], []
            for j in range(GROUP):
                q = list_ref[l, i * GROUP + j]
                blocks.append(table_ref[q])
                lens.append(len_ref[q])
                live.append(jnp.where(i * GROUP + j < count, 1.0, 0.0))
            many = jnp.concatenate(blocks, axis=1)
            kq, vq, gq = many[:HDIM], many[HDIM : 2 * HDIM], many[2 * HDIM :]
            scores = jnp.dot(kp, kq, preferred_element_type=jnp.float32)
            d_rows = jnp.dot(gp, vq, preferred_element_type=jnp.float32)
            d_cols = jnp.dot(vp, gq, preferred_element_type=jnp.float32)
            a_parts, b_parts, ds_parts = [], [], []
            for j in range(GROUP):
                part = slice(j * CROP, (j + 1) * CROP)
                s = scores[:, part] * SCALE
                sa = s + jnp.where(columns < lens[j], 0.0, -1e30)
                ea = jnp.exp2(sa - jnp.max(sa, axis=1, keepdims=True))
                a = ea * (live[j] / jnp.sum(ea, axis=1, keepdims=True))
                sb = s + row_bias
                eb = jnp.exp2(sb - jnp.max(sb, axis=0, keepdims=True))
                b = eb * (live[j] / jnp.sum(eb, axis=0, keepdims=True))
                ta = a * d_rows[:, part]
                tb = b * d_cols[:, part]
                ds = (ta - a * jnp.sum(ta, axis=1, keepdims=True)) + (
                    tb - b * jnp.sum(tb, axis=0, keepdims=True)
                )
                a_parts.append(a.astype(jnp.bfloat16))
                b_parts.append(b.astype(jnp.bfloat16))
                ds_parts.append(ds.astype(jnp.bfloat16))
            for acc, parts, other in ((out_acc, a_parts, vq), (dv_acc, b_parts, gq), (dk_acc, ds_parts, kq)):
                acc[...] += lax.dot_general(
                    jnp.concatenate(parts, axis=1), other, NT, preferred_element_type=jnp.float32
                )
            return carry

        lax.fori_loop(0, (count + GROUP - 1) // GROUP, step, 0)
        ok = rows[:, :HDIM] < len_ref[me]
        hid_ref[l // 2, :, (l % 2) * HDIM : (l % 2 + 1) * HDIM] = jnp.where(ok, out_acc[...], 0.0).astype(
            jnp.bfloat16
        )
        turned = jnp.concatenate([dk_acc[...] * HDIM**-0.5, dv_acc[...]], axis=1).T
        for core in range(2):
            eights = []
            for xd in range(NX):
                at = (xd * 2 + core) * 8
                eights += [turned[at : at + 8], turned[HDIM + at : HDIM + at + 8]]
            grad_ref[core, :, l * CROP : (l + 1) * CROP] = jnp.concatenate(eights, axis=0).astype(jnp.bfloat16)


def pair_call(codes, lengths, first, table):
    smem = pl.BlockSpec(memory_space=pltpu.SMEM)
    vmem = pl.BlockSpec(memory_space=pltpu.VMEM)
    return pl.pallas_call(
        pair_kernel,
        out_shape=(
            jax.ShapeDtypeStruct((2, CROP, 2 * HDIM), jnp.bfloat16),
            jax.ShapeDtypeStruct((2, HDIM, LOCALS * CROP), jnp.bfloat16),
        ),
        in_specs=[smem, smem, smem, vmem],
        out_specs=(vmem, vmem),
        scratch_shapes=[
            pltpu.SMEM((LOCALS + 1, 2 * CROP), jnp.int32),
            pltpu.SMEM((LOCALS + 1,), jnp.int32),
            pltpu.VMEM((CROP, HDIM), jnp.float32),
            pltpu.VMEM((CROP, HDIM), jnp.float32),
            pltpu.VMEM((CROP, HDIM), jnp.float32),
        ],
        compiler_params=pltpu.CompilerParams(vmem_limit_bytes=VMEM_LIMIT),
    )(codes, lengths, first, table)


def ring_sum(n, term, plus, minus, send, recv, ssem, rsem, between=None):
    steps = n // 2
    half = send.shape[-1] // 2
    sent = []
    for s in range(steps):
        d = steps - s
        for way, to in ((0, plus), (1, minus)):
            value = term(d if way == 0 else n - d)
            spot = slice(way * half, (way + 1) * half) if s == 0 else slice(None)
            if s == 0:
                send[way, s, :, spot] = value[:, spot].astype(jnp.bfloat16)
            else:
                back = slice(way * half, (way + 1) * half) if s == 1 else slice(None)
                landing = recv.at[way, s - 1, :, back]
                remote(landing, landing, ssem.at[way, s - 1], rsem.at[way, s - 1], to).wait_recv()
                if s == 1:
                    send[way, s] = value.astype(jnp.bfloat16)
                    send[way, s, :, back] = (value[:, back] + recv[way, 0, :, back].astype(jnp.float32)).astype(
                        jnp.bfloat16
                    )
                else:
                    send[way, s] = (value + recv[way, s - 1].astype(jnp.float32)).astype(jnp.bfloat16)
            copy = remote(
                send.at[way, s, :, spot], recv.at[way, s, :, spot], ssem.at[way, s], rsem.at[way, s], to
            )
            copy.start()
            sent.append(copy)
        if s == 0 and between is not None:
            between()
    total = term(0)
    for way, to in ((0, plus), (1, minus)):
        landing = recv.at[way, steps - 1]
        remote(landing, landing, ssem.at[way, steps - 1], rsem.at[way, steps - 1], to).wait_recv()
        total = total + recv[way, steps - 1].astype(jnp.float32)
    for copy in sent:
        copy.wait_send()
    return total


def finish_kernel(
    hid_ref, grad_ref, emb_ref, sib_ref, wo_ref, att_ref, sum_ref,
    hid_recv, g_recv, terms, hidden, z0_send, z0_recv, x0_send, x0_recv, x1_send, x1_recv, z1_send, z1_recv, held,
    h_ssem, h_rsem, g_ssem, g_rsem, zs_sem, zr_sem, xs_sem, xr_sem,
):
    z, x, c, y = place()
    mine = y * 2 + c
    column = [(cd, d) for d in (2, 1, 3) for cd in (0, 1)]
    sibling = device(z, x, 1 - c, y)
    up, down = device((z + 1) % NZ, x, c, y), device((z + NZ - 1) % NZ, x, c, y)
    east, west = device(z, (x + 1) % NX, c, y), device(z, (x + NX - 1) % NX, c, y)
    greet([device(z, x, cd, (y + d) % NY) for cd, d in column] + [sibling, up, down, east, west])

    def copies(cd, yd):
        slot = yd * 2 + cd
        to = device(z, x, cd, yd)
        return (
            remote(grad_ref.at[cd], g_recv.at[mine], g_ssem.at[slot], g_rsem.at[mine], to),
            remote(hid_ref.at[cd], hid_recv.at[mine], h_ssem.at[slot], h_rsem.at[mine], to),
        )

    outgoing = [copies(cd, (y + d) % NY) for cd, d in column] + [copies(1 - c, y)]
    for kind in (0, 1):
        for copy in outgoing:
            copy[kind].start()
    g_recv[mine] = grad_ref[c]
    hid_recv[mine] = hid_ref[c]

    def arrive_g(step, carry):
        slot = (mine + step) % (2 * NY)
        remote(g_recv.at[slot], g_recv.at[slot], g_ssem.at[slot], g_rsem.at[slot], sibling).wait_recv()
        return carry

    lax.fori_loop(1, 2 * NY, arrive_g, 0)
    spots = 2 * NY * HDIM
    all_g = g_recv[...].reshape(spots, 4 * CROP)
    own = jnp.where(c == 0, all_g[:, : 2 * CROP], all_g[:, 2 * CROP :])
    theirs = jnp.where(c == 0, all_g[:, 2 * CROP :], all_g[:, : 2 * CROP])
    terms[...] = (
        jnp.dot(own, emb_ref[...], preferred_element_type=jnp.float32)
        + jnp.dot(theirs, sib_ref[...], preferred_element_type=jnp.float32)
    ).reshape(terms.shape)

    def attend():
        def arrive_h(step, carry):
            slot = (mine + step) % (2 * NY)
            remote(hid_recv.at[slot], hid_recv.at[slot], h_ssem.at[slot], h_rsem.at[slot], sibling).wait_recv()
            return carry

        lax.fori_loop(1, 2 * NY, arrive_h, 0)
        low = lax.broadcasted_iota(jnp.int32, (CROP, 2 * HDIM), 1) < HDIM
        for yy in range(NY):
            even = hid_recv[2 * yy].astype(jnp.float32)
            odd = hid_recv[2 * yy + 1].astype(jnp.float32)
            at = slice(yy * 2 * HDIM, (yy + 1) * 2 * HDIM)
            hidden[:CROP, at] = jnp.where(low, even, swap_halves(odd)).astype(jnp.bfloat16)
            hidden[CROP:, at] = jnp.where(low, swap_halves(even), odd).astype(jnp.bfloat16)
        att_ref[...] = jnp.dot(hidden[...], wo_ref[...], preferred_element_type=jnp.float32).astype(jnp.bfloat16)

    @pl.when(c == 0)
    def _():
        line = ring_sum(
            NZ,
            lambda d: terms[(z + d) % NZ].reshape(HDIM, terms.shape[-1]),
            up, down, z0_send, z0_recv, zs_sem, zr_sem, attend,
        )
        held[...] = line.reshape(held.shape)
        sum_ref[...] = ring_sum(
            NX, lambda d: held[(x + d) % NX], east, west, x0_send, x0_recv, xs_sem, xr_sem
        )

    @pl.when(c == 1)
    def _():
        plane = ring_sum(
            NX,
            lambda d: terms[:, (x + d) % NX].reshape(NZ * 16, terms.shape[-1]),
            east, west, x1_send, x1_recv, xs_sem, xr_sem, attend,
        )
        terms[:, 0] = plane.reshape(NZ, 16, terms.shape[-1])
        sum_ref[...] = ring_sum(
            NZ, lambda d: terms[(z + d) % NZ, 0], up, down, z1_send, z1_recv, zs_sem, zr_sem
        )

    for pair in outgoing:
        for copy in pair:
            copy.wait_send()


def finish_call(hid, grads, emb, sib, w_out):
    rows, width = emb.shape
    vmem = pl.BlockSpec(memory_space=pltpu.VMEM)
    dma = pltpu.SemaphoreType.DMA
    bf = jnp.bfloat16
    return pl.pallas_call(
        finish_kernel,
        out_shape=(
            jax.ShapeDtypeStruct((rows, width), bf),
            jax.ShapeDtypeStruct((16, width), jnp.float32),
        ),
        in_specs=[vmem] * 5,
        out_specs=(vmem, vmem),
        scratch_shapes=[
            pltpu.VMEM((2 * NY, CROP, 2 * HDIM), bf),
            pltpu.VMEM((2 * NY, HDIM, 4 * CROP), bf),
            pltpu.VMEM((NZ, NX, 16, width), jnp.float32),
            pltpu.VMEM((2 * CROP, 2 * NY * HDIM), bf),
            pltpu.VMEM((2, NZ // 2, HDIM, width), bf),
            pltpu.VMEM((2, NZ // 2, HDIM, width), bf),
            pltpu.VMEM((2, NX // 2, 16, width), bf),
            pltpu.VMEM((2, NX // 2, 16, width), bf),
            pltpu.VMEM((2, NX // 2, NZ * 16, width), bf),
            pltpu.VMEM((2, NX // 2, NZ * 16, width), bf),
            pltpu.VMEM((2, NZ // 2, 16, width), bf),
            pltpu.VMEM((2, NZ // 2, 16, width), bf),
            pltpu.VMEM((NX, 16, width), jnp.float32),
            dma((2 * NY,)),
            dma((2 * NY,)),
            dma((2 * NY,)),
            dma((2 * NY,)),
            dma((2, NZ // 2)),
            dma((2, NZ // 2)),
            dma((2, NX // 2)),
            dma((2, NX // 2)),
        ],
        compiler_params=pltpu.CompilerParams(
            collective_id=1, has_side_effects=True, vmem_limit_bytes=VMEM_LIMIT
        ),
    )(hid, grads, emb, sib, w_out)


def on_device(embeddings, cotangent, w_qk, w_value, w_out, lengths, pair_list):
    owned, crop, width = embeddings.shape
    rows = owned * crop
    emb = embeddings.reshape(rows, width)
    chip = lax.axis_index("pairs") // 2
    named = pair_list.reshape(lax.axis_size("pairs"), -1)
    partner = pair_list[:, ::-1].reshape(named.shape)
    owner = 2 * chip + jnp.arange(2, dtype=jnp.int32)[:, None, None]
    codes = jnp.where(named[None] // owned == owner, 1 + (named[None] - 4 * chip) * CROP + partner[None], 0)
    codes = jnp.sum(codes, axis=2).astype(jnp.int32).reshape(-1)
    table, sib = gather_call(lengths, emb, cotangent.reshape(rows, width), w_qk, w_value, w_out)
    hid, grads = pair_call(codes, lengths, (LOCALS * chip).reshape(1), table)
    attended, sums = finish_call(hid, grads, emb, sib, w_out)
    return (attended.reshape(embeddings.shape), sums[:8].T, sums[8:].T)


def solution(mesh):
    in_specs = (
        P("pairs", None, "mp"),
        P("pairs", None, "mp"),
        P("mp", None),
        P("mp", None),
        P(None, "mp"),
        P(),
        P(),
    )
    out_specs = (P("pairs", None, "mp"), P("mp", "pairs"), P("mp", "pairs"))
    return jax.shard_map(on_device, mesh=mesh, in_specs=in_specs, out_specs=out_specs, check_vma=False)
```

```python
import math

import jax
import jax.numpy as jnp
from jax import lax
from jax.experimental import pallas as pl
from jax.experimental.pallas import tpu as pltpu
from jax.sharding import PartitionSpec as P

HDIM = 64
CROP = 128
SCALE = HDIM**-0.5 * math.log2(math.e)
NT = (((1,), (1,)), ((), ()))
NZ, NX, NY = 8, 4, 4
CHIPS = NZ * NX
LOCALS = 4
HEADS = 2 * NY
MESH = pl.DeviceIdType.MESH
VMEM_LIMIT = 56 * 1024 * 1024


def place():
    me = lax.axis_index("pairs")
    chip = me // 2
    return chip // NX, chip % NX, me % 2, lax.axis_index("mp")


def device(z, x, c, y):
    return ((z * NX + x) * 2 + c, y)


def column_of(x, c):
    return jnp.where(c == x // 2, x, NX - 1 - x)


def mate_of(x):
    return x + 1 - 2 * (x % 2)


def remote(src, dst, send, recv, to):
    return pltpu.make_async_remote_copy(
        src_ref=src, dst_ref=dst, send_sem=send, recv_sem=recv, device_id=to, device_id_type=MESH
    )


def greet(others):
    barrier = pltpu.get_barrier_semaphore()
    for other in others:
        pl.semaphore_signal(barrier, inc=1, device_id=other, device_id_type=MESH)
    pl.semaphore_wait(barrier, len(others))


def gather_kernel(
    len_ref, pairs_ref, emb_hbm, cot_hbm, wq_hbm, wv_hbm, wo_hbm, table_ref, sib_ref, codes_ref,
    emb, cot, wq, wv, wo, k_send, k_recv, vg_send, vg_recv, block, seed,
    lsem, k_ssem, k_rsem, vg_ssem, vg_rsem, bsem, ssem, rsem,
):
    z, x, c, y = place()
    mine = y * 2 + c
    sibling = device(z, x, 1 - c, y)
    partner = device(z, NX - 1 - x, 1 - c, y)
    mate = device(z, mate_of(x), c, y)
    up, down = device((z + 1) % NZ, x, c, y), device((z + NZ - 1) % NZ, x, c, y)
    col, mate_col = column_of(x, c), column_of(mate_of(x), c)
    sib_col, sib_mate_col = column_of(x, 1 - c), column_of(mate_of(x), 1 - c)
    kept = c == x // 2

    loads = [
        pltpu.make_async_copy(src, dst, lsem.at[i])
        for i, (src, dst) in enumerate(
            ((emb_hbm, emb), (wq_hbm, wq), (wv_hbm, wv), (cot_hbm, cot), (wo_hbm, wo))
        )
    ]
    for load in loads:
        load.start()
    greet(
        [device(z, x, cd, (y + d) % NY) for d in (1, 2, 3) for cd in (0, 1)] + [sibling, partner, mate, up, down]
    )
    for load in loads:
        load.wait()
    share = remote(emb, sib_ref, lsem.at[5], lsem.at[6], sibling)
    share.start()

    def copies(j, slot, to):
        return (
            remote(k_send.at[j, slot], k_recv.at[j, mine], k_ssem.at[j, slot], k_rsem.at[j, mine], to),
            remote(vg_send.at[j, slot], vg_recv.at[j, mine], vg_ssem.at[j, slot], vg_rsem.at[j, mine], to),
        )

    def project(j):
        rows = slice(j * CROP, (j + 1) * CROP)

        def pieces(yd):
            at = pl.ds(pl.multiple_of(yd * 2 * HDIM, 2 * HDIM), 2 * HDIM)
            k = jnp.dot(emb[rows], wq[:, at], preferred_element_type=jnp.float32).T
            v = jnp.dot(emb[rows], wv[:, at], preferred_element_type=jnp.float32).T.astype(jnp.bfloat16)
            g = lax.dot_general(cot[rows], wo[at, :], NT, preferred_element_type=jnp.float32).T.astype(jnp.bfloat16)
            return [
                (k[cd * HDIM : (cd + 1) * HDIM], v[cd * HDIM : (cd + 1) * HDIM], g[cd * HDIM : (cd + 1) * HDIM])
                for cd in (0, 1)
            ]

        def away(step, carry):
            d = jnp.where(step == 0, 2, jnp.where(step == 1, 1, 3))
            yd = (y + d) % NY
            for cd, (k, v, g) in enumerate(pieces(yd)):
                slot = yd * 2 + cd
                k_send[j, slot] = k
                vg_send[j, slot, :HDIM] = v
                vg_send[j, slot, HDIM:] = g
                for copy in copies(j, slot, device(z, x, cd, yd)):
                    copy.start()
            return carry

        lax.fori_loop(0, 3, away, 0)
        both = pieces(y)
        other = y * 2 + 1 - c
        k_send[j, other] = jnp.where(c == 0, both[1][0], both[0][0])
        vg_send[j, other, :HDIM] = jnp.where(c == 0, both[1][1], both[0][1])
        vg_send[j, other, HDIM:] = jnp.where(c == 0, both[1][2], both[0][2])
        for copy in copies(j, other, sibling):
            copy.start()
        k_recv[j, mine] = jnp.where(c == 0, both[0][0], both[1][0])
        vg_recv[j, mine, :HDIM] = jnp.where(c == 0, both[0][1], both[1][1])
        vg_recv[j, mine, HDIM:] = jnp.where(c == 0, both[0][2], both[1][2])

    def settle(j):
        def arrive(step, carry):
            slot = (mine + step) % HEADS
            for copy in (
                remote(k_recv.at[j, slot], k_recv.at[j, slot], k_ssem.at[j, slot], k_rsem.at[j, slot], sibling),
                remote(vg_recv.at[j, slot], vg_recv.at[j, slot], vg_ssem.at[j, slot], vg_rsem.at[j, slot], sibling),
            ):
                copy.wait_recv()
            return carry

        lax.fori_loop(1, HEADS, arrive, 0)
        lanes = lax.broadcasted_iota(jnp.int32, (HDIM, CROP), 1)

        def fill(ref):
            for cs in (0, 1):
                k = (k_recv[j, cs] + k_recv[j, 2 + cs]) + (k_recv[j, 4 + cs] + k_recv[j, 6 + cs])
                vg = [vg_recv[j, 2 * yy + cs].astype(jnp.float32) for yy in range(NY)]
                vg = (vg[0] + vg[1]) + (vg[2] + vg[3])
                ok = lanes < len_ref[(z * NX + x) * LOCALS + 2 * cs + j]
                ref[j, cs, :HDIM] = k.astype(jnp.bfloat16)
                ref[j, cs, HDIM : 2 * HDIM] = vg[:HDIM].astype(jnp.bfloat16)
                ref[j, cs, 2 * HDIM :] = jnp.where(ok, vg[HDIM:], 0.0).astype(jnp.bfloat16)

        @pl.when(kept)
        def _():
            fill(seed)

        @pl.when(jnp.logical_not(kept))
        def _():
            fill(block)
            swap = remote(block.at[j], seed.at[j], bsem.at[0, j], bsem.at[1, j], partner)
            swap.start()
            swap.wait_recv()

        pltpu.make_async_copy(seed.at[j], part(j, z, col), bsem.at[2, j]).start()

    def part(j, bz, bx, half=None):
        at = j * 2 * CHIPS + (bz * NX + bx) * 2
        return table_ref.at[pl.ds(at, 2)] if half is None else table_ref.at[pl.ds(at + half, 1)]

    def landed(j, bz, bx, half=None):
        ref = part(j, bz, bx, half)
        remote(ref, ref, ssem.at[0], rsem.at[j, bz * NX + bx, half or 0], sibling).wait_recv()

    def spread(j, sent, first):
        def push(bz, bx, to, half=None, src=None):
            dst = part(j, bz, bx, half)
            sem = rsem.at[j, bz * NX + bx, half or 0]
            copy = remote(dst if src is None else src, dst, ssem.at[len(sent)], sem, to)
            copy.start()
            sent.append(copy)

        def hop(s, bx, extra):
            for bz, to, half in (((z + NZ - s) % NZ, up, 0), ((z + s) % NZ, down, 1)):
                landed(j, bz, bx)
                push(bz, bx, to, half if s == NZ // 2 - 1 else None)
                for other in extra:
                    push(bz, bx, other)

        def meet(bx, extra):
            bz = (z + NZ // 2) % NZ
            landed(j, bz, bx, 0)
            landed(j, bz, bx, 1)
            for other in extra:
                push(bz, bx, other)

        def relay(bz):
            landed(j, bz, mate_col)
            push(bz, mate_col, sibling)

        if first == "z":
            for to in (up, down, mate, sibling):
                push(z, col, to, src=seed.at[j])
            ready = [z]
            yield
            for s in range(1, NZ // 2):
                hop(s, col, (mate, sibling))
                for bz in ready:
                    relay(bz)
                ready = [(z + NZ - s) % NZ, (z + s) % NZ]
                yield
            meet(col, (mate, sibling))
            for bz in ready:
                relay(bz)
            yield
            relay((z + NZ // 2) % NZ)
            yield
        else:
            for to in (mate, up, down, sibling):
                push(z, col, to, src=seed.at[j])
            yield
            landed(j, z, mate_col)
            for to in (up, down, sibling):
                push(z, mate_col, to)
            yield
            for s in range(1, NZ // 2):
                for bx in (col, mate_col):
                    hop(s, bx, (sibling,))
                yield
            for bx in (col, mate_col):
                meet(bx, (sibling,))
            yield

    def whole(first):
        sent = []
        now, later = spread(0, sent, first), spread(1, sent, first)
        next(now)
        project(1)
        next(now)
        next(now)
        settle(1)
        live = [later, now]
        while live:
            for one in list(live):
                if next(one, 1) == 1:
                    live.remove(one)
        for j in (0, 1):
            for bz in range(NZ):
                landed(j, bz, sib_col)
                landed(j, bz, sib_mate_col)
        for copy in sent:
            copy.wait_send()

    project(0)
    first = (z * NX + col) * LOCALS
    a, b = pairs_ref[0:1], pairs_ref[1:2]
    owners = lax.broadcasted_iota(jnp.int32, (8, 1), 0) + first // 2
    codes = jnp.where(a // 2 == owners, 1 + (a - first) * CROP + b, 0) + jnp.where(
        b // 2 == owners, 1 + (b - first) * CROP + a, 0
    )
    count = pairs_ref.shape[1]
    each = count // (2 * CHIPS)
    segment = (
        lax.broadcasted_iota(jnp.int32, (count, CROP), 0) // each
        == lax.broadcasted_iota(jnp.int32, (count, CROP), 1)
    ).astype(jnp.float32)
    codes_ref[...] = jnp.dot(
        codes.astype(jnp.float32), segment, precision=lax.Precision.HIGHEST, preferred_element_type=jnp.float32
    ).astype(jnp.int32)
    settle(0)

    @pl.when(c == 0)
    def _():
        whole("z")

    @pl.when(c == 1)
    def _():
        whole("x")

    for j in (0, 1):

        def leave(step, carry):
            for copy in copies(j, (mine + step) % HEADS, sibling):
                copy.wait_send()
            return carry

        lax.fori_loop(1, HEADS, leave, 0)
        pltpu.make_async_copy(seed.at[j], part(j, z, col), bsem.at[2, j]).wait()

        @pl.when(jnp.logical_not(kept))
        def _():
            remote(block.at[j], seed.at[j], bsem.at[0, j], bsem.at[1, j], partner).wait_send()

    share.wait()


def gather_call(lengths, pairs, emb, cot, w_qk, w_value, w_out):
    rows, width = emb.shape
    smem = pl.BlockSpec(memory_space=pltpu.SMEM)
    vmem = pl.BlockSpec(memory_space=pltpu.VMEM)
    hbm = pl.BlockSpec(memory_space=pl.ANY)
    dma = pltpu.SemaphoreType.DMA
    bf = jnp.bfloat16
    return pl.pallas_call(
        gather_kernel,
        out_shape=(
            jax.ShapeDtypeStruct((CHIPS * LOCALS, 3 * HDIM, CROP), bf),
            jax.ShapeDtypeStruct((rows, width), bf),
            jax.ShapeDtypeStruct((8, CROP), jnp.int32),
        ),
        in_specs=[smem, vmem] + [hbm] * 5,
        out_specs=(hbm, hbm, vmem),
        scratch_shapes=[pltpu.VMEM(v.shape, bf) for v in (emb, cot, w_qk, w_value, w_out)]
        + [
            pltpu.VMEM((2, HEADS, HDIM, CROP), jnp.float32),
            pltpu.VMEM((2, HEADS, HDIM, CROP), jnp.float32),
            pltpu.VMEM((2, HEADS, 2 * HDIM, CROP), bf),
            pltpu.VMEM((2, HEADS, 2 * HDIM, CROP), bf),
            pltpu.VMEM((2, 2, 3 * HDIM, CROP), bf),
            pltpu.VMEM((2, 2, 3 * HDIM, CROP), bf),
            dma((7,)),
            dma((2, HEADS)),
            dma((2, HEADS)),
            dma((2, HEADS)),
            dma((2, HEADS)),
            dma((3, 2)),
            dma((72,)),
            dma((2, CHIPS, 2)),
        ],
        compiler_params=pltpu.CompilerParams(
            collective_id=0, has_side_effects=True, vmem_limit_bytes=VMEM_LIMIT
        ),
    )(lengths, pairs, emb, cot, w_qk, w_value, w_out)


def pair_kernel(
    codes_ref, len_ref, first_ref, table_hbm, hid_ref, grad_ref, table_ref, list_ref, count_ref, out_acc, dk_acc, dv_acc, sem
):
    load = pltpu.make_async_copy(table_hbm, table_ref, sem.at[0])
    load.start()
    for l in range(LOCALS + 1):
        count_ref[l] = 0

    def sort(i, carry):
        for o in (0, 1):
            code = codes_ref[o, i]
            local = jnp.where(code > 0, (code - 1) // CROP, LOCALS)
            at = count_ref[local]
            list_ref[local, at] = jnp.maximum(code - 1, 0) % CROP
            count_ref[local] = at + 1
        return carry

    lax.fori_loop(0, 2 * CHIPS, sort, 0)
    rows = lax.broadcasted_iota(jnp.int32, (CROP, CROP), 0)
    columns = lax.broadcasted_iota(jnp.int32, (1, CROP), 1)
    load.wait()

    def spot(p):
        return (p % 2) * 2 * CHIPS + p // 2

    for l in range(LOCALS):
        me = first_ref[0] + l
        row_bias = jnp.where(rows < len_ref[me], 0.0, -1e30)
        count = count_ref[l]
        for extra in range(8):
            list_ref[l, count + extra] = 0
        own = table_ref[spot(me)].astype(jnp.float32)
        kp = own[:HDIM].T.astype(jnp.bfloat16)
        vp = own[HDIM : 2 * HDIM].T.astype(jnp.bfloat16)
        gp = own[2 * HDIM :].T.astype(jnp.bfloat16)
        out_acc[...] = jnp.zeros_like(out_acc)
        dk_acc[...] = jnp.zeros_like(dk_acc)
        dv_acc[...] = jnp.zeros_like(dv_acc)

        def step(base, group):
            blocks, lens, live = [], [], []
            for j in range(group):
                q = list_ref[l, base + j]
                blocks.append(table_ref[spot(q)])
                lens.append(len_ref[q])
                live.append(jnp.where(base + j < count, 1.0, 0.0))
            many = jnp.concatenate(blocks, axis=1)
            kq, vq, gq = many[:HDIM], many[HDIM : 2 * HDIM], many[2 * HDIM :]
            scores = jnp.dot(kp, kq, preferred_element_type=jnp.float32)
            d_rows = jnp.dot(gp, vq, preferred_element_type=jnp.float32)
            d_cols = jnp.dot(vp, gq, preferred_element_type=jnp.float32)
            a_parts, b_parts, ds_parts = [], [], []
            for j in range(group):
                part = slice(j * CROP, (j + 1) * CROP)
                s = scores[:, part] * SCALE
                sa = s + jnp.where(columns < lens[j], 0.0, -1e30)
                ea = jnp.exp2(sa - jnp.max(sa, axis=1, keepdims=True))
                a = ea * (live[j] / jnp.sum(ea, axis=1, keepdims=True))
                sb = s + row_bias
                eb = jnp.exp2(sb - jnp.max(sb, axis=0, keepdims=True))
                b = eb * (live[j] / jnp.sum(eb, axis=0, keepdims=True))
                ta = a * d_rows[:, part]
                tb = b * d_cols[:, part]
                ds = (ta - a * jnp.sum(ta, axis=1, keepdims=True)) + (
                    tb - b * jnp.sum(tb, axis=0, keepdims=True)
                )
                a_parts.append(a.astype(jnp.bfloat16))
                b_parts.append(b.astype(jnp.bfloat16))
                ds_parts.append(ds.astype(jnp.bfloat16))
            for acc, parts, other in ((out_acc, a_parts, vq), (dv_acc, b_parts, gq), (dk_acc, ds_parts, kq)):
                acc[...] += lax.dot_general(
                    jnp.concatenate(parts, axis=1), other, NT, preferred_element_type=jnp.float32
                )

        def eight(i, carry):
            step(i * 8, 8)
            return carry

        def four(i, carry):
            step(big * 8, 4)
            return carry

        big = (count + 3) // 8
        lax.fori_loop(0, big, eight, 0)
        lax.fori_loop(0, jnp.where(count > big * 8, 1, 0), four, 0)
        ok = rows[:, :HDIM] < len_ref[me]
        hid_ref[l // 2, :, (l % 2) * HDIM : (l % 2 + 1) * HDIM] = jnp.where(ok, out_acc[...], 0.0).astype(
            jnp.bfloat16
        )
        turned = jnp.concatenate([dk_acc[...] * HDIM**-0.5, dv_acc[...]], axis=1).T
        for core in range(2):
            eights = []
            for xd in range(NX):
                at = (xd * 2 + core) * 8
                eights += [turned[at : at + 8], turned[HDIM + at : HDIM + at + 8]]
            grad_ref[core, :, l * CROP : (l + 1) * CROP] = jnp.concatenate(eights, axis=0).astype(jnp.bfloat16)


def pair_call(codes, lengths, first, table):
    smem = pl.BlockSpec(memory_space=pltpu.SMEM)
    vmem = pl.BlockSpec(memory_space=pltpu.VMEM)
    hbm = pl.BlockSpec(memory_space=pl.ANY)
    return pl.pallas_call(
        pair_kernel,
        out_shape=(
            jax.ShapeDtypeStruct((2, CROP, 2 * HDIM), jnp.bfloat16),
            jax.ShapeDtypeStruct((2, HDIM, LOCALS * CROP), jnp.bfloat16),
        ),
        in_specs=[smem, smem, smem, hbm],
        out_specs=(vmem, vmem),
        scratch_shapes=[
            pltpu.VMEM(table.shape, jnp.bfloat16),
            pltpu.SMEM((LOCALS + 1, 2 * CROP), jnp.int32),
            pltpu.SMEM((LOCALS + 1,), jnp.int32),
            pltpu.VMEM((CROP, HDIM), jnp.float32),
            pltpu.VMEM((CROP, HDIM), jnp.float32),
            pltpu.VMEM((CROP, HDIM), jnp.float32),
            pltpu.SemaphoreType.DMA((1,)),
        ],
        compiler_params=pltpu.CompilerParams(vmem_limit_bytes=VMEM_LIMIT),
    )(codes, lengths, first, table)


def ring_sum(n, term, plus, minus, send, recv, ssem, rsem, done):
    steps = n // 2
    half = send.shape[-1] // 2
    sent = []
    for s in range(steps):
        d = steps - s
        for way, to in ((0, plus), (1, minus)):
            own = slice(way * half, (way + 1) * half)
            rest = slice((1 - way) * half, (2 - way) * half)
            value = term(d if way == 0 else n - d)
            if s > 0:
                landing = recv.at[way, s - 1, :, own] if s == 1 else recv.at[way, s - 1]
                remote(landing, landing, ssem.at[way, s - 1], rsem.at[way, s - 1], to).wait_recv()
            send[way, s, :, own] = (
                value[:, own] if s == 0 else value[:, own] + recv[way, s - 1, :, own].astype(jnp.float32)
            ).astype(jnp.bfloat16)
            if s == 1:
                send[way, s, :, rest] = value[:, rest].astype(jnp.bfloat16)
            elif s > 1:
                send[way, s, :, rest] = (
                    value[:, rest] + recv[way, s - 1, :, rest].astype(jnp.float32)
                ).astype(jnp.bfloat16)
            spot = own if s == 0 else slice(None)
            copy = remote(
                send.at[way, s, :, spot], recv.at[way, s, :, spot], ssem.at[way, s], rsem.at[way, s], to
            )
            copy.start()
            sent.append(copy)
        yield
    total = term(0)
    for way, to in ((0, plus), (1, minus)):
        landing = recv.at[way, steps - 1]
        remote(landing, landing, ssem.at[way, steps - 1], rsem.at[way, steps - 1], to).wait_recv()
        total = total + recv[way, steps - 1].astype(jnp.float32)
    done(total)
    for copy in sent:
        copy.wait_send()
    yield


def together(*rings):
    live = list(rings)
    while live:
        for one in list(live):
            if next(one, 1) == 1:
                live.remove(one)


def finish_kernel(
    hid_ref, grad_ref, emb_hbm, sib_hbm, hidden_ref, qk_ref, value_ref,
    emb, sib, hid_recv, g_recv, terms, z_send, z_recv, x_send, x_recv, line, last_send, last_recv,
    lsem, h_ssem, h_rsem, g_ssem, g_rsem, zs_sem, zr_sem, xs_sem, xr_sem, ls_sem, lr_sem,
):
    z, x, c, y = place()
    col = column_of(x, c)
    kept = c == x // 2
    mine = 2 * y + x // 2
    loads = [pltpu.make_async_copy(emb_hbm, emb, lsem.at[0]), pltpu.make_async_copy(sib_hbm, sib, lsem.at[1])]
    for load in loads:
        load.start()
    sibling = device(z, x, 1 - c, y)
    up, down = device((z + 1) % NZ, x, c, y), device((z + NZ - 1) % NZ, x, c, y)
    east, west = device(z, (x + 1) % NX, c, y), device(z, (x + NX - 1) % NX, c, y)
    near = [device(z, x, cd, (y + d) % NY) for d in (1, 2, 3) for cd in (0, 1)] + [sibling]
    near += [device(z, NX - 1 - x, cd, (y + d) % NY) for d in range(NY) for cd in (0, 1)]
    near += [device(z, (x + d) % NX, c, y) for d in range(1, NX)]
    near += [device((z + d) % NZ, x, c, y) for d in range(1, NZ)]
    greet(near)

    ways = [(d, cd) for d in (2, 1, 3, 0) for cd in (0, 1)]

    def outgoing(d, cd, kind):
        yd = (y + d) % NY
        slot = yd * 2 + cd
        to = device(z, col, cd, yd)
        if kind == 0:
            return remote(grad_ref.at[cd], g_recv.at[mine], g_ssem.at[slot], g_rsem.at[mine], to)
        return remote(hid_ref.at[cd], hid_recv.at[mine], h_ssem.at[slot], h_rsem.at[mine], to)

    def away(d, cd):
        return jnp.logical_not(kept & (cd == c)) if d == 0 else None

    for kind in (0, 1):
        for d, cd in ways:
            if d:
                outgoing(d, cd, kind).start()
            else:

                @pl.when(away(d, cd))
                def _():
                    outgoing(d, cd, kind).start()

    @pl.when(kept)
    def _():
        g_recv[mine] = grad_ref[c]
        hid_recv[mine] = hid_ref[c]

    def arrive(ref, ss, rs):
        def one(slot, carry):
            @pl.when(jnp.logical_not(kept & (slot == mine)))
            def _():
                remote(ref.at[slot], ref.at[slot], ss.at[slot], rs.at[slot], sibling).wait_recv()

            return carry

        lax.fori_loop(0, HEADS, one, 0)

    for load in loads:
        load.wait()
    arrive(g_recv, g_ssem, g_rsem)
    width = emb.shape[-1]
    all_g = g_recv[...].reshape(HEADS * HDIM, LOCALS * CROP)
    own = jnp.where(c == 0, all_g[:, : 2 * CROP], all_g[:, 2 * CROP :])
    theirs = jnp.where(c == 0, all_g[:, 2 * CROP :], all_g[:, : 2 * CROP])
    terms[...] = (
        jnp.dot(own, emb[...], preferred_element_type=jnp.float32)
        + jnp.dot(theirs, sib[...], preferred_element_type=jnp.float32)
    ).reshape(terms.shape)

    def finish(n, term, to):
        sends = []
        for d in sorted(range(1, n), key=lambda d: -min(d, n - d)):
            last_send[d] = term(d).astype(jnp.bfloat16)
            copy = remote(last_send.at[d], last_recv.at[d], ls_sem.at[d], lr_sem.at[d], to(d))
            copy.start()
            sends.append(copy)
        total = term(0)
        for copy in sends:
            copy.wait_recv()
        for d in range(1, n):
            total = total + last_recv[d].astype(jnp.float32)
        qk_ref[...] = total[:8]
        value_ref[...] = total[8:]
        for copy in sends:
            copy.wait_send()

    def heads():
        arrive(hid_recv, h_ssem, h_rsem)
        low = lax.broadcasted_iota(jnp.int32, (CROP, 2 * HDIM), 1) < HDIM
        for yy in range(NY):
            even = hid_recv[2 * yy].astype(jnp.float32)
            odd = hid_recv[2 * yy + 1].astype(jnp.float32)
            at = slice(yy * 2 * HDIM, (yy + 1) * 2 * HDIM)
            hidden_ref[:CROP, at] = jnp.where(low, even, pltpu.roll(odd, HDIM, 1)).astype(jnp.bfloat16)
            hidden_ref[CROP:, at] = jnp.where(low, pltpu.roll(even, HDIM, 1), odd).astype(jnp.bfloat16)

    @pl.when(c == 0)
    def _():
        def ring(i):
            def done(total):
                line[2 * i : 2 * i + 2] = total.reshape(2, 16, width)

            return ring_sum(
                NZ,
                lambda d: terms[(z + d) % NZ, 2 * i : 2 * i + 2].reshape(32, width),
                up, down, z_send.at[i], z_recv.at[i], zs_sem.at[i], zr_sem.at[i], done,
            )

        together(ring(0), ring(1))
        finish(NX, lambda d: line[(x + d) % NX], lambda d: device(z, (x + d) % NX, c, y))

    @pl.when(c == 1)
    def _():
        def ring(i):
            def done(total):
                line[4 * i : 4 * i + 4] = total.reshape(4, 16, width)

            return ring_sum(
                NX,
                lambda d: terms[4 * i : 4 * i + 4, (x + d) % NX].reshape(64, width),
                east, west, x_send.at[i], x_recv.at[i], xs_sem.at[i], xr_sem.at[i], done,
            )

        together(ring(0), ring(1))
        finish(NZ, lambda d: line[(z + d) % NZ], lambda d: device((z + d) % NZ, x, c, y))

    heads()
    for d, cd in ways:
        for kind in (0, 1):
            if d:
                outgoing(d, cd, kind).wait_send()
            else:

                @pl.when(away(d, cd))
                def _():
                    outgoing(d, cd, kind).wait_send()


def finish_call(hid, grads, emb, sib):
    rows, width = emb.shape
    vmem = pl.BlockSpec(memory_space=pltpu.VMEM)
    hbm = pl.BlockSpec(memory_space=pl.ANY)
    dma = pltpu.SemaphoreType.DMA
    bf = jnp.bfloat16
    return pl.pallas_call(
        finish_kernel,
        out_shape=(
            jax.ShapeDtypeStruct((rows, HEADS * HDIM), bf),
            jax.ShapeDtypeStruct((8, width), jnp.float32),
            jax.ShapeDtypeStruct((8, width), jnp.float32),
        ),
        in_specs=[vmem, vmem, hbm, hbm],
        out_specs=(vmem, vmem, vmem),
        scratch_shapes=[
            pltpu.VMEM((rows, width), bf),
            pltpu.VMEM((rows, width), bf),
            pltpu.VMEM((HEADS, CROP, 2 * HDIM), bf),
            pltpu.VMEM((HEADS, HDIM, LOCALS * CROP), bf),
            pltpu.VMEM((NZ, NX, 16, width), jnp.float32),
            pltpu.VMEM((2, 2, NZ // 2, 32, width), bf),
            pltpu.VMEM((2, 2, NZ // 2, 32, width), bf),
            pltpu.VMEM((2, 2, NX // 2, 64, width), bf),
            pltpu.VMEM((2, 2, NX // 2, 64, width), bf),
            pltpu.VMEM((NZ, 16, width), jnp.float32),
            pltpu.VMEM((NZ, 16, width), bf),
            pltpu.VMEM((NZ, 16, width), bf),
            dma((2,)),
            dma((HEADS,)),
            dma((HEADS,)),
            dma((HEADS,)),
            dma((HEADS,)),
            dma((2, 2, NZ // 2)),
            dma((2, 2, NZ // 2)),
            dma((2, 2, NX // 2)),
            dma((2, 2, NX // 2)),
            dma((NZ,)),
            dma((NZ,)),
        ],
        compiler_params=pltpu.CompilerParams(
            collective_id=1, has_side_effects=True, vmem_limit_bytes=VMEM_LIMIT
        ),
    )(hid, grads, emb, sib)


def on_device(embeddings, cotangent, w_qk, w_value, w_out, lengths, pair_list):
    owned, crop, width = embeddings.shape
    rows = owned * crop
    emb = embeddings.reshape(rows, width)
    z, x, c, _ = place()
    first = LOCALS * (z * NX + column_of(x, c))
    table, sib, codes = gather_call(
        lengths, pair_list.T, emb, cotangent.reshape(rows, width), w_qk, w_value, w_out
    )
    hid, grads = pair_call(codes, lengths, first.reshape(1), table)
    hidden, grad_qk, grad_value = finish_call(hid, grads, emb, sib)
    attended = jnp.dot(hidden, w_out, preferred_element_type=jnp.float32).astype(jnp.bfloat16)
    return (attended.reshape(embeddings.shape), grad_qk.T, grad_value.T)


def solution(mesh):
    in_specs = (
        P("pairs", None, "mp"),
        P("pairs", None, "mp"),
        P("mp", None),
        P("mp", None),
        P(None, "mp"),
        P(),
        P(),
    )
    out_specs = (P("pairs", None, "mp"), P("mp", "pairs"), P("mp", "pairs"))
    return jax.shard_map(on_device, mesh=mesh, in_specs=in_specs, out_specs=out_specs, check_vma=False)
```

```python
import math

import jax
import jax.numpy as jnp
from jax import lax
from jax.experimental import pallas as pl
from jax.experimental.pallas import tpu as pltpu
from jax.sharding import PartitionSpec as P

HDIM = 64
CROP = 128
SCALE = HDIM**-0.5 * math.log2(math.e)
NT = (((1,), (1,)), ((), ()))
NZ, NX, NY = 8, 4, 4
CHIPS = NZ * NX
LOCALS = 4
HEADS = 2 * NY
MESH = pl.DeviceIdType.MESH
VMEM_LIMIT = 56 * 1024 * 1024
SCHEDULE = (0, 1, None, 2, 3)


def place():
    me = lax.axis_index("pairs")
    chip = me // 2
    return chip // NX, chip % NX, me % 2, lax.axis_index("mp")


def device(z, x, c, y):
    return ((z * NX + x) * 2 + c, y)


def column_of(x, c):
    return jnp.where(c == x // 2, x, NX - 1 - x)


def mate_of(x):
    return x + 1 - 2 * (x % 2)


def remote(src, dst, send, recv, to):
    return pltpu.make_async_remote_copy(
        src_ref=src, dst_ref=dst, send_sem=send, recv_sem=recv, device_id=to, device_id_type=MESH
    )


def greet(others):
    barrier = pltpu.get_barrier_semaphore()
    for other in others:
        pl.semaphore_signal(barrier, inc=1, device_id=other, device_id_type=MESH)
    pl.semaphore_wait(barrier, len(others))


def gather_kernel(
    len_ref, pairs_ref, emb_hbm, cot_hbm, wq_hbm, wv_hbm, wo_hbm, table_ref, sib_ref, codes_ref,
    emb, cot, wq, wv, wo, k_send, k_recv, vg_send, vg_recv, seed,
    lsem, k_ssem, k_rsem, vg_ssem, vg_rsem, bsem, ssem, rsem,
):
    z, x, c, y = place()
    mine = y * 2 + c
    sibling = device(z, x, 1 - c, y)
    above, below = (z + 1) % NZ, (z + NZ - 1) % NZ
    mate = device(z, mate_of(x), c, y)
    up, down = device(above, x, c, y), device(below, x, c, y)
    mate_up, mate_down = device(above, mate_of(x), c, y), device(below, mate_of(x), c, y)
    col, mate_col = column_of(x, c), column_of(mate_of(x), c)
    sib_col, sib_mate_col = column_of(x, 1 - c), column_of(mate_of(x), 1 - c)
    kept = c == x // 2

    loads = [
        pltpu.make_async_copy(src, dst, lsem.at[i])
        for i, (src, dst) in enumerate(
            ((emb_hbm, emb), (wq_hbm, wq), (wv_hbm, wv), (cot_hbm, cot), (wo_hbm, wo))
        )
    ]
    for load in loads:
        load.start()
    greet(
        [device(z, x, cd, (y + d) % NY) for d in (1, 2, 3) for cd in (0, 1)]
        + [device(z, NX - 1 - x, cd, (y + d) % NY) for d in range(NY) for cd in (0, 1)]
        + [sibling, mate, up, down, mate_up, mate_down]
    )
    for load in loads:
        load.wait()

    def copies(j, slot, to):
        return (
            remote(k_send.at[j, slot], k_recv.at[j, mine], k_ssem.at[j, slot], k_rsem.at[j, mine], to),
            remote(vg_send.at[j, slot], vg_recv.at[j, mine], vg_ssem.at[j, slot], vg_rsem.at[j, mine], to),
        )

    def project(j):
        rows = slice(j * CROP, (j + 1) * CROP)

        def away(step, carry):
            d = jnp.where(step == 0, 2, jnp.where(step == 1, 1, jnp.where(step == 2, 3, 0)))
            yd = (y + d) % NY
            at = pl.ds(pl.multiple_of(yd * 2 * HDIM, 2 * HDIM), 2 * HDIM)
            k = jnp.dot(emb[rows], wq[:, at], preferred_element_type=jnp.float32).T
            v = jnp.dot(emb[rows], wv[:, at], preferred_element_type=jnp.float32).T.astype(jnp.bfloat16)
            g = lax.dot_general(cot[rows], wo[at, :], NT, preferred_element_type=jnp.float32).T.astype(jnp.bfloat16)
            for h in (0, 1):
                slot = yd * 2 + h
                part = slice(h * HDIM, (h + 1) * HDIM)
                here = kept & (slot == mine)

                @pl.when(here)
                def _():
                    k_recv[j, mine] = k[part]
                    vg_recv[j, mine, :HDIM] = v[part]
                    vg_recv[j, mine, HDIM:] = g[part]

                @pl.when(jnp.logical_not(here))
                def _():
                    k_send[j, slot] = k[part]
                    vg_send[j, slot, :HDIM] = v[part]
                    vg_send[j, slot, HDIM:] = g[part]
                    to = device(z, jnp.where(x // 2 == h, x, NX - 1 - x), x // 2, yd)
                    for copy in copies(j, slot, to):
                        copy.start()

            return carry

        lax.fori_loop(0, NY, away, 0)

    def settle(j):
        def arrive(slot, carry):
            @pl.when(jnp.logical_not(kept & (slot == mine)))
            def _():
                for ref, ss, rs in ((k_recv, k_ssem, k_rsem), (vg_recv, vg_ssem, vg_rsem)):
                    remote(ref.at[j, slot], ref.at[j, slot], ss.at[j, slot], rs.at[j, slot], sibling).wait_recv()

            return carry

        lax.fori_loop(0, HEADS, arrive, 0)
        lanes = lax.broadcasted_iota(jnp.int32, (HDIM, CROP), 1)
        for cs in (0, 1):
            k = (k_recv[j, cs] + k_recv[j, 2 + cs]) + (k_recv[j, 4 + cs] + k_recv[j, 6 + cs])
            vg = [vg_recv[j, 2 * yy + cs].astype(jnp.float32) for yy in range(NY)]
            vg = (vg[0] + vg[1]) + (vg[2] + vg[3])
            ok = lanes < len_ref[(z * NX + col) * LOCALS + 2 * cs + j]
            seed[j, cs, :HDIM] = k.astype(jnp.bfloat16)
            seed[j, cs, HDIM : 2 * HDIM] = vg[:HDIM].astype(jnp.bfloat16)
            seed[j, cs, 2 * HDIM :] = jnp.where(ok, vg[HDIM:], 0.0).astype(jnp.bfloat16)
        keep(j).start()

    def keep(j):
        at = pl.ds(j * 2 * CHIPS + (z * NX + col) * 2, 2)
        return pltpu.make_async_copy(seed.at[j], table_ref.at[at], bsem.at[j])

    def spread(j, cs, sent, first):
        lane = 2 * j + cs

        def part(bz, bx, half):
            at = j * 2 * CHIPS + (bz * NX + bx) * 2 + cs
            if half is None:
                return table_ref.at[at]
            return table_ref.at[at, pl.ds(half * 3 * HDIM // 2, 3 * HDIM // 2)]

        def signal(bz, bx, half):
            return rsem.at[lane, CHIPS + jnp.where(bx == col, 0, 1) if half == 1 else bz * NX + bx]

        def landed(bz, bx, half=None):
            ref = part(bz, bx, half)
            remote(ref, ref, ssem.at[0], signal(bz, bx, half), sibling).wait_recv()

        def push(bz, bx, to, half=None, src=None, far=None):
            dst = part(bz, bx, half)
            sem = signal(bz, bx, half) if far is None else rsem.at[lane, far]
            copy = remote(dst if src is None else src, dst, ssem.at[len(sent)], sem, to)
            copy.start()
            sent.append(copy)

        def hop(s, bx, extra):
            for bz, to, half in (((z + NZ - s) % NZ, up, 0), ((z + s) % NZ, down, 1)):
                landed(bz, bx)
                push(bz, bx, to, half if s == NZ // 2 - 1 else None)
                for other in extra:
                    push(bz, bx, other)

        def meet(bx, extra):
            bz = (z + NZ // 2) % NZ
            landed(bz, bx, 0)
            landed(bz, bx, 1)
            for other in extra:
                push(bz, bx, other)

        def relay(bz):
            landed(bz, mate_col)
            push(bz, mate_col, sibling)

        own = seed.at[j, cs]
        if first == "z":
            for to in (up, down, mate, sibling):
                push(z, col, to, src=own)
            ready = [z]
            yield
            for s in range(1, NZ // 2):
                hop(s, col, (mate, sibling))
                for bz in ready:
                    relay(bz)
                ready = [(z + NZ - s) % NZ, (z + s) % NZ]
                yield
            meet(col, (mate, sibling))
            for bz in ready:
                relay(bz)
            yield
            relay((z + NZ // 2) % NZ)
            yield
        else:
            for to in (up, down, mate_up, mate_down, mate, sibling):
                push(z, col, to, src=own)
            yield
            for s in range(1, NZ // 2):
                for bx in (col, mate_col):
                    hop(s, bx, (sibling,))
                if s == 1:
                    relay(z)
                yield
            for bx in (col, mate_col):
                meet(bx, (sibling,))
            yield
        for bz in range(NZ):
            landed(bz, sib_col)
            landed(bz, sib_mate_col)
        yield

    def whole(first):
        sent = []
        flows = [spread(j, cs, sent, first) for j in (0, 1) for cs in (0, 1)]
        for what in SCHEDULE:
            if what is None:
                settle(1)
            else:
                next(flows[what])
        live = list(flows)
        while live:
            for one in list(live):
                if next(one, 1) == 1:
                    live.remove(one)
        for copy in sent:
            copy.wait_send()

    project(0)
    project(1)
    share = remote(emb, sib_ref, lsem.at[5], lsem.at[6], sibling)
    share.start()
    first = (z * NX + col) * LOCALS
    a, b = pairs_ref[0:1], pairs_ref[1:2]
    owners = lax.broadcasted_iota(jnp.int32, (8, 1), 0) + first // 2
    codes = jnp.where(a // 2 == owners, 1 + (a - first) * CROP + b, 0) + jnp.where(
        b // 2 == owners, 1 + (b - first) * CROP + a, 0
    )
    count = pairs_ref.shape[1]
    each = count // (2 * CHIPS)
    segment = (
        lax.broadcasted_iota(jnp.int32, (count, CROP), 0) // each
        == lax.broadcasted_iota(jnp.int32, (count, CROP), 1)
    ).astype(jnp.float32)
    codes_ref[...] = jnp.dot(
        codes.astype(jnp.float32), segment, precision=lax.Precision.HIGHEST, preferred_element_type=jnp.float32
    ).astype(jnp.int32)
    settle(0)

    @pl.when(c == 0)
    def _():
        whole("z")

    @pl.when(c == 1)
    def _():
        whole("x")

    for j in (0, 1):

        def leave(slot, carry):
            @pl.when(jnp.logical_not(kept & (slot == mine)))
            def _():
                for copy in copies(j, slot, sibling):
                    copy.wait_send()

            return carry

        lax.fori_loop(0, HEADS, leave, 0)
        keep(j).wait()
    share.wait()


def gather_call(lengths, pairs, emb, cot, w_qk, w_value, w_out):
    rows, width = emb.shape
    smem = pl.BlockSpec(memory_space=pltpu.SMEM)
    vmem = pl.BlockSpec(memory_space=pltpu.VMEM)
    hbm = pl.BlockSpec(memory_space=pl.ANY)
    dma = pltpu.SemaphoreType.DMA
    bf = jnp.bfloat16
    return pl.pallas_call(
        gather_kernel,
        out_shape=(
            jax.ShapeDtypeStruct((CHIPS * LOCALS, 3 * HDIM, CROP), bf),
            jax.ShapeDtypeStruct((rows, width), bf),
            jax.ShapeDtypeStruct((8, CROP), jnp.int32),
        ),
        in_specs=[smem, vmem] + [hbm] * 5,
        out_specs=(hbm, hbm, vmem),
        scratch_shapes=[pltpu.VMEM(v.shape, bf) for v in (emb, cot, w_qk, w_value, w_out)]
        + [
            pltpu.VMEM((2, HEADS, HDIM, CROP), jnp.float32),
            pltpu.VMEM((2, HEADS, HDIM, CROP), jnp.float32),
            pltpu.VMEM((2, HEADS, 2 * HDIM, CROP), bf),
            pltpu.VMEM((2, HEADS, 2 * HDIM, CROP), bf),
            pltpu.VMEM((2, 2, 3 * HDIM, CROP), bf),
            dma((7,)),
            dma((2, HEADS)),
            dma((2, HEADS)),
            dma((2, HEADS)),
            dma((2, HEADS)),
            dma((2,)),
            dma((144,)),
            dma((LOCALS, CHIPS + 2)),
        ],
        compiler_params=pltpu.CompilerParams(
            collective_id=0, has_side_effects=True, vmem_limit_bytes=VMEM_LIMIT
        ),
    )(lengths, pairs, emb, cot, w_qk, w_value, w_out)


def pair_kernel(
    codes_ref, len_ref, first_ref, table_hbm, hid_ref, grad_ref, table_ref, list_ref, count_ref, out_acc, dk_acc, dv_acc, sem
):
    load = pltpu.make_async_copy(table_hbm, table_ref, sem.at[0])
    load.start()
    for l in range(LOCALS + 1):
        count_ref[l] = 0

    def sort(i, carry):
        for o in (0, 1):
            code = codes_ref[o, i]
            local = jnp.where(code > 0, (code - 1) // CROP, LOCALS)
            at = count_ref[local]
            list_ref[local, at] = jnp.maximum(code - 1, 0) % CROP
            count_ref[local] = at + 1
        return carry

    lax.fori_loop(0, 2 * CHIPS, sort, 0)
    rows = lax.broadcasted_iota(jnp.int32, (CROP, CROP), 0)
    columns = lax.broadcasted_iota(jnp.int32, (1, CROP), 1)
    load.wait()

    def spot(p):
        return (p % 2) * 2 * CHIPS + p // 2

    for l in range(LOCALS):
        me = first_ref[0] + l
        row_bias = jnp.where(rows < len_ref[me], 0.0, -1e30)
        count = count_ref[l]
        for extra in range(8):
            list_ref[l, count + extra] = 0
        own = table_ref[spot(me)].astype(jnp.float32)
        kp = own[:HDIM].T.astype(jnp.bfloat16)
        vp = own[HDIM : 2 * HDIM].T.astype(jnp.bfloat16)
        gp = own[2 * HDIM :].T.astype(jnp.bfloat16)
        out_acc[...] = jnp.zeros_like(out_acc)
        dk_acc[...] = jnp.zeros_like(dk_acc)
        dv_acc[...] = jnp.zeros_like(dv_acc)

        def step(base, group):
            blocks, lens, live = [], [], []
            for j in range(group):
                q = list_ref[l, base + j]
                blocks.append(table_ref[spot(q)])
                lens.append(len_ref[q])
                live.append(jnp.where(base + j < count, 1.0, 0.0))
            many = jnp.concatenate(blocks, axis=1)
            kq, vq, gq = many[:HDIM], many[HDIM : 2 * HDIM], many[2 * HDIM :]
            scores = jnp.dot(kp, kq, preferred_element_type=jnp.float32)
            d_rows = jnp.dot(gp, vq, preferred_element_type=jnp.float32)
            d_cols = jnp.dot(vp, gq, preferred_element_type=jnp.float32)
            a_parts, b_parts, ds_parts = [], [], []
            for j in range(group):
                part = slice(j * CROP, (j + 1) * CROP)
                s = scores[:, part] * SCALE
                sa = s + jnp.where(columns < lens[j], 0.0, -1e30)
                ea = jnp.exp2(sa - jnp.max(sa, axis=1, keepdims=True))
                a = ea * (live[j] / jnp.sum(ea, axis=1, keepdims=True))
                sb = s + row_bias
                eb = jnp.exp2(sb - jnp.max(sb, axis=0, keepdims=True))
                b = eb * (live[j] / jnp.sum(eb, axis=0, keepdims=True))
                ta = a * d_rows[:, part]
                tb = b * d_cols[:, part]
                ds = (ta - a * jnp.sum(ta, axis=1, keepdims=True)) + (
                    tb - b * jnp.sum(tb, axis=0, keepdims=True)
                )
                a_parts.append(a.astype(jnp.bfloat16))
                b_parts.append(b.astype(jnp.bfloat16))
                ds_parts.append(ds.astype(jnp.bfloat16))
            for acc, parts, other in ((out_acc, a_parts, vq), (dv_acc, b_parts, gq), (dk_acc, ds_parts, kq)):
                acc[...] += lax.dot_general(
                    jnp.concatenate(parts, axis=1), other, NT, preferred_element_type=jnp.float32
                )

        def eight(i, carry):
            step(i * 8, 8)
            return carry

        def four(i, carry):
            step(big * 8, 4)
            return carry

        big = (count + 3) // 8
        lax.fori_loop(0, big, eight, 0)
        lax.fori_loop(0, jnp.where(count > big * 8, 1, 0), four, 0)
        ok = rows[:, :HDIM] < len_ref[me]
        hid_ref[l // 2, :, (l % 2) * HDIM : (l % 2 + 1) * HDIM] = jnp.where(ok, out_acc[...], 0.0).astype(
            jnp.bfloat16
        )
        turned = jnp.concatenate([dk_acc[...] * HDIM**-0.5, dv_acc[...]], axis=1).T
        for core in range(2):
            eights = []
            for xd in range(NX):
                at = (xd * 2 + core) * 8
                eights += [turned[at : at + 8], turned[HDIM + at : HDIM + at + 8]]
            grad_ref[core, :, l * CROP : (l + 1) * CROP] = jnp.concatenate(eights, axis=0).astype(jnp.bfloat16)


def pair_call(codes, lengths, first, table):
    smem = pl.BlockSpec(memory_space=pltpu.SMEM)
    vmem = pl.BlockSpec(memory_space=pltpu.VMEM)
    hbm = pl.BlockSpec(memory_space=pl.ANY)
    return pl.pallas_call(
        pair_kernel,
        out_shape=(
            jax.ShapeDtypeStruct((2, CROP, 2 * HDIM), jnp.bfloat16),
            jax.ShapeDtypeStruct((2, HDIM, LOCALS * CROP), jnp.bfloat16),
        ),
        in_specs=[smem, smem, smem, hbm],
        out_specs=(vmem, vmem),
        scratch_shapes=[
            pltpu.VMEM(table.shape, jnp.bfloat16),
            pltpu.SMEM((LOCALS + 1, 2 * CROP), jnp.int32),
            pltpu.SMEM((LOCALS + 1,), jnp.int32),
            pltpu.VMEM((CROP, HDIM), jnp.float32),
            pltpu.VMEM((CROP, HDIM), jnp.float32),
            pltpu.VMEM((CROP, HDIM), jnp.float32),
            pltpu.SemaphoreType.DMA((1,)),
        ],
        compiler_params=pltpu.CompilerParams(vmem_limit_bytes=VMEM_LIMIT),
    )(codes, lengths, first, table)


def ring_sum(n, term, plus, minus, send, recv, ssem, rsem, done):
    steps = n // 2
    half = send.shape[-1] // 2
    sent = []
    for s in range(steps):
        d = steps - s
        for way, to in ((0, plus), (1, minus)):
            own = slice(way * half, (way + 1) * half)
            rest = slice((1 - way) * half, (2 - way) * half)
            value = term(d if way == 0 else n - d)
            if s > 0:
                landing = recv.at[way, s - 1, :, own] if s == 1 else recv.at[way, s - 1]
                remote(landing, landing, ssem.at[way, s - 1], rsem.at[way, s - 1], to).wait_recv()
            send[way, s, :, own] = (
                value[:, own] if s == 0 else value[:, own] + recv[way, s - 1, :, own].astype(jnp.float32)
            ).astype(jnp.bfloat16)
            if s == 1:
                send[way, s, :, rest] = value[:, rest].astype(jnp.bfloat16)
            elif s > 1:
                send[way, s, :, rest] = (
                    value[:, rest] + recv[way, s - 1, :, rest].astype(jnp.float32)
                ).astype(jnp.bfloat16)
            spot = own if s == 0 else slice(None)
            copy = remote(
                send.at[way, s, :, spot], recv.at[way, s, :, spot], ssem.at[way, s], rsem.at[way, s], to
            )
            copy.start()
            sent.append(copy)
        yield
    total = term(0)
    for way, to in ((0, plus), (1, minus)):
        landing = recv.at[way, steps - 1]
        remote(landing, landing, ssem.at[way, steps - 1], rsem.at[way, steps - 1], to).wait_recv()
        total = total + recv[way, steps - 1].astype(jnp.float32)
    done(total)
    for copy in sent:
        copy.wait_send()
    yield


def together(*rings):
    live = list(rings)
    while live:
        for one in list(live):
            if next(one, 1) == 1:
                live.remove(one)


def finish_kernel(
    hid_ref, grad_ref, emb_hbm, sib_hbm, hidden_ref, qk_ref, value_ref,
    emb, sib, hid_recv, g_recv, terms, z_send, z_recv, x_send, x_recv, line, last_send, last_recv,
    lsem, h_ssem, h_rsem, g_ssem, g_rsem, zs_sem, zr_sem, xs_sem, xr_sem, ls_sem, lr_sem,
):
    z, x, c, y = place()
    col = column_of(x, c)
    kept = c == x // 2
    mine = 2 * y + x // 2
    loads = [pltpu.make_async_copy(emb_hbm, emb, lsem.at[0]), pltpu.make_async_copy(sib_hbm, sib, lsem.at[1])]
    for load in loads:
        load.start()
    sibling = device(z, x, 1 - c, y)
    up, down = device((z + 1) % NZ, x, c, y), device((z + NZ - 1) % NZ, x, c, y)
    east, west = device(z, (x + 1) % NX, c, y), device(z, (x + NX - 1) % NX, c, y)
    near = [device(z, x, cd, (y + d) % NY) for d in (1, 2, 3) for cd in (0, 1)] + [sibling]
    near += [device(z, NX - 1 - x, cd, (y + d) % NY) for d in range(NY) for cd in (0, 1)]
    near += [device(z, (x + d) % NX, c, y) for d in range(1, NX)]
    near += [device((z + d) % NZ, x, c, y) for d in range(1, NZ)]
    greet(near)

    ways = [(d, cd) for d in (2, 1, 3, 0) for cd in (0, 1)]

    def outgoing(d, cd, kind):
        yd = (y + d) % NY
        slot = yd * 2 + cd
        to = device(z, col, cd, yd)
        if kind == 0:
            return remote(grad_ref.at[cd], g_recv.at[mine], g_ssem.at[slot], g_rsem.at[mine], to)
        return remote(hid_ref.at[cd], hid_recv.at[mine], h_ssem.at[slot], h_rsem.at[mine], to)

    def away(d, cd):
        return jnp.logical_not(kept & (cd == c)) if d == 0 else None

    for kind in (0, 1):
        for d, cd in ways:
            if d:
                outgoing(d, cd, kind).start()
            else:

                @pl.when(away(d, cd))
                def _():
                    outgoing(d, cd, kind).start()

    @pl.when(kept)
    def _():
        g_recv[mine] = grad_ref[c]
        hid_recv[mine] = hid_ref[c]

    def arrive(ref, ss, rs):
        def one(slot, carry):
            @pl.when(jnp.logical_not(kept & (slot == mine)))
            def _():
                remote(ref.at[slot], ref.at[slot], ss.at[slot], rs.at[slot], sibling).wait_recv()

            return carry

        lax.fori_loop(0, HEADS, one, 0)

    for load in loads:
        load.wait()
    arrive(g_recv, g_ssem, g_rsem)
    width = emb.shape[-1]
    all_g = g_recv[...].reshape(HEADS * HDIM, LOCALS * CROP)
    own = jnp.where(c == 0, all_g[:, : 2 * CROP], all_g[:, 2 * CROP :])
    theirs = jnp.where(c == 0, all_g[:, 2 * CROP :], all_g[:, : 2 * CROP])
    terms[...] = (
        jnp.dot(own, emb[...], preferred_element_type=jnp.float32)
        + jnp.dot(theirs, sib[...], preferred_element_type=jnp.float32)
    ).reshape(terms.shape)

    def finish(n, term, to):
        sends = []
        for d in sorted(range(1, n), key=lambda d: -min(d, n - d)):
            last_send[d] = term(d).astype(jnp.bfloat16)
            copy = remote(last_send.at[d], last_recv.at[d], ls_sem.at[d], lr_sem.at[d], to(d))
            copy.start()
            sends.append(copy)
        total = term(0)
        for copy in sends:
            copy.wait_recv()
        for d in range(1, n):
            total = total + last_recv[d].astype(jnp.float32)
        qk_ref[...] = total[:8]
        value_ref[...] = total[8:]
        for copy in sends:
            copy.wait_send()

    def heads():
        arrive(hid_recv, h_ssem, h_rsem)
        low = lax.broadcasted_iota(jnp.int32, (CROP, 2 * HDIM), 1) < HDIM
        for yy in range(NY):
            even = hid_recv[2 * yy].astype(jnp.float32)
            odd = hid_recv[2 * yy + 1].astype(jnp.float32)
            at = slice(yy * 2 * HDIM, (yy + 1) * 2 * HDIM)
            hidden_ref[:CROP, at] = jnp.where(low, even, pltpu.roll(odd, HDIM, 1)).astype(jnp.bfloat16)
            hidden_ref[CROP:, at] = jnp.where(low, pltpu.roll(even, HDIM, 1), odd).astype(jnp.bfloat16)

    @pl.when(c == 0)
    def _():
        def ring(i):
            def done(total):
                line[2 * i : 2 * i + 2] = total.reshape(2, 16, width)

            return ring_sum(
                NZ,
                lambda d: terms[(z + d) % NZ, 2 * i : 2 * i + 2].reshape(32, width),
                up, down, z_send.at[i], z_recv.at[i], zs_sem.at[i], zr_sem.at[i], done,
            )

        together(ring(0), ring(1))
        finish(NX, lambda d: line[(x + d) % NX], lambda d: device(z, (x + d) % NX, c, y))

    @pl.when(c == 1)
    def _():
        def ring(i):
            def done(total):
                line[4 * i : 4 * i + 4] = total.reshape(4, 16, width)

            return ring_sum(
                NX,
                lambda d: terms[4 * i : 4 * i + 4, (x + d) % NX].reshape(64, width),
                east, west, x_send.at[i], x_recv.at[i], xs_sem.at[i], xr_sem.at[i], done,
            )

        together(ring(0), ring(1))
        finish(NZ, lambda d: line[(z + d) % NZ], lambda d: device((z + d) % NZ, x, c, y))

    heads()
    for d, cd in ways:
        for kind in (0, 1):
            if d:
                outgoing(d, cd, kind).wait_send()
            else:

                @pl.when(away(d, cd))
                def _():
                    outgoing(d, cd, kind).wait_send()


def finish_call(hid, grads, emb, sib):
    rows, width = emb.shape
    vmem = pl.BlockSpec(memory_space=pltpu.VMEM)
    hbm = pl.BlockSpec(memory_space=pl.ANY)
    dma = pltpu.SemaphoreType.DMA
    bf = jnp.bfloat16
    return pl.pallas_call(
        finish_kernel,
        out_shape=(
            jax.ShapeDtypeStruct((rows, HEADS * HDIM), bf),
            jax.ShapeDtypeStruct((8, width), jnp.float32),
            jax.ShapeDtypeStruct((8, width), jnp.float32),
        ),
        in_specs=[vmem, vmem, hbm, hbm],
        out_specs=(vmem, vmem, vmem),
        scratch_shapes=[
            pltpu.VMEM((rows, width), bf),
            pltpu.VMEM((rows, width), bf),
            pltpu.VMEM((HEADS, CROP, 2 * HDIM), bf),
            pltpu.VMEM((HEADS, HDIM, LOCALS * CROP), bf),
            pltpu.VMEM((NZ, NX, 16, width), jnp.float32),
            pltpu.VMEM((2, 2, NZ // 2, 32, width), bf),
            pltpu.VMEM((2, 2, NZ // 2, 32, width), bf),
            pltpu.VMEM((2, 2, NX // 2, 64, width), bf),
            pltpu.VMEM((2, 2, NX // 2, 64, width), bf),
            pltpu.VMEM((NZ, 16, width), jnp.float32),
            pltpu.VMEM((NZ, 16, width), bf),
            pltpu.VMEM((NZ, 16, width), bf),
            dma((2,)),
            dma((HEADS,)),
            dma((HEADS,)),
            dma((HEADS,)),
            dma((HEADS,)),
            dma((2, 2, NZ // 2)),
            dma((2, 2, NZ // 2)),
            dma((2, 2, NX // 2)),
            dma((2, 2, NX // 2)),
            dma((NZ,)),
            dma((NZ,)),
        ],
        compiler_params=pltpu.CompilerParams(
            collective_id=1, has_side_effects=True, vmem_limit_bytes=VMEM_LIMIT
        ),
    )(hid, grads, emb, sib)


def output_kernel(hidden_ref, wo_ref, qk_ref, value_ref, att_ref, out_qk_ref, out_value_ref):
    att_ref[...] = jnp.dot(hidden_ref[...], wo_ref[...], preferred_element_type=jnp.float32).astype(jnp.bfloat16)
    out_qk_ref[...] = qk_ref[...]
    out_value_ref[...] = value_ref[...]


def output_call(hidden, w_out, grad_qk, grad_value):
    vmem = pl.BlockSpec(memory_space=pltpu.VMEM)
    return pl.pallas_call(
        output_kernel,
        out_shape=(
            jax.ShapeDtypeStruct((hidden.shape[0], w_out.shape[1]), jnp.bfloat16),
            jax.ShapeDtypeStruct(grad_qk.shape, grad_qk.dtype),
            jax.ShapeDtypeStruct(grad_value.shape, grad_value.dtype),
        ),
        in_specs=[vmem] * 4,
        out_specs=(vmem,) * 3,
        compiler_params=pltpu.CompilerParams(vmem_limit_bytes=16 * 1024 * 1024),
    )(hidden, w_out, grad_qk, grad_value)


def on_device(embeddings, cotangent, w_qk, w_value, w_out, lengths, pair_list):
    owned, crop, width = embeddings.shape
    rows = owned * crop
    emb = embeddings.reshape(rows, width)
    z, x, c, _ = place()
    first = LOCALS * (z * NX + column_of(x, c))
    table, sib, codes = gather_call(
        lengths, pair_list.T, emb, cotangent.reshape(rows, width), w_qk, w_value, w_out
    )
    hid, grads = pair_call(codes, lengths, first.reshape(1), table)
    hidden, grad_qk, grad_value = finish_call(hid, grads, emb, sib)
    attended, grad_qk, grad_value = output_call(hidden, w_out, grad_qk, grad_value)
    return (attended.reshape(embeddings.shape), grad_qk.T, grad_value.T)


def solution(mesh):
    in_specs = (
        P("pairs", None, "mp"),
        P("pairs", None, "mp"),
        P("mp", None),
        P("mp", None),
        P(None, "mp"),
        P(),
        P(),
    )
    out_specs = (P("pairs", None, "mp"), P("mp", "pairs"), P("mp", "pairs"))
    return jax.shard_map(on_device, mesh=mesh, in_specs=in_specs, out_specs=out_specs, check_vma=False)
```

```python
import math

import jax
import jax.numpy as jnp
from jax import lax
from jax.experimental import pallas as pl
from jax.experimental.pallas import tpu as pltpu
from jax.sharding import PartitionSpec as P

HDIM = 64
CROP = 128
SCALE = HDIM**-0.5 * math.log2(math.e)
NT = (((1,), (1,)), ((), ()))
NZ, NX, NY = 8, 4, 4
CHIPS = NZ * NX
LOCALS = 4
HEADS = 2 * NY
GROUPS = 20
MESH = pl.DeviceIdType.MESH
VMEM_LIMIT = 56 * 1024 * 1024
SCHEDULE = (0, 1, None, 2, 3)


def place():
    me = lax.axis_index("pairs")
    chip = me // 2
    return chip // NX, chip % NX, me % 2, lax.axis_index("mp")


def device(z, x, c, y):
    return ((z * NX + x) * 2 + c, y)


def column_of(x, c):
    return jnp.where(c == x // 2, x, NX - 1 - x)


def mate_of(x):
    return x + 1 - 2 * (x % 2)


def remote(src, dst, send, recv, to):
    return pltpu.make_async_remote_copy(
        src_ref=src, dst_ref=dst, send_sem=send, recv_sem=recv, device_id=to, device_id_type=MESH
    )


def greet(others):
    barrier = pltpu.get_barrier_semaphore()
    for other in others:
        pl.semaphore_signal(barrier, inc=1, device_id=other, device_id_type=MESH)
    pl.semaphore_wait(barrier, len(others))


def gather_kernel(
    len_ref, pairs_ref, emb_hbm, cot_hbm, wq_hbm, wv_hbm, wo_hbm, table_ref, sib_ref, codes_ref,
    emb, cot, wq, wv, wo, k_send, k_recv, vg_send, vg_recv, seed,
    lsem, k_ssem, k_rsem, vg_ssem, vg_rsem, bsem, ssem, rsem,
):
    z, x, c, y = place()
    mine = y * 2 + c
    sibling = device(z, x, 1 - c, y)
    above, below = (z + 1) % NZ, (z + NZ - 1) % NZ
    mate = device(z, mate_of(x), c, y)
    up, down = device(above, x, c, y), device(below, x, c, y)
    mate_up, mate_down = device(above, mate_of(x), c, y), device(below, mate_of(x), c, y)
    col, mate_col = column_of(x, c), column_of(mate_of(x), c)
    sib_col, sib_mate_col = column_of(x, 1 - c), column_of(mate_of(x), 1 - c)
    kept = c == x // 2

    loads = [
        pltpu.make_async_copy(src, dst, lsem.at[i])
        for i, (src, dst) in enumerate(
            ((emb_hbm, emb), (wq_hbm, wq), (wv_hbm, wv), (cot_hbm, cot), (wo_hbm, wo))
        )
    ]
    for load in loads:
        load.start()
    greet(
        [device(z, x, cd, (y + d) % NY) for d in (1, 2, 3) for cd in (0, 1)]
        + [device(z, NX - 1 - x, cd, (y + d) % NY) for d in range(NY) for cd in (0, 1)]
        + [sibling, mate, up, down, mate_up, mate_down]
    )
    for load in loads:
        load.wait()

    def copies(j, slot, to):
        return (
            remote(k_send.at[j, slot], k_recv.at[j, mine], k_ssem.at[j, slot], k_rsem.at[j, mine], to),
            remote(vg_send.at[j, slot], vg_recv.at[j, mine], vg_ssem.at[j, slot], vg_rsem.at[j, mine], to),
        )

    def project(j):
        rows = slice(j * CROP, (j + 1) * CROP)

        def away(step, carry):
            d = jnp.where(step == 0, 2, jnp.where(step == 1, 1, jnp.where(step == 2, 3, 0)))
            yd = (y + d) % NY
            at = pl.ds(pl.multiple_of(yd * 2 * HDIM, 2 * HDIM), 2 * HDIM)
            k = jnp.dot(emb[rows], wq[:, at], preferred_element_type=jnp.float32).T
            v = jnp.dot(emb[rows], wv[:, at], preferred_element_type=jnp.float32).T.astype(jnp.bfloat16)
            g = lax.dot_general(cot[rows], wo[at, :], NT, preferred_element_type=jnp.float32).T.astype(jnp.bfloat16)
            for h in (0, 1):
                slot = yd * 2 + h
                part = slice(h * HDIM, (h + 1) * HDIM)
                here = kept & (slot == mine)

                @pl.when(here)
                def _():
                    k_recv[j, mine] = k[part]
                    vg_recv[j, mine, :HDIM] = v[part]
                    vg_recv[j, mine, HDIM:] = g[part]

                @pl.when(jnp.logical_not(here))
                def _():
                    k_send[j, slot] = k[part]
                    vg_send[j, slot, :HDIM] = v[part]
                    vg_send[j, slot, HDIM:] = g[part]
                    to = device(z, jnp.where(x // 2 == h, x, NX - 1 - x), x // 2, yd)
                    for copy in copies(j, slot, to):
                        copy.start()

            return carry

        lax.fori_loop(0, NY, away, 0)

    def settle(j):
        def arrive(slot, carry):
            @pl.when(jnp.logical_not(kept & (slot == mine)))
            def _():
                for ref, ss, rs in ((k_recv, k_ssem, k_rsem), (vg_recv, vg_ssem, vg_rsem)):
                    remote(ref.at[j, slot], ref.at[j, slot], ss.at[j, slot], rs.at[j, slot], sibling).wait_recv()

            return carry

        lax.fori_loop(0, HEADS, arrive, 0)
        lanes = lax.broadcasted_iota(jnp.int32, (HDIM, CROP), 1)
        for cs in (0, 1):
            k = (k_recv[j, cs] + k_recv[j, 2 + cs]) + (k_recv[j, 4 + cs] + k_recv[j, 6 + cs])
            vg = [vg_recv[j, 2 * yy + cs].astype(jnp.float32) for yy in range(NY)]
            vg = (vg[0] + vg[1]) + (vg[2] + vg[3])
            ok = lanes < len_ref[(z * NX + col) * LOCALS + 2 * cs + j]
            seed[j, cs, :HDIM] = k.astype(jnp.bfloat16)
            seed[j, cs, HDIM : 2 * HDIM] = vg[:HDIM].astype(jnp.bfloat16)
            seed[j, cs, 2 * HDIM :] = jnp.where(ok, vg[HDIM:], 0.0).astype(jnp.bfloat16)
        keep(j).start()

    def keep(j):
        at = pl.ds(j * 2 * CHIPS + (z * NX + col) * 2, 2)
        return pltpu.make_async_copy(seed.at[j], table_ref.at[at], bsem.at[j])

    def spread(j, cs, sent, first):
        lane = 2 * j + cs

        def part(bz, bx, half):
            at = j * 2 * CHIPS + (bz * NX + bx) * 2 + cs
            if half is None:
                return table_ref.at[at]
            return table_ref.at[at, pl.ds(half * 3 * HDIM // 2, 3 * HDIM // 2)]

        def signal(bz, bx, half):
            return rsem.at[lane, CHIPS + jnp.where(bx == col, 0, 1) if half == 1 else bz * NX + bx]

        def landed(bz, bx, half=None):
            ref = part(bz, bx, half)
            remote(ref, ref, ssem.at[0], signal(bz, bx, half), sibling).wait_recv()

        def push(bz, bx, to, half=None, src=None, far=None):
            dst = part(bz, bx, half)
            sem = signal(bz, bx, half) if far is None else rsem.at[lane, far]
            copy = remote(dst if src is None else src, dst, ssem.at[len(sent)], sem, to)
            copy.start()
            sent.append(copy)

        def hop(s, bx, extra):
            for bz, to, half in (((z + NZ - s) % NZ, up, 0), ((z + s) % NZ, down, 1)):
                landed(bz, bx)
                push(bz, bx, to, half if s == NZ // 2 - 1 else None)
                for other in extra:
                    push(bz, bx, other)

        def meet(bx, extra):
            bz = (z + NZ // 2) % NZ
            landed(bz, bx, 0)
            landed(bz, bx, 1)
            for other in extra:
                push(bz, bx, other)

        def relay(bz):
            landed(bz, mate_col)
            push(bz, mate_col, sibling)

        own = seed.at[j, cs]
        if first == "z":
            for to in (up, down, mate, sibling):
                push(z, col, to, src=own)
            ready = [z]
            yield
            for s in range(1, NZ // 2):
                hop(s, col, (mate, sibling))
                for bz in ready:
                    relay(bz)
                ready = [(z + NZ - s) % NZ, (z + s) % NZ]
                yield
            meet(col, (mate, sibling))
            for bz in ready:
                relay(bz)
            yield
            relay((z + NZ // 2) % NZ)
            yield
        else:
            for to in (up, down, mate_up, mate_down, mate, sibling):
                push(z, col, to, src=own)
            yield
            for s in range(1, NZ // 2):
                for bx in (col, mate_col):
                    hop(s, bx, (sibling,))
                if s == 1:
                    relay(z)
                yield
            for bx in (col, mate_col):
                meet(bx, (sibling,))
            yield
        for bz in range(NZ):
            landed(bz, sib_col)
            landed(bz, sib_mate_col)
        yield

    def whole(first):
        sent = []
        flows = [spread(j, cs, sent, first) for j in (0, 1) for cs in (0, 1)]
        for what in SCHEDULE:
            if what is None:
                settle(1)
            else:
                next(flows[what])
        live = list(flows)
        while live:
            for one in list(live):
                if next(one, 1) == 1:
                    live.remove(one)
        for copy in sent:
            copy.wait_send()

    project(0)
    project(1)
    share = remote(emb, sib_ref, lsem.at[5], lsem.at[6], sibling)
    share.start()
    first = (z * NX + col) * LOCALS
    a, b = pairs_ref[0:1], pairs_ref[1:2]
    owners = lax.broadcasted_iota(jnp.int32, (8, 1), 0) + first // 2
    codes = jnp.where(a // 2 == owners, 1 + (a - first) * CROP + b, 0) + jnp.where(
        b // 2 == owners, 1 + (b - first) * CROP + a, 0
    )
    count = pairs_ref.shape[1]
    each = count // (2 * CHIPS)
    segment = (
        lax.broadcasted_iota(jnp.int32, (count, CROP), 0) // each
        == lax.broadcasted_iota(jnp.int32, (count, CROP), 1)
    ).astype(jnp.float32)
    codes = jnp.dot(
        codes.astype(jnp.float32), segment, precision=lax.Precision.HIGHEST, preferred_element_type=jnp.float32
    )
    index = lax.broadcasted_iota(jnp.int32, (8, CROP), 0)
    named = jnp.where(index < 2, codes[0:1], codes[1:2])
    base = (index * CROP).astype(jnp.float32)
    member = (named > base) & (named <= base + CROP) & (index < LOCALS)
    member = member.astype(jnp.float32)
    before = lax.broadcasted_iota(jnp.int32, (CROP, CROP), 0) < lax.broadcasted_iota(jnp.int32, (CROP, CROP), 1)
    rank = jnp.dot(member, before.astype(jnp.float32), preferred_element_type=jnp.float32)
    many = jnp.broadcast_to(jnp.sum(member, axis=1, keepdims=True), (8, CROP))
    groups = jnp.floor((many + 7.0) * 0.125)
    start, starts = jnp.zeros((1, CROP), jnp.float32), []
    for l in range(LOCALS):
        starts.append(start)
        start = start + 8.0 * groups[l : l + 1]
    starts = jnp.concatenate(starts + [start] * 4, axis=0)
    spot = jnp.where(member > 0, rank + starts, -1.0).T
    partner = (named - base - 1.0).astype(jnp.bfloat16)
    across = lax.broadcasted_iota(jnp.int32, (CROP, 2 * CROP), 1).astype(jnp.float32)
    flat = jnp.zeros((1, 2 * CROP), jnp.float32)
    for l in range(LOCALS):
        hot = (spot[:, l : l + 1] == across).astype(jnp.bfloat16)
        flat = flat + jnp.dot(partner[l : l + 1], hot, preferred_element_type=jnp.float32)
    zero = jnp.zeros((2, CROP), jnp.float32)
    codes_ref[...] = jnp.concatenate(
        [flat[:, :CROP], flat[:, CROP:], zero, many[:LOCALS]], axis=0
    ).astype(jnp.int32)
    settle(0)

    @pl.when(c == 0)
    def _():
        whole("z")

    @pl.when(c == 1)
    def _():
        whole("x")

    for j in (0, 1):

        def leave(slot, carry):
            @pl.when(jnp.logical_not(kept & (slot == mine)))
            def _():
                for copy in copies(j, slot, sibling):
                    copy.wait_send()

            return carry

        lax.fori_loop(0, HEADS, leave, 0)
        keep(j).wait()
    share.wait()


def gather_call(lengths, pairs, emb, cot, w_qk, w_value, w_out):
    rows, width = emb.shape
    smem = pl.BlockSpec(memory_space=pltpu.SMEM)
    vmem = pl.BlockSpec(memory_space=pltpu.VMEM)
    hbm = pl.BlockSpec(memory_space=pl.ANY)
    dma = pltpu.SemaphoreType.DMA
    bf = jnp.bfloat16
    return pl.pallas_call(
        gather_kernel,
        out_shape=(
            jax.ShapeDtypeStruct((CHIPS * LOCALS, 3 * HDIM, CROP), bf),
            jax.ShapeDtypeStruct((rows, width), bf),
            jax.ShapeDtypeStruct((8, CROP), jnp.int32),
        ),
        in_specs=[smem, vmem] + [hbm] * 5,
        out_specs=(hbm, hbm, vmem),
        scratch_shapes=[pltpu.VMEM(v.shape, bf) for v in (emb, cot, w_qk, w_value, w_out)]
        + [
            pltpu.VMEM((2, HEADS, HDIM, CROP), jnp.float32),
            pltpu.VMEM((2, HEADS, HDIM, CROP), jnp.float32),
            pltpu.VMEM((2, HEADS, 2 * HDIM, CROP), bf),
            pltpu.VMEM((2, HEADS, 2 * HDIM, CROP), bf),
            pltpu.VMEM((2, 2, 3 * HDIM, CROP), bf),
            dma((7,)),
            dma((2, HEADS)),
            dma((2, HEADS)),
            dma((2, HEADS)),
            dma((2, HEADS)),
            dma((2,)),
            dma((144,)),
            dma((LOCALS, CHIPS + 2)),
        ],
        compiler_params=pltpu.CompilerParams(
            collective_id=0, has_side_effects=True, vmem_limit_bytes=VMEM_LIMIT
        ),
    )(lengths, pairs, emb, cot, w_qk, w_value, w_out)


def pair_kernel(
    lists_ref, len_ref, first_ref, table_hbm, hid_ref, grad_ref, blocks_ref, own_ref, out_acc, dk_acc, dv_acc, sem, own_sem
):
    counts = [lists_ref[LOCALS + l, 0] for l in range(LOCALS)]
    total = sum((count + 7) // 8 for count in counts)

    def spot(p):
        return (p % 2) * 2 * CHIPS + p // 2

    def partner(group, j):
        return lists_ref[group // 16, (group % 16) * 8 + j]

    def fetch(group, carry):
        for j in range(8):
            pltpu.make_async_copy(
                table_hbm.at[spot(partner(group, j))], blocks_ref.at[group * 8 + j], sem.at[group]
            ).start()
        return carry

    def mine(l):
        return pltpu.make_async_copy(table_hbm.at[spot(first_ref[0] + l)], own_ref.at[l], own_sem.at[l])

    mine(0).start()
    lax.fori_loop(0, total, fetch, 0)
    for l in range(1, LOCALS):
        mine(l).start()
    rows = lax.broadcasted_iota(jnp.int32, (CROP, CROP), 0)
    columns = lax.broadcasted_iota(jnp.int32, (1, CROP), 1)
    done = 0
    for l in range(LOCALS):
        me = first_ref[0] + l
        row_bias = jnp.where(rows < len_ref[me], 0.0, -1e30)
        count = counts[l]
        mine(l).wait()
        own = own_ref[l].astype(jnp.float32)
        kp = own[:HDIM].T.astype(jnp.bfloat16)
        vp = own[HDIM : 2 * HDIM].T.astype(jnp.bfloat16)
        gp = own[2 * HDIM :].T.astype(jnp.bfloat16)
        out_acc[...] = jnp.zeros_like(out_acc)
        dk_acc[...] = jnp.zeros_like(dk_acc)
        dv_acc[...] = jnp.zeros_like(dv_acc)

        def step(base, group, at):
            pltpu.make_async_copy(
                table_hbm.at[pl.ds(0, 8)], blocks_ref.at[pl.ds(at * 8, 8)], sem.at[at]
            ).wait()
            blocks, lens, live = [], [], []
            for j in range(group):
                blocks.append(blocks_ref[at * 8 + j])
                lens.append(len_ref[partner(at, j)])
                live.append(jnp.where(base + j < count, 1.0, 0.0))
            many = jnp.concatenate(blocks, axis=1)
            kq, vq, gq = many[:HDIM], many[HDIM : 2 * HDIM], many[2 * HDIM :]
            scores = jnp.dot(kp, kq, preferred_element_type=jnp.float32)
            d_rows = jnp.dot(gp, vq, preferred_element_type=jnp.float32)
            d_cols = jnp.dot(vp, gq, preferred_element_type=jnp.float32)
            a_parts, b_parts, ds_parts = [], [], []
            for j in range(group):
                part = slice(j * CROP, (j + 1) * CROP)
                s = scores[:, part] * SCALE
                sa = s + jnp.where(columns < lens[j], 0.0, -1e30)
                ea = jnp.exp2(sa - jnp.max(sa, axis=1, keepdims=True))
                a = ea * (live[j] / jnp.sum(ea, axis=1, keepdims=True))
                sb = s + row_bias
                eb = jnp.exp2(sb - jnp.max(sb, axis=0, keepdims=True))
                b = eb * (live[j] / jnp.sum(eb, axis=0, keepdims=True))
                ta = a * d_rows[:, part]
                tb = b * d_cols[:, part]
                ds = (ta - a * jnp.sum(ta, axis=1, keepdims=True)) + (
                    tb - b * jnp.sum(tb, axis=0, keepdims=True)
                )
                a_parts.append(a.astype(jnp.bfloat16))
                b_parts.append(b.astype(jnp.bfloat16))
                ds_parts.append(ds.astype(jnp.bfloat16))
            for acc, parts, other in ((out_acc, a_parts, vq), (dv_acc, b_parts, gq), (dk_acc, ds_parts, kq)):
                acc[...] += lax.dot_general(
                    jnp.concatenate(parts, axis=1), other, NT, preferred_element_type=jnp.float32
                )

        def eight(i, carry):
            step(i * 8, 8, done + i)
            return carry

        def four(i, carry):
            step(big * 8, 4, done + big)
            return carry

        big = (count + 3) // 8
        lax.fori_loop(0, big, eight, 0)
        lax.fori_loop(0, jnp.where(count > big * 8, 1, 0), four, 0)
        done = done + (count + 7) // 8
        ok = rows[:, :HDIM] < len_ref[me]
        hid_ref[l // 2, :, (l % 2) * HDIM : (l % 2 + 1) * HDIM] = jnp.where(ok, out_acc[...], 0.0).astype(
            jnp.bfloat16
        )
        turned = jnp.concatenate([dk_acc[...] * HDIM**-0.5, dv_acc[...]], axis=1).T
        for core in range(2):
            eights = []
            for xd in range(NX):
                at = (xd * 2 + core) * 8
                eights += [turned[at : at + 8], turned[HDIM + at : HDIM + at + 8]]
            grad_ref[core, :, l * CROP : (l + 1) * CROP] = jnp.concatenate(eights, axis=0).astype(jnp.bfloat16)


def pair_call(lists, lengths, first, table):
    smem = pl.BlockSpec(memory_space=pltpu.SMEM)
    vmem = pl.BlockSpec(memory_space=pltpu.VMEM)
    hbm = pl.BlockSpec(memory_space=pl.ANY)
    return pl.pallas_call(
        pair_kernel,
        out_shape=(
            jax.ShapeDtypeStruct((2, CROP, 2 * HDIM), jnp.bfloat16),
            jax.ShapeDtypeStruct((2, HDIM, LOCALS * CROP), jnp.bfloat16),
        ),
        in_specs=[smem, smem, smem, hbm],
        out_specs=(vmem, vmem),
        scratch_shapes=[
            pltpu.VMEM((8 * GROUPS, 3 * HDIM, CROP), jnp.bfloat16),
            pltpu.VMEM((LOCALS, 3 * HDIM, CROP), jnp.bfloat16),
            pltpu.VMEM((CROP, HDIM), jnp.float32),
            pltpu.VMEM((CROP, HDIM), jnp.float32),
            pltpu.VMEM((CROP, HDIM), jnp.float32),
            pltpu.SemaphoreType.DMA((GROUPS,)),
            pltpu.SemaphoreType.DMA((LOCALS,)),
        ],
        compiler_params=pltpu.CompilerParams(vmem_limit_bytes=VMEM_LIMIT),
    )(lists, lengths, first, table)


def ring_sum(n, term, plus, minus, send, recv, ssem, rsem, done):
    steps = n // 2
    half = send.shape[-1] // 2
    sent = []
    for s in range(steps):
        d = steps - s
        for way, to in ((0, plus), (1, minus)):
            own = slice(way * half, (way + 1) * half)
            rest = slice((1 - way) * half, (2 - way) * half)
            value = term(d if way == 0 else n - d)
            if s > 0:
                landing = recv.at[way, s - 1, :, own] if s == 1 else recv.at[way, s - 1]
                remote(landing, landing, ssem.at[way, s - 1], rsem.at[way, s - 1], to).wait_recv()
            send[way, s, :, own] = (
                value[:, own] if s == 0 else value[:, own] + recv[way, s - 1, :, own].astype(jnp.float32)
            ).astype(jnp.bfloat16)
            if s == 1:
                send[way, s, :, rest] = value[:, rest].astype(jnp.bfloat16)
            elif s > 1:
                send[way, s, :, rest] = (
                    value[:, rest] + recv[way, s - 1, :, rest].astype(jnp.float32)
                ).astype(jnp.bfloat16)
            spot = own if s == 0 else slice(None)
            copy = remote(
                send.at[way, s, :, spot], recv.at[way, s, :, spot], ssem.at[way, s], rsem.at[way, s], to
            )
            copy.start()
            sent.append(copy)
        yield
    total = term(0)
    for way, to in ((0, plus), (1, minus)):
        landing = recv.at[way, steps - 1]
        remote(landing, landing, ssem.at[way, steps - 1], rsem.at[way, steps - 1], to).wait_recv()
        total = total + recv[way, steps - 1].astype(jnp.float32)
    done(total)
    for copy in sent:
        copy.wait_send()
    yield


def together(*rings):
    live = list(rings)
    while live:
        for one in list(live):
            if next(one, 1) == 1:
                live.remove(one)


def finish_kernel(
    hid_ref, grad_ref, emb_hbm, sib_hbm, hidden_ref, qk_ref, value_ref,
    emb, sib, hid_recv, g_recv, terms, z_send, z_recv, x_send, x_recv, line, last_send, last_recv,
    lsem, h_ssem, h_rsem, g_ssem, g_rsem, zs_sem, zr_sem, xs_sem, xr_sem, ls_sem, lr_sem,
):
    z, x, c, y = place()
    col = column_of(x, c)
    kept = c == x // 2
    mine = 2 * y + x // 2
    loads = [pltpu.make_async_copy(emb_hbm, emb, lsem.at[0]), pltpu.make_async_copy(sib_hbm, sib, lsem.at[1])]
    for load in loads:
        load.start()
    sibling = device(z, x, 1 - c, y)
    up, down = device((z + 1) % NZ, x, c, y), device((z + NZ - 1) % NZ, x, c, y)
    east, west = device(z, (x + 1) % NX, c, y), device(z, (x + NX - 1) % NX, c, y)
    near = [device(z, x, cd, (y + d) % NY) for d in (1, 2, 3) for cd in (0, 1)] + [sibling]
    near += [device(z, NX - 1 - x, cd, (y + d) % NY) for d in range(NY) for cd in (0, 1)]
    near += [device(z, (x + d) % NX, c, y) for d in range(1, NX)]
    near += [device((z + d) % NZ, x, c, y) for d in range(1, NZ)]
    greet(near)

    ways = [(d, cd) for d in (2, 1, 3, 0) for cd in (0, 1)]

    def outgoing(d, cd, kind):
        yd = (y + d) % NY
        slot = yd * 2 + cd
        to = device(z, col, cd, yd)
        if kind == 0:
            return remote(grad_ref.at[cd], g_recv.at[mine], g_ssem.at[slot], g_rsem.at[mine], to)
        return remote(hid_ref.at[cd], hid_recv.at[mine], h_ssem.at[slot], h_rsem.at[mine], to)

    def away(d, cd):
        return jnp.logical_not(kept & (cd == c)) if d == 0 else None

    def launch(kind):
        for d, cd in ways:
            if d:
                outgoing(d, cd, kind).start()
            else:

                @pl.when(away(d, cd))
                def _():
                    outgoing(d, cd, kind).start()

    launch(0)

    @pl.when(kept)
    def _():
        g_recv[mine] = grad_ref[c]
        hid_recv[mine] = hid_ref[c]

    def arrive(ref, ss, rs):
        def one(slot, carry):
            @pl.when(jnp.logical_not(kept & (slot == mine)))
            def _():
                remote(ref.at[slot], ref.at[slot], ss.at[slot], rs.at[slot], sibling).wait_recv()

            return carry

        lax.fori_loop(0, HEADS, one, 0)

    for load in loads:
        load.wait()
    arrive(g_recv, g_ssem, g_rsem)
    launch(1)
    width = emb.shape[-1]
    all_g = g_recv[...].reshape(HEADS * HDIM, LOCALS * CROP)
    own = jnp.where(c == 0, all_g[:, : 2 * CROP], all_g[:, 2 * CROP :])
    theirs = jnp.where(c == 0, all_g[:, 2 * CROP :], all_g[:, : 2 * CROP])
    terms[...] = (
        jnp.dot(own, emb[...], preferred_element_type=jnp.float32)
        + jnp.dot(theirs, sib[...], preferred_element_type=jnp.float32)
    ).reshape(terms.shape)

    def finish(n, term, to):
        sends = []
        for d in sorted(range(1, n), key=lambda d: -min(d, n - d)):
            last_send[d] = term(d).astype(jnp.bfloat16)
            copy = remote(last_send.at[d], last_recv.at[d], ls_sem.at[d], lr_sem.at[d], to(d))
            copy.start()
            sends.append(copy)
        total = term(0)
        for copy in sends:
            copy.wait_recv()
        for d in range(1, n):
            total = total + last_recv[d].astype(jnp.float32)
        qk_ref[...] = total[:8]
        value_ref[...] = total[8:]
        for copy in sends:
            copy.wait_send()

    def heads():
        arrive(hid_recv, h_ssem, h_rsem)
        low = lax.broadcasted_iota(jnp.int32, (CROP, 2 * HDIM), 1) < HDIM
        for yy in range(NY):
            even = hid_recv[2 * yy].astype(jnp.float32)
            odd = hid_recv[2 * yy + 1].astype(jnp.float32)
            at = slice(yy * 2 * HDIM, (yy + 1) * 2 * HDIM)
            hidden_ref[:CROP, at] = jnp.where(low, even, pltpu.roll(odd, HDIM, 1)).astype(jnp.bfloat16)
            hidden_ref[CROP:, at] = jnp.where(low, pltpu.roll(even, HDIM, 1), odd).astype(jnp.bfloat16)

    @pl.when(c == 0)
    def _():
        def ring(i):
            def done(total):
                line[2 * i : 2 * i + 2] = total.reshape(2, 16, width)

            return ring_sum(
                NZ,
                lambda d: terms[(z + d) % NZ, 2 * i : 2 * i + 2].reshape(32, width),
                up, down, z_send.at[i], z_recv.at[i], zs_sem.at[i], zr_sem.at[i], done,
            )

        together(ring(0), ring(1))
        finish(NX, lambda d: line[(x + d) % NX], lambda d: device(z, (x + d) % NX, c, y))

    @pl.when(c == 1)
    def _():
        def ring(i):
            def done(total):
                line[4 * i : 4 * i + 4] = total.reshape(4, 16, width)

            return ring_sum(
                NX,
                lambda d: terms[4 * i : 4 * i + 4, (x + d) % NX].reshape(64, width),
                east, west, x_send.at[i], x_recv.at[i], xs_sem.at[i], xr_sem.at[i], done,
            )

        together(ring(0), ring(1))
        finish(NZ, lambda d: line[(z + d) % NZ], lambda d: device((z + d) % NZ, x, c, y))

    heads()
    for d, cd in ways:
        for kind in (0, 1):
            if d:
                outgoing(d, cd, kind).wait_send()
            else:

                @pl.when(away(d, cd))
                def _():
                    outgoing(d, cd, kind).wait_send()


def finish_call(hid, grads, emb, sib):
    rows, width = emb.shape
    vmem = pl.BlockSpec(memory_space=pltpu.VMEM)
    hbm = pl.BlockSpec(memory_space=pl.ANY)
    dma = pltpu.SemaphoreType.DMA
    bf = jnp.bfloat16
    return pl.pallas_call(
        finish_kernel,
        out_shape=(
            jax.ShapeDtypeStruct((rows, HEADS * HDIM), bf),
            jax.ShapeDtypeStruct((8, width), jnp.float32),
            jax.ShapeDtypeStruct((8, width), jnp.float32),
        ),
        in_specs=[vmem, vmem, hbm, hbm],
        out_specs=(vmem, vmem, vmem),
        scratch_shapes=[
            pltpu.VMEM((rows, width), bf),
            pltpu.VMEM((rows, width), bf),
            pltpu.VMEM((HEADS, CROP, 2 * HDIM), bf),
            pltpu.VMEM((HEADS, HDIM, LOCALS * CROP), bf),
            pltpu.VMEM((NZ, NX, 16, width), jnp.float32),
            pltpu.VMEM((2, 2, NZ // 2, 32, width), bf),
            pltpu.VMEM((2, 2, NZ // 2, 32, width), bf),
            pltpu.VMEM((2, 2, NX // 2, 64, width), bf),
            pltpu.VMEM((2, 2, NX // 2, 64, width), bf),
            pltpu.VMEM((NZ, 16, width), jnp.float32),
            pltpu.VMEM((NZ, 16, width), bf),
            pltpu.VMEM((NZ, 16, width), bf),
            dma((2,)),
            dma((HEADS,)),
            dma((HEADS,)),
            dma((HEADS,)),
            dma((HEADS,)),
            dma((2, 2, NZ // 2)),
            dma((2, 2, NZ // 2)),
            dma((2, 2, NX // 2)),
            dma((2, 2, NX // 2)),
            dma((NZ,)),
            dma((NZ,)),
        ],
        compiler_params=pltpu.CompilerParams(
            collective_id=1, has_side_effects=True, vmem_limit_bytes=VMEM_LIMIT
        ),
    )(hid, grads, emb, sib)


def output_kernel(hidden_ref, wo_ref, qk_ref, value_ref, att_ref, out_qk_ref, out_value_ref):
    att_ref[...] = jnp.dot(hidden_ref[...], wo_ref[...], preferred_element_type=jnp.float32).astype(jnp.bfloat16)
    out_qk_ref[...] = qk_ref[...]
    out_value_ref[...] = value_ref[...]


def output_call(hidden, w_out, grad_qk, grad_value):
    vmem = pl.BlockSpec(memory_space=pltpu.VMEM)
    return pl.pallas_call(
        output_kernel,
        out_shape=(
            jax.ShapeDtypeStruct((hidden.shape[0], w_out.shape[1]), jnp.bfloat16),
            jax.ShapeDtypeStruct(grad_qk.shape, grad_qk.dtype),
            jax.ShapeDtypeStruct(grad_value.shape, grad_value.dtype),
        ),
        in_specs=[vmem] * 4,
        out_specs=(vmem,) * 3,
        compiler_params=pltpu.CompilerParams(vmem_limit_bytes=VMEM_LIMIT),
    )(hidden, w_out, grad_qk, grad_value)


def on_device(embeddings, cotangent, w_qk, w_value, w_out, lengths, pair_list):
    owned, crop, width = embeddings.shape
    rows = owned * crop
    emb = embeddings.reshape(rows, width)
    z, x, c, _ = place()
    first = LOCALS * (z * NX + column_of(x, c))
    table, sib, lists = gather_call(
        lengths, pair_list.T, emb, cotangent.reshape(rows, width), w_qk, w_value, w_out
    )
    hid, grads = pair_call(lists, lengths, first.reshape(1), table)
    hidden, grad_qk, grad_value = finish_call(hid, grads, emb, sib)
    attended, grad_qk, grad_value = output_call(hidden, w_out, grad_qk, grad_value)
    return (attended.reshape(embeddings.shape), grad_qk.T, grad_value.T)


def solution(mesh):
    in_specs = (
        P("pairs", None, "mp"),
        P("pairs", None, "mp"),
        P("mp", None),
        P("mp", None),
        P(None, "mp"),
        P(),
        P(),
    )
    out_specs = (P("pairs", None, "mp"), P("mp", "pairs"), P("mp", "pairs"))
    return jax.shard_map(on_device, mesh=mesh, in_specs=in_specs, out_specs=out_specs, check_vma=False)
```

```python
import math

import jax
import jax.numpy as jnp
from jax import lax
from jax.experimental import pallas as pl
from jax.experimental.pallas import tpu as pltpu
from jax.sharding import PartitionSpec as P

HDIM = 64
CROP = 128
SCALE = HDIM**-0.5 * math.log2(math.e)
NT = (((1,), (1,)), ((), ()))
NZ, NX, NY = 8, 4, 4
CHIPS = NZ * NX
LOCALS = 4
HEADS = 2 * NY
GROUPS = 20
MESH = pl.DeviceIdType.MESH
VMEM_LIMIT = 56 * 1024 * 1024
SCHEDULE = (0, 1, None, 2, 3)


def place():
    me = lax.axis_index("pairs")
    chip = me // 2
    return chip // NX, chip % NX, me % 2, lax.axis_index("mp")


def device(z, x, c, y):
    return ((z * NX + x) * 2 + c, y)


def column_of(x, c):
    return jnp.where(c == x // 2, x, NX - 1 - x)


def mate_of(x):
    return x + 1 - 2 * (x % 2)


def remote(src, dst, send, recv, to):
    return pltpu.make_async_remote_copy(
        src_ref=src, dst_ref=dst, send_sem=send, recv_sem=recv, device_id=to, device_id_type=MESH
    )


def greet(others):
    barrier = pltpu.get_barrier_semaphore()
    for other in others:
        pl.semaphore_signal(barrier, inc=1, device_id=other, device_id_type=MESH)
    pl.semaphore_wait(barrier, len(others))


def gather_kernel(
    len_ref, pairs_ref, emb_hbm, cot_hbm, wq_hbm, wv_hbm, wo_hbm, table_ref, sib_ref, codes_ref,
    emb, cot, wq, wv, wo, k_send, k_recv, vg_send, vg_recv, seed,
    lsem, k_ssem, k_rsem, vg_ssem, vg_rsem, bsem, ssem, rsem,
):
    z, x, c, y = place()
    mine = y * 2 + c
    sibling = device(z, x, 1 - c, y)
    above, below = (z + 1) % NZ, (z + NZ - 1) % NZ
    mate = device(z, mate_of(x), c, y)
    up, down = device(above, x, c, y), device(below, x, c, y)
    mate_up, mate_down = device(above, mate_of(x), c, y), device(below, mate_of(x), c, y)
    col, mate_col = column_of(x, c), column_of(mate_of(x), c)
    sib_col, sib_mate_col = column_of(x, 1 - c), column_of(mate_of(x), 1 - c)
    kept = c == x // 2

    loads = [
        pltpu.make_async_copy(src, dst, lsem.at[i])
        for i, (src, dst) in enumerate(
            ((emb_hbm, emb), (wq_hbm, wq), (wv_hbm, wv), (cot_hbm, cot), (wo_hbm, wo))
        )
    ]
    for load in loads:
        load.start()
    greet(
        [device(z, x, cd, (y + d) % NY) for d in (1, 2, 3) for cd in (0, 1)]
        + [device(z, NX - 1 - x, cd, (y + d) % NY) for d in range(NY) for cd in (0, 1)]
        + [sibling, mate, up, down, mate_up, mate_down]
    )
    for load in loads:
        load.wait()

    def copies(j, slot, to):
        return (
            remote(k_send.at[j, slot], k_recv.at[j, mine], k_ssem.at[j, slot], k_rsem.at[j, mine], to),
            remote(vg_send.at[j, slot], vg_recv.at[j, mine], vg_ssem.at[j, slot], vg_rsem.at[j, mine], to),
        )

    def project(j):
        rows = slice(j * CROP, (j + 1) * CROP)

        def away(step, carry):
            d = jnp.where(step == 0, 2, jnp.where(step == 1, 1, jnp.where(step == 2, 3, 0)))
            yd = (y + d) % NY
            at = pl.ds(pl.multiple_of(yd * 2 * HDIM, 2 * HDIM), 2 * HDIM)
            k = jnp.dot(emb[rows], wq[:, at], preferred_element_type=jnp.float32).T
            v = jnp.dot(emb[rows], wv[:, at], preferred_element_type=jnp.float32).T.astype(jnp.bfloat16)
            g = lax.dot_general(cot[rows], wo[at, :], NT, preferred_element_type=jnp.float32).T.astype(jnp.bfloat16)
            for h in (0, 1):
                slot = yd * 2 + h
                part = slice(h * HDIM, (h + 1) * HDIM)
                here = kept & (slot == mine)

                @pl.when(here)
                def _():
                    k_recv[j, mine] = k[part]
                    vg_recv[j, mine, :HDIM] = v[part]
                    vg_recv[j, mine, HDIM:] = g[part]

                @pl.when(jnp.logical_not(here))
                def _():
                    k_send[j, slot] = k[part]
                    vg_send[j, slot, :HDIM] = v[part]
                    vg_send[j, slot, HDIM:] = g[part]
                    to = device(z, jnp.where(x // 2 == h, x, NX - 1 - x), x // 2, yd)
                    for copy in copies(j, slot, to):
                        copy.start()

            return carry

        lax.fori_loop(0, NY, away, 0)

    def settle(j):
        def arrive(slot, carry):
            @pl.when(jnp.logical_not(kept & (slot == mine)))
            def _():
                for ref, ss, rs in ((k_recv, k_ssem, k_rsem), (vg_recv, vg_ssem, vg_rsem)):
                    remote(ref.at[j, slot], ref.at[j, slot], ss.at[j, slot], rs.at[j, slot], sibling).wait_recv()

            return carry

        lax.fori_loop(0, HEADS, arrive, 0)
        lanes = lax.broadcasted_iota(jnp.int32, (HDIM, CROP), 1)
        for cs in (0, 1):
            k = (k_recv[j, cs] + k_recv[j, 2 + cs]) + (k_recv[j, 4 + cs] + k_recv[j, 6 + cs])
            vg = [vg_recv[j, 2 * yy + cs].astype(jnp.float32) for yy in range(NY)]
            vg = (vg[0] + vg[1]) + (vg[2] + vg[3])
            ok = lanes < len_ref[(z * NX + col) * LOCALS + 2 * cs + j]
            seed[j, cs, :HDIM] = k.astype(jnp.bfloat16)
            seed[j, cs, HDIM : 2 * HDIM] = vg[:HDIM].astype(jnp.bfloat16)
            seed[j, cs, 2 * HDIM :] = jnp.where(ok, vg[HDIM:], 0.0).astype(jnp.bfloat16)
        keep(j).start()

    def keep(j):
        at = pl.ds(j * 2 * CHIPS + (z * NX + col) * 2, 2)
        return pltpu.make_async_copy(seed.at[j], table_ref.at[at], bsem.at[j])

    def spread(j, cs, sent, first):
        lane = 2 * j + cs

        def part(bz, bx, half):
            at = j * 2 * CHIPS + (bz * NX + bx) * 2 + cs
            if half is None:
                return table_ref.at[at]
            return table_ref.at[at, pl.ds(half * 3 * HDIM // 2, 3 * HDIM // 2)]

        def signal(bz, bx, half):
            return rsem.at[lane, CHIPS + jnp.where(bx == col, 0, 1) if half == 1 else bz * NX + bx]

        def landed(bz, bx, half=None):
            ref = part(bz, bx, half)
            remote(ref, ref, ssem.at[0], signal(bz, bx, half), sibling).wait_recv()

        def push(bz, bx, to, half=None, src=None, far=None):
            dst = part(bz, bx, half)
            sem = signal(bz, bx, half) if far is None else rsem.at[lane, far]
            copy = remote(dst if src is None else src, dst, ssem.at[len(sent)], sem, to)
            copy.start()
            sent.append(copy)

        def hop(s, bx, extra):
            for bz, to, half in (((z + NZ - s) % NZ, up, 0), ((z + s) % NZ, down, 1)):
                landed(bz, bx)
                push(bz, bx, to, half if s == NZ // 2 - 1 else None)
                for other in extra:
                    push(bz, bx, other)

        def meet(bx, extra):
            bz = (z + NZ // 2) % NZ
            landed(bz, bx, 0)
            landed(bz, bx, 1)
            for other in extra:
                push(bz, bx, other)

        def relay(bz):
            landed(bz, mate_col)
            push(bz, mate_col, sibling)

        own = seed.at[j, cs]
        if first == "z":
            for to in (up, down, mate, sibling):
                push(z, col, to, src=own)
            ready = [z]
            yield
            for s in range(1, NZ // 2):
                hop(s, col, (mate, sibling))
                for bz in ready:
                    relay(bz)
                ready = [(z + NZ - s) % NZ, (z + s) % NZ]
                yield
            meet(col, (mate, sibling))
            for bz in ready:
                relay(bz)
            yield
            relay((z + NZ // 2) % NZ)
            yield
        else:
            for to in (up, down, mate_up, mate_down, mate, sibling):
                push(z, col, to, src=own)
            yield
            for s in range(1, NZ // 2):
                for bx in (col, mate_col):
                    hop(s, bx, (sibling,))
                if s == 1:
                    relay(z)
                yield
            for bx in (col, mate_col):
                meet(bx, (sibling,))
            yield
        for bz in range(NZ):
            landed(bz, sib_col)
            landed(bz, sib_mate_col)
        yield

    def whole(first):
        sent = []
        flows = [spread(j, cs, sent, first) for j in (0, 1) for cs in (0, 1)]
        for what in SCHEDULE:
            if what is None:
                settle(1)
            else:
                next(flows[what])
        live = list(flows)
        while live:
            for one in list(live):
                if next(one, 1) == 1:
                    live.remove(one)
        for copy in sent:
            copy.wait_send()

    project(0)
    project(1)
    share = remote(emb, sib_ref, lsem.at[5], lsem.at[6], sibling)
    share.start()
    first = (z * NX + col) * LOCALS
    a, b = pairs_ref[0:1], pairs_ref[1:2]
    owners = lax.broadcasted_iota(jnp.int32, (8, 1), 0) + first // 2
    codes = jnp.where(a // 2 == owners, 1 + (a - first) * CROP + b, 0) + jnp.where(
        b // 2 == owners, 1 + (b - first) * CROP + a, 0
    )
    count = pairs_ref.shape[1]
    each = count // (2 * CHIPS)
    segment = (
        lax.broadcasted_iota(jnp.int32, (count, CROP), 0) // each
        == lax.broadcasted_iota(jnp.int32, (count, CROP), 1)
    ).astype(jnp.float32)
    codes = jnp.dot(
        codes.astype(jnp.float32), segment, precision=lax.Precision.HIGHEST, preferred_element_type=jnp.float32
    )
    index = lax.broadcasted_iota(jnp.int32, (8, CROP), 0)
    named = jnp.where(index < 2, codes[0:1], codes[1:2])
    base = (index * CROP).astype(jnp.float32)
    member = (named > base) & (named <= base + CROP) & (index < LOCALS)
    member = member.astype(jnp.float32)
    before = lax.broadcasted_iota(jnp.int32, (CROP, CROP), 0) < lax.broadcasted_iota(jnp.int32, (CROP, CROP), 1)
    rank = jnp.dot(member, before.astype(jnp.float32), preferred_element_type=jnp.float32)
    many = jnp.broadcast_to(jnp.sum(member, axis=1, keepdims=True), (8, CROP))
    groups = jnp.floor((many + 7.0) * 0.125)
    start, starts = jnp.zeros((1, CROP), jnp.float32), []
    for l in range(LOCALS):
        starts.append(start)
        start = start + 8.0 * groups[l : l + 1]
    starts = jnp.concatenate(starts + [start] * 4, axis=0)
    spot = jnp.where(member > 0, rank + starts, -1.0).T
    partner = (named - base - 1.0).astype(jnp.bfloat16)
    across = lax.broadcasted_iota(jnp.int32, (CROP, 2 * CROP), 1).astype(jnp.float32)
    flat = jnp.zeros((1, 2 * CROP), jnp.float32)
    for l in range(LOCALS):
        hot = (spot[:, l : l + 1] == across).astype(jnp.bfloat16)
        flat = flat + jnp.dot(partner[l : l + 1], hot, preferred_element_type=jnp.float32)
    zero = jnp.zeros((2, CROP), jnp.float32)
    codes_ref[...] = jnp.concatenate(
        [flat[:, :CROP], flat[:, CROP:], zero, many[:LOCALS]], axis=0
    ).astype(jnp.int32)
    settle(0)

    @pl.when(c == 0)
    def _():
        whole("z")

    @pl.when(c == 1)
    def _():
        whole("x")

    for j in (0, 1):

        def leave(slot, carry):
            @pl.when(jnp.logical_not(kept & (slot == mine)))
            def _():
                for copy in copies(j, slot, sibling):
                    copy.wait_send()

            return carry

        lax.fori_loop(0, HEADS, leave, 0)
        keep(j).wait()
    share.wait()


def gather_call(lengths, pairs, emb, cot, w_qk, w_value, w_out):
    rows, width = emb.shape
    smem = pl.BlockSpec(memory_space=pltpu.SMEM)
    vmem = pl.BlockSpec(memory_space=pltpu.VMEM)
    hbm = pl.BlockSpec(memory_space=pl.ANY)
    dma = pltpu.SemaphoreType.DMA
    bf = jnp.bfloat16
    return pl.pallas_call(
        gather_kernel,
        out_shape=(
            jax.ShapeDtypeStruct((CHIPS * LOCALS, 3 * HDIM, CROP), bf),
            jax.ShapeDtypeStruct((rows, width), bf),
            jax.ShapeDtypeStruct((8, CROP), jnp.int32),
        ),
        in_specs=[smem, vmem] + [hbm] * 5,
        out_specs=(hbm, hbm, vmem),
        scratch_shapes=[pltpu.VMEM(v.shape, bf) for v in (emb, cot, w_qk, w_value, w_out)]
        + [
            pltpu.VMEM((2, HEADS, HDIM, CROP), jnp.float32),
            pltpu.VMEM((2, HEADS, HDIM, CROP), jnp.float32),
            pltpu.VMEM((2, HEADS, 2 * HDIM, CROP), bf),
            pltpu.VMEM((2, HEADS, 2 * HDIM, CROP), bf),
            pltpu.VMEM((2, 2, 3 * HDIM, CROP), bf),
            dma((7,)),
            dma((2, HEADS)),
            dma((2, HEADS)),
            dma((2, HEADS)),
            dma((2, HEADS)),
            dma((2,)),
            dma((144,)),
            dma((LOCALS, CHIPS + 2)),
        ],
        compiler_params=pltpu.CompilerParams(
            collective_id=0, has_side_effects=True, vmem_limit_bytes=VMEM_LIMIT
        ),
    )(lengths, pairs, emb, cot, w_qk, w_value, w_out)


def pair_kernel(
    lists_ref, len_ref, first_ref, table_hbm, hid_ref, grad_ref, blocks_ref, own_ref, out_acc, dk_acc, dv_acc, sem, own_sem
):
    counts = [lists_ref[LOCALS + l, 0] for l in range(LOCALS)]
    total = sum((count + 7) // 8 for count in counts)

    def spot(p):
        return (p % 2) * 2 * CHIPS + p // 2

    def partner(group, j):
        return lists_ref[group // 16, (group % 16) * 8 + j]

    def fetch(group, carry):
        for j in range(8):
            pltpu.make_async_copy(
                table_hbm.at[spot(partner(group, j))], blocks_ref.at[group * 8 + j], sem.at[group]
            ).start()
        return carry

    def mine(l):
        return pltpu.make_async_copy(table_hbm.at[spot(first_ref[0] + l)], own_ref.at[l], own_sem.at[l])

    mine(0).start()
    lax.fori_loop(0, total, fetch, 0)
    for l in range(1, LOCALS):
        mine(l).start()
    rows = lax.broadcasted_iota(jnp.int32, (CROP, CROP), 0)
    columns = lax.broadcasted_iota(jnp.int32, (1, CROP), 1)
    done = 0
    for l in range(LOCALS):
        me = first_ref[0] + l
        row_bias = jnp.where(rows < len_ref[me], 0.0, -1e30)
        count = counts[l]
        mine(l).wait()
        own = own_ref[l].astype(jnp.float32)
        kp = own[:HDIM].T.astype(jnp.bfloat16)
        vp = own[HDIM : 2 * HDIM].T.astype(jnp.bfloat16)
        gp = own[2 * HDIM :].T.astype(jnp.bfloat16)
        out_acc[...] = jnp.zeros_like(out_acc)
        dk_acc[...] = jnp.zeros_like(dk_acc)
        dv_acc[...] = jnp.zeros_like(dv_acc)

        def step(base, group, at):
            pltpu.make_async_copy(
                table_hbm.at[pl.ds(0, 8)], blocks_ref.at[pl.ds(at * 8, 8)], sem.at[at]
            ).wait()
            blocks, lens, live = [], [], []
            for j in range(group):
                blocks.append(blocks_ref[at * 8 + j])
                lens.append(len_ref[partner(at, j)])
                live.append(jnp.where(base + j < count, 1.0, 0.0))
            many = jnp.concatenate(blocks, axis=1)
            kq, vq, gq = many[:HDIM], many[HDIM : 2 * HDIM], many[2 * HDIM :]
            scores = jnp.dot(kp, kq, preferred_element_type=jnp.float32)
            d_rows = jnp.dot(gp, vq, preferred_element_type=jnp.float32)
            d_cols = jnp.dot(vp, gq, preferred_element_type=jnp.float32)
            a_parts, b_parts, ds_parts = [], [], []
            for j in range(group):
                part = slice(j * CROP, (j + 1) * CROP)
                s = scores[:, part] * SCALE
                sa = s + jnp.where(columns < lens[j], 0.0, -1e30)
                ea = jnp.exp2(sa - jnp.max(sa, axis=1, keepdims=True))
                a = ea * (live[j] / jnp.sum(ea, axis=1, keepdims=True))
                sb = s + row_bias
                eb = jnp.exp2(sb - jnp.max(sb, axis=0, keepdims=True))
                b = eb * (live[j] / jnp.sum(eb, axis=0, keepdims=True))
                ta = a * d_rows[:, part]
                tb = b * d_cols[:, part]
                ds = (ta - a * jnp.sum(ta, axis=1, keepdims=True)) + (
                    tb - b * jnp.sum(tb, axis=0, keepdims=True)
                )
                a_parts.append(a.astype(jnp.bfloat16))
                b_parts.append(b.astype(jnp.bfloat16))
                ds_parts.append(ds.astype(jnp.bfloat16))
            for acc, parts, other in ((out_acc, a_parts, vq), (dv_acc, b_parts, gq), (dk_acc, ds_parts, kq)):
                acc[...] += lax.dot_general(
                    jnp.concatenate(parts, axis=1), other, NT, preferred_element_type=jnp.float32
                )

        def eight(i, carry):
            step(i * 8, 8, done + i)
            return carry

        def four(i, carry):
            step(big * 8, 4, done + big)
            return carry

        big = (count + 3) // 8
        lax.fori_loop(0, big, eight, 0)
        lax.fori_loop(0, jnp.where(count > big * 8, 1, 0), four, 0)
        done = done + (count + 7) // 8
        ok = rows[:, :HDIM] < len_ref[me]
        hid_ref[l // 2, :, (l % 2) * HDIM : (l % 2 + 1) * HDIM] = jnp.where(ok, out_acc[...], 0.0).astype(
            jnp.bfloat16
        )
        turned = jnp.concatenate([dk_acc[...] * HDIM**-0.5, dv_acc[...]], axis=1).T
        for core in range(2):
            eights = []
            for xd in range(NX):
                at = (xd * 2 + core) * 8
                eights += [turned[at : at + 8], turned[HDIM + at : HDIM + at + 8]]
            grad_ref[core, :, l * CROP : (l + 1) * CROP] = jnp.concatenate(eights, axis=0).astype(jnp.bfloat16)


def pair_call(lists, lengths, first, table):
    smem = pl.BlockSpec(memory_space=pltpu.SMEM)
    vmem = pl.BlockSpec(memory_space=pltpu.VMEM)
    hbm = pl.BlockSpec(memory_space=pl.ANY)
    return pl.pallas_call(
        pair_kernel,
        out_shape=(
            jax.ShapeDtypeStruct((2, CROP, 2 * HDIM), jnp.bfloat16),
            jax.ShapeDtypeStruct((2, HDIM, LOCALS * CROP), jnp.bfloat16),
        ),
        in_specs=[smem, smem, smem, hbm],
        out_specs=(vmem, vmem),
        scratch_shapes=[
            pltpu.VMEM((8 * GROUPS, 3 * HDIM, CROP), jnp.bfloat16),
            pltpu.VMEM((LOCALS, 3 * HDIM, CROP), jnp.bfloat16),
            pltpu.VMEM((CROP, HDIM), jnp.float32),
            pltpu.VMEM((CROP, HDIM), jnp.float32),
            pltpu.VMEM((CROP, HDIM), jnp.float32),
            pltpu.SemaphoreType.DMA((GROUPS,)),
            pltpu.SemaphoreType.DMA((LOCALS,)),
        ],
        compiler_params=pltpu.CompilerParams(vmem_limit_bytes=VMEM_LIMIT),
    )(lists, lengths, first, table)


def ring_sum(n, term, plus, minus, send, recv, ssem, rsem, done):
    steps = n // 2
    half = send.shape[-1] // 2
    sent = []
    for s in range(steps):
        d = steps - s
        for way, to in ((0, plus), (1, minus)):
            own = slice(way * half, (way + 1) * half)
            rest = slice((1 - way) * half, (2 - way) * half)
            value = term(d if way == 0 else n - d)
            if s > 0:
                landing = recv.at[way, s - 1, :, own] if s == 1 else recv.at[way, s - 1]
                remote(landing, landing, ssem.at[way, s - 1], rsem.at[way, s - 1], to).wait_recv()
            send[way, s, :, own] = (
                value[:, own] if s == 0 else value[:, own] + recv[way, s - 1, :, own].astype(jnp.float32)
            ).astype(jnp.bfloat16)
            if s == 1:
                send[way, s, :, rest] = value[:, rest].astype(jnp.bfloat16)
            elif s > 1:
                send[way, s, :, rest] = (
                    value[:, rest] + recv[way, s - 1, :, rest].astype(jnp.float32)
                ).astype(jnp.bfloat16)
            spot = own if s == 0 else slice(None)
            copy = remote(
                send.at[way, s, :, spot], recv.at[way, s, :, spot], ssem.at[way, s], rsem.at[way, s], to
            )
            copy.start()
            sent.append(copy)
        yield
    total = term(0)
    for way, to in ((0, plus), (1, minus)):
        landing = recv.at[way, steps - 1]
        remote(landing, landing, ssem.at[way, steps - 1], rsem.at[way, steps - 1], to).wait_recv()
        total = total + recv[way, steps - 1].astype(jnp.float32)
    done(total)
    for copy in sent:
        copy.wait_send()
    yield


def line_sum(term, ways, send, recv, ssem, rsem, done):
    half = send.shape[-1] // 2
    whole = slice(None)
    sent = []

    def copy(way, s, spot, to):
        return remote(send.at[way, s, :, spot], recv.at[way, s, :, spot], ssem.at[way, s], rsem.at[way, s], to)

    def go(way, s, spot, to):
        sent.append(copy(way, s, spot, to))
        sent[-1].start()

    def got(way, s, spot):
        copy(way, s, spot, ways[way][0]).wait_recv()
        return recv[way, s, :, spot].astype(jnp.float32)

    for way, (one, two) in enumerate(ways):
        own = slice(way * half, (way + 1) * half)
        send[way, 0, :, own] = term(4)[:, own].astype(jnp.bfloat16)
        go(way, 0, own, two)
        send[way, 1] = term(3 if way == 0 else 5).astype(jnp.bfloat16)
        go(way, 1, whole, one)
    yield
    for way, (one, two) in enumerate(ways):
        own = slice(way * half, (way + 1) * half)
        rest = slice((1 - way) * half, (2 - way) * half)
        value = term(2 if way == 0 else 6) + got(way, 1, whole)
        send[way, 2, :, rest] = value[:, rest].astype(jnp.bfloat16)
        send[way, 2, :, own] = (value[:, own] + got(way, 0, own)).astype(jnp.bfloat16)
        go(way, 2, whole, one)
    yield
    for way, (one, two) in enumerate(ways):
        send[way, 3] = (term(1 if way == 0 else 7) + got(way, 2, whole)).astype(jnp.bfloat16)
        go(way, 3, whole, one)
    yield
    done(term(0) + got(0, 3, whole) + got(1, 3, whole))
    for one in sent:
        one.wait_send()
    yield


def together(*rings):
    live = list(rings)
    while live:
        for one in list(live):
            if next(one, 1) == 1:
                live.remove(one)


def finish_kernel(
    hid_ref, grad_ref, emb_hbm, sib_hbm, hidden_ref, qk_ref, value_ref,
    emb, sib, hid_recv, g_recv, terms, z_send, z_recv, x_send, x_recv, line, last_send, last_recv,
    lsem, h_ssem, h_rsem, g_ssem, g_rsem, zs_sem, zr_sem, xs_sem, xr_sem, ls_sem, lr_sem,
):
    z, x, c, y = place()
    col = column_of(x, c)
    kept = c == x // 2
    mine = 2 * y + x // 2
    loads = [pltpu.make_async_copy(emb_hbm, emb, lsem.at[0]), pltpu.make_async_copy(sib_hbm, sib, lsem.at[1])]
    for load in loads:
        load.start()
    sibling = device(z, x, 1 - c, y)
    up, down = device((z + 1) % NZ, x, c, y), device((z + NZ - 1) % NZ, x, c, y)
    east, west = device(z, (x + 1) % NX, c, y), device(z, (x + NX - 1) % NX, c, y)
    near = [device(z, x, cd, (y + d) % NY) for d in (1, 2, 3) for cd in (0, 1)] + [sibling]
    near += [device(z, NX - 1 - x, cd, (y + d) % NY) for d in range(NY) for cd in (0, 1)]
    near += [device(z, (x + d) % NX, c, y) for d in range(1, NX)]
    near += [device((z + d) % NZ, x, c, y) for d in range(1, NZ)]
    greet(near)

    ways = [(d, cd) for d in (2, 1, 3, 0) for cd in (0, 1)]

    def outgoing(d, cd, kind):
        yd = (y + d) % NY
        slot = yd * 2 + cd
        to = device(z, col, cd, yd)
        if kind == 0:
            return remote(grad_ref.at[cd], g_recv.at[mine], g_ssem.at[slot], g_rsem.at[mine], to)
        return remote(hid_ref.at[cd], hid_recv.at[mine], h_ssem.at[slot], h_rsem.at[mine], to)

    def away(d, cd):
        return jnp.logical_not(kept & (cd == c)) if d == 0 else None

    def launch(kind):
        for d, cd in ways:
            if d:
                outgoing(d, cd, kind).start()
            else:

                @pl.when(away(d, cd))
                def _():
                    outgoing(d, cd, kind).start()

    launch(0)

    @pl.when(kept)
    def _():
        g_recv[mine] = grad_ref[c]
        hid_recv[mine] = hid_ref[c]

    def arrive(ref, ss, rs):
        def one(slot, carry):
            @pl.when(jnp.logical_not(kept & (slot == mine)))
            def _():
                remote(ref.at[slot], ref.at[slot], ss.at[slot], rs.at[slot], sibling).wait_recv()

            return carry

        lax.fori_loop(0, HEADS, one, 0)

    for load in loads:
        load.wait()
    arrive(g_recv, g_ssem, g_rsem)
    launch(1)
    width = emb.shape[-1]
    all_g = g_recv[...].reshape(HEADS * HDIM, LOCALS * CROP)
    own = jnp.where(c == 0, all_g[:, : 2 * CROP], all_g[:, 2 * CROP :])
    theirs = jnp.where(c == 0, all_g[:, 2 * CROP :], all_g[:, : 2 * CROP])
    terms[...] = (
        jnp.dot(own, emb[...], preferred_element_type=jnp.float32)
        + jnp.dot(theirs, sib[...], preferred_element_type=jnp.float32)
    ).reshape(terms.shape)

    def finish(n, term, to):
        sends = []
        for d in sorted(range(1, n), key=lambda d: -min(d, n - d)):
            last_send[d] = term(d).astype(jnp.bfloat16)
            copy = remote(last_send.at[d], last_recv.at[d], ls_sem.at[d], lr_sem.at[d], to(d))
            copy.start()
            sends.append(copy)
        total = term(0)
        for copy in sends:
            copy.wait_recv()
        for d in range(1, n):
            total = total + last_recv[d].astype(jnp.float32)
        qk_ref[...] = total[:8]
        value_ref[...] = total[8:]
        for copy in sends:
            copy.wait_send()

    def heads():
        arrive(hid_recv, h_ssem, h_rsem)
        low = lax.broadcasted_iota(jnp.int32, (CROP, 2 * HDIM), 1) < HDIM
        for yy in range(NY):
            even = hid_recv[2 * yy].astype(jnp.float32)
            odd = hid_recv[2 * yy + 1].astype(jnp.float32)
            at = slice(yy * 2 * HDIM, (yy + 1) * 2 * HDIM)
            hidden_ref[:CROP, at] = jnp.where(low, even, pltpu.roll(odd, HDIM, 1)).astype(jnp.bfloat16)
            hidden_ref[CROP:, at] = jnp.where(low, pltpu.roll(even, HDIM, 1), odd).astype(jnp.bfloat16)

    @pl.when(c == 0)
    def _():
        def ring(i):
            def done(total):
                line[2 * i : 2 * i + 2] = total.reshape(2, 16, width)

            return line_sum(
                lambda d: terms[(z + d) % NZ, 2 * i : 2 * i + 2].reshape(32, width),
                ((up, device((z + 2) % NZ, x, c, y)), (down, device((z + NZ - 2) % NZ, x, c, y))), z_send.at[i], z_recv.at[i], zs_sem.at[i], zr_sem.at[i], done,
            )

        together(ring(0), ring(1))
        finish(NX, lambda d: line[(x + d) % NX], lambda d: device(z, (x + d) % NX, c, y))

    @pl.when(c == 1)
    def _():
        def ring(i):
            def done(total):
                line[4 * i : 4 * i + 4] = total.reshape(4, 16, width)

            return ring_sum(
                NX,
                lambda d: terms[4 * i : 4 * i + 4, (x + d) % NX].reshape(64, width),
                east, west, x_send.at[i], x_recv.at[i], xs_sem.at[i], xr_sem.at[i], done,
            )

        together(ring(0), ring(1))
        finish(NZ, lambda d: line[(z + d) % NZ], lambda d: device((z + d) % NZ, x, c, y))

    heads()
    for d, cd in ways:
        for kind in (0, 1):
            if d:
                outgoing(d, cd, kind).wait_send()
            else:

                @pl.when(away(d, cd))
                def _():
                    outgoing(d, cd, kind).wait_send()


def finish_call(hid, grads, emb, sib):
    rows, width = emb.shape
    vmem = pl.BlockSpec(memory_space=pltpu.VMEM)
    hbm = pl.BlockSpec(memory_space=pl.ANY)
    dma = pltpu.SemaphoreType.DMA
    bf = jnp.bfloat16
    return pl.pallas_call(
        finish_kernel,
        out_shape=(
            jax.ShapeDtypeStruct((rows, HEADS * HDIM), bf),
            jax.ShapeDtypeStruct((8, width), jnp.float32),
            jax.ShapeDtypeStruct((8, width), jnp.float32),
        ),
        in_specs=[vmem, vmem, hbm, hbm],
        out_specs=(vmem, vmem, vmem),
        scratch_shapes=[
            pltpu.VMEM((rows, width), bf),
            pltpu.VMEM((rows, width), bf),
            pltpu.VMEM((HEADS, CROP, 2 * HDIM), bf),
            pltpu.VMEM((HEADS, HDIM, LOCALS * CROP), bf),
            pltpu.VMEM((NZ, NX, 16, width), jnp.float32),
            pltpu.VMEM((2, 2, NZ // 2, 32, width), bf),
            pltpu.VMEM((2, 2, NZ // 2, 32, width), bf),
            pltpu.VMEM((2, 2, NX // 2, 64, width), bf),
            pltpu.VMEM((2, 2, NX // 2, 64, width), bf),
            pltpu.VMEM((NZ, 16, width), jnp.float32),
            pltpu.VMEM((NZ, 16, width), bf),
            pltpu.VMEM((NZ, 16, width), bf),
            dma((2,)),
            dma((HEADS,)),
            dma((HEADS,)),
            dma((HEADS,)),
            dma((HEADS,)),
            dma((2, 2, NZ // 2)),
            dma((2, 2, NZ // 2)),
            dma((2, 2, NX // 2)),
            dma((2, 2, NX // 2)),
            dma((NZ,)),
            dma((NZ,)),
        ],
        compiler_params=pltpu.CompilerParams(
            collective_id=1, has_side_effects=True, vmem_limit_bytes=VMEM_LIMIT
        ),
    )(hid, grads, emb, sib)


def output_kernel(hidden_ref, wo_ref, qk_ref, value_ref, att_ref, out_qk_ref, out_value_ref):
    att_ref[...] = jnp.dot(hidden_ref[...], wo_ref[...], preferred_element_type=jnp.float32).astype(jnp.bfloat16)
    out_qk_ref[...] = qk_ref[...]
    out_value_ref[...] = value_ref[...]


def output_call(hidden, w_out, grad_qk, grad_value):
    vmem = pl.BlockSpec(memory_space=pltpu.VMEM)
    return pl.pallas_call(
        output_kernel,
        out_shape=(
            jax.ShapeDtypeStruct((hidden.shape[0], w_out.shape[1]), jnp.bfloat16),
            jax.ShapeDtypeStruct(grad_qk.shape, grad_qk.dtype),
            jax.ShapeDtypeStruct(grad_value.shape, grad_value.dtype),
        ),
        in_specs=[vmem] * 4,
        out_specs=(vmem,) * 3,
        compiler_params=pltpu.CompilerParams(vmem_limit_bytes=VMEM_LIMIT),
    )(hidden, w_out, grad_qk, grad_value)


def on_device(embeddings, cotangent, w_qk, w_value, w_out, lengths, pair_list):
    owned, crop, width = embeddings.shape
    rows = owned * crop
    emb = embeddings.reshape(rows, width)
    z, x, c, _ = place()
    first = LOCALS * (z * NX + column_of(x, c))
    table, sib, lists = gather_call(
        lengths, pair_list.T, emb, cotangent.reshape(rows, width), w_qk, w_value, w_out
    )
    hid, grads = pair_call(lists, lengths, first.reshape(1), table)
    hidden, grad_qk, grad_value = finish_call(hid, grads, emb, sib)
    attended, grad_qk, grad_value = output_call(hidden, w_out, grad_qk, grad_value)
    return (attended.reshape(embeddings.shape), grad_qk.T, grad_value.T)


def solution(mesh):
    in_specs = (
        P("pairs", None, "mp"),
        P("pairs", None, "mp"),
        P("mp", None),
        P("mp", None),
        P(None, "mp"),
        P(),
        P(),
    )
    out_specs = (P("pairs", None, "mp"), P("mp", "pairs"), P("mp", "pairs"))
    return jax.shard_map(on_device, mesh=mesh, in_specs=in_specs, out_specs=out_specs, check_vma=False)
```

```python
import math

import jax
import jax.numpy as jnp
from jax import lax
from jax.experimental import pallas as pl
from jax.experimental.pallas import tpu as pltpu
from jax.sharding import PartitionSpec as P

HDIM = 64
CROP = 128
SCALE = HDIM**-0.5 * math.log2(math.e)
NT = (((1,), (1,)), ((), ()))
NZ, NX, NY = 8, 4, 4
CHIPS = NZ * NX
LOCALS = 4
HEADS = 2 * NY
GROUPS = 20
PIECES = 2
MESH = pl.DeviceIdType.MESH
VMEM_LIMIT = 56 * 1024 * 1024
SCHEDULE = (0, 1, None, 2, 3)


def place():
    me = lax.axis_index("pairs")
    chip = me // 2
    return chip // NX, chip % NX, me % 2, lax.axis_index("mp")


def device(z, x, c, y):
    return ((z * NX + x) * 2 + c, y)


def column_of(x, c):
    return jnp.where(c == x // 2, x, NX - 1 - x)


def mate_of(x):
    return x + 1 - 2 * (x % 2)


def remote(src, dst, send, recv, to):
    return pltpu.make_async_remote_copy(
        src_ref=src, dst_ref=dst, send_sem=send, recv_sem=recv, device_id=to, device_id_type=MESH
    )


def greet(others):
    barrier = pltpu.get_barrier_semaphore()
    for other in others:
        pl.semaphore_signal(barrier, inc=1, device_id=other, device_id_type=MESH)
    pl.semaphore_wait(barrier, len(others))


def gather_kernel(
    len_ref, pairs_ref, emb_hbm, cot_hbm, wq_hbm, wv_hbm, wo_hbm, table_ref, sib_ref, codes_ref,
    emb, cot, wq, wv, wo, k_send, k_recv, vg_send, vg_recv, seed,
    lsem, k_ssem, k_rsem, vg_ssem, vg_rsem, bsem, ssem, rsem,
):
    z, x, c, y = place()
    mine = y * 2 + c
    sibling = device(z, x, 1 - c, y)
    above, below = (z + 1) % NZ, (z + NZ - 1) % NZ
    mate = device(z, mate_of(x), c, y)
    up, down = device(above, x, c, y), device(below, x, c, y)
    mate_up, mate_down = device(above, mate_of(x), c, y), device(below, mate_of(x), c, y)
    col, mate_col = column_of(x, c), column_of(mate_of(x), c)
    sib_col, sib_mate_col = column_of(x, 1 - c), column_of(mate_of(x), 1 - c)
    kept = c == x // 2

    loads = [
        pltpu.make_async_copy(src, dst, lsem.at[i])
        for i, (src, dst) in enumerate(
            ((emb_hbm, emb), (wq_hbm, wq), (wv_hbm, wv), (cot_hbm, cot), (wo_hbm, wo))
        )
    ]
    for load in loads:
        load.start()
    greet(
        [device(z, x, cd, (y + d) % NY) for d in (1, 2, 3) for cd in (0, 1)]
        + [device(z, NX - 1 - x, cd, (y + d) % NY) for d in range(NY) for cd in (0, 1)]
        + [sibling, mate, up, down, mate_up, mate_down]
    )
    for load in loads:
        load.wait()

    def copies(j, slot, to):
        return (
            remote(k_send.at[j, slot], k_recv.at[j, mine], k_ssem.at[j, slot], k_rsem.at[j, mine], to),
            remote(vg_send.at[j, slot], vg_recv.at[j, mine], vg_ssem.at[j, slot], vg_rsem.at[j, mine], to),
        )

    def project(j):
        rows = slice(j * CROP, (j + 1) * CROP)

        def away(step, carry):
            d = jnp.where(step == 0, 2, jnp.where(step == 1, 1, jnp.where(step == 2, 3, 0)))
            yd = (y + d) % NY
            at = pl.ds(pl.multiple_of(yd * 2 * HDIM, 2 * HDIM), 2 * HDIM)
            k = jnp.dot(emb[rows], wq[:, at], preferred_element_type=jnp.float32).T
            v = jnp.dot(emb[rows], wv[:, at], preferred_element_type=jnp.float32).T.astype(jnp.bfloat16)
            g = lax.dot_general(cot[rows], wo[at, :], NT, preferred_element_type=jnp.float32).T.astype(jnp.bfloat16)
            for h in (0, 1):
                slot = yd * 2 + h
                part = slice(h * HDIM, (h + 1) * HDIM)
                here = kept & (slot == mine)

                @pl.when(here)
                def _():
                    k_recv[j, mine] = k[part]
                    vg_recv[j, mine, :HDIM] = v[part]
                    vg_recv[j, mine, HDIM:] = g[part]

                @pl.when(jnp.logical_not(here))
                def _():
                    k_send[j, slot] = k[part]
                    vg_send[j, slot, :HDIM] = v[part]
                    vg_send[j, slot, HDIM:] = g[part]
                    to = device(z, jnp.where(x // 2 == h, x, NX - 1 - x), x // 2, yd)
                    for copy in copies(j, slot, to):
                        copy.start()

            return carry

        lax.fori_loop(0, NY, away, 0)

    def settle(j):
        def arrive(slot, carry):
            @pl.when(jnp.logical_not(kept & (slot == mine)))
            def _():
                for ref, ss, rs in ((k_recv, k_ssem, k_rsem), (vg_recv, vg_ssem, vg_rsem)):
                    remote(ref.at[j, slot], ref.at[j, slot], ss.at[j, slot], rs.at[j, slot], sibling).wait_recv()

            return carry

        lax.fori_loop(0, HEADS, arrive, 0)
        lanes = lax.broadcasted_iota(jnp.int32, (HDIM, CROP), 1)
        for cs in (0, 1):
            k = (k_recv[j, cs] + k_recv[j, 2 + cs]) + (k_recv[j, 4 + cs] + k_recv[j, 6 + cs])
            vg = [vg_recv[j, 2 * yy + cs].astype(jnp.float32) for yy in range(NY)]
            vg = (vg[0] + vg[1]) + (vg[2] + vg[3])
            ok = lanes < len_ref[(z * NX + col) * LOCALS + 2 * cs + j]
            seed[j, cs, :HDIM] = k.astype(jnp.bfloat16)
            seed[j, cs, HDIM : 2 * HDIM] = vg[:HDIM].astype(jnp.bfloat16)
            seed[j, cs, 2 * HDIM :] = jnp.where(ok, vg[HDIM:], 0.0).astype(jnp.bfloat16)
        keep(j).start()

    def keep(j):
        at = pl.ds(j * 2 * CHIPS + (z * NX + col) * 2, 2)
        return pltpu.make_async_copy(seed.at[j], table_ref.at[at], bsem.at[j])

    def spread(j, cs, sent, first):
        lane = 2 * j + cs

        def part(bz, bx, half):
            at = j * 2 * CHIPS + (bz * NX + bx) * 2 + cs
            if half is None:
                return table_ref.at[at]
            return table_ref.at[at, pl.ds(half * 3 * HDIM // 2, 3 * HDIM // 2)]

        def signal(bz, bx, half):
            return rsem.at[lane, CHIPS + jnp.where(bx == col, 0, 1) if half == 1 else bz * NX + bx]

        def landed(bz, bx, half=None):
            ref = part(bz, bx, half)
            remote(ref, ref, ssem.at[0], signal(bz, bx, half), sibling).wait_recv()

        def push(bz, bx, to, half=None, src=None, far=None):
            dst = part(bz, bx, half)
            sem = signal(bz, bx, half) if far is None else rsem.at[lane, far]
            copy = remote(dst if src is None else src, dst, ssem.at[len(sent)], sem, to)
            copy.start()
            sent.append(copy)

        def hop(s, bx, extra):
            for bz, to, half in (((z + NZ - s) % NZ, up, 0), ((z + s) % NZ, down, 1)):
                landed(bz, bx)
                push(bz, bx, to, half if s == NZ // 2 - 1 else None)
                for other in extra:
                    push(bz, bx, other)

        def meet(bx, extra):
            bz = (z + NZ // 2) % NZ
            landed(bz, bx, 0)
            landed(bz, bx, 1)
            for other in extra:
                push(bz, bx, other)

        def relay(bz):
            landed(bz, mate_col)
            push(bz, mate_col, sibling)

        own = seed.at[j, cs]
        if first == "z":
            for to in (up, down, mate, sibling):
                push(z, col, to, src=own)
            ready = [z]
            yield
            for s in range(1, NZ // 2):
                hop(s, col, (mate, sibling))
                for bz in ready:
                    relay(bz)
                ready = [(z + NZ - s) % NZ, (z + s) % NZ]
                yield
            meet(col, (mate, sibling))
            for bz in ready:
                relay(bz)
            yield
            relay((z + NZ // 2) % NZ)
            yield
        else:
            for to in (up, down, mate_up, mate_down, mate, sibling):
                push(z, col, to, src=own)
            yield
            for s in range(1, NZ // 2):
                for bx in (col, mate_col):
                    hop(s, bx, (sibling,))
                if s == 1:
                    relay(z)
                yield
            for bx in (col, mate_col):
                meet(bx, (sibling,))
            yield
        for bz in range(NZ):
            landed(bz, sib_col)
            landed(bz, sib_mate_col)
        yield

    def whole(first):
        sent = []
        flows = [spread(j, cs, sent, first) for j in (0, 1) for cs in (0, 1)]
        for what in SCHEDULE:
            if what is None:
                settle(1)
            else:
                next(flows[what])
        live = list(flows)
        while live:
            for one in list(live):
                if next(one, 1) == 1:
                    live.remove(one)
        for copy in sent:
            copy.wait_send()

    project(0)
    project(1)
    share = remote(emb, sib_ref, lsem.at[5], lsem.at[6], sibling)
    share.start()
    first = (z * NX + col) * LOCALS
    a, b = pairs_ref[0:1], pairs_ref[1:2]
    owners = lax.broadcasted_iota(jnp.int32, (8, 1), 0) + first // 2
    codes = jnp.where(a // 2 == owners, 1 + (a - first) * CROP + b, 0) + jnp.where(
        b // 2 == owners, 1 + (b - first) * CROP + a, 0
    )
    count = pairs_ref.shape[1]
    each = count // (2 * CHIPS)
    segment = (
        lax.broadcasted_iota(jnp.int32, (count, CROP), 0) // each
        == lax.broadcasted_iota(jnp.int32, (count, CROP), 1)
    ).astype(jnp.float32)
    codes = jnp.dot(
        codes.astype(jnp.float32), segment, precision=lax.Precision.HIGHEST, preferred_element_type=jnp.float32
    )
    index = lax.broadcasted_iota(jnp.int32, (8, CROP), 0)
    named = jnp.where(index < 2, codes[0:1], codes[1:2])
    base = (index * CROP).astype(jnp.float32)
    member = (named > base) & (named <= base + CROP) & (index < LOCALS)
    member = member.astype(jnp.float32)
    before = lax.broadcasted_iota(jnp.int32, (CROP, CROP), 0) < lax.broadcasted_iota(jnp.int32, (CROP, CROP), 1)
    rank = jnp.dot(member, before.astype(jnp.float32), preferred_element_type=jnp.float32)
    many = jnp.broadcast_to(jnp.sum(member, axis=1, keepdims=True), (8, CROP))
    groups = jnp.floor((many + 7.0) * 0.125)
    start, starts = jnp.zeros((1, CROP), jnp.float32), []
    for l in range(LOCALS):
        starts.append(start)
        start = start + 8.0 * groups[l : l + 1]
    starts = jnp.concatenate(starts + [start] * 4, axis=0)
    spot = jnp.where(member > 0, rank + starts, -1.0).T
    partner = (named - base - 1.0).astype(jnp.bfloat16)
    across = lax.broadcasted_iota(jnp.int32, (CROP, 2 * CROP), 1).astype(jnp.float32)
    flat = jnp.zeros((1, 2 * CROP), jnp.float32)
    for l in range(LOCALS):
        hot = (spot[:, l : l + 1] == across).astype(jnp.bfloat16)
        flat = flat + jnp.dot(partner[l : l + 1], hot, preferred_element_type=jnp.float32)
    zero = jnp.zeros((2, CROP), jnp.float32)
    codes_ref[...] = jnp.concatenate(
        [flat[:, :CROP], flat[:, CROP:], zero, many[:LOCALS]], axis=0
    ).astype(jnp.int32)
    settle(0)

    @pl.when(c == 0)
    def _():
        whole("z")

    @pl.when(c == 1)
    def _():
        whole("x")

    for j in (0, 1):

        def leave(slot, carry):
            @pl.when(jnp.logical_not(kept & (slot == mine)))
            def _():
                for copy in copies(j, slot, sibling):
                    copy.wait_send()

            return carry

        lax.fori_loop(0, HEADS, leave, 0)
        keep(j).wait()
    share.wait()


def gather_call(lengths, pairs, emb, cot, w_qk, w_value, w_out):
    rows, width = emb.shape
    smem = pl.BlockSpec(memory_space=pltpu.SMEM)
    vmem = pl.BlockSpec(memory_space=pltpu.VMEM)
    hbm = pl.BlockSpec(memory_space=pl.ANY)
    dma = pltpu.SemaphoreType.DMA
    bf = jnp.bfloat16
    return pl.pallas_call(
        gather_kernel,
        out_shape=(
            jax.ShapeDtypeStruct((CHIPS * LOCALS, 3 * HDIM, CROP), bf),
            jax.ShapeDtypeStruct((rows, width), bf),
            jax.ShapeDtypeStruct((8, CROP), jnp.int32),
        ),
        in_specs=[smem, vmem] + [hbm] * 5,
        out_specs=(hbm, hbm, vmem),
        scratch_shapes=[pltpu.VMEM(v.shape, bf) for v in (emb, cot, w_qk, w_value, w_out)]
        + [
            pltpu.VMEM((2, HEADS, HDIM, CROP), jnp.float32),
            pltpu.VMEM((2, HEADS, HDIM, CROP), jnp.float32),
            pltpu.VMEM((2, HEADS, 2 * HDIM, CROP), bf),
            pltpu.VMEM((2, HEADS, 2 * HDIM, CROP), bf),
            pltpu.VMEM((2, 2, 3 * HDIM, CROP), bf),
            dma((7,)),
            dma((2, HEADS)),
            dma((2, HEADS)),
            dma((2, HEADS)),
            dma((2, HEADS)),
            dma((2,)),
            dma((144,)),
            dma((LOCALS, CHIPS + 2)),
        ],
        compiler_params=pltpu.CompilerParams(
            collective_id=0, has_side_effects=True, vmem_limit_bytes=VMEM_LIMIT
        ),
    )(lengths, pairs, emb, cot, w_qk, w_value, w_out)


def pair_kernel(
    lists_ref, len_ref, first_ref, table_hbm, hid_ref, grad_ref, blocks_ref, own_ref, out_acc, dk_acc, dv_acc, sem, own_sem
):
    counts = [lists_ref[LOCALS + l, 0] for l in range(LOCALS)]
    total = sum((count + 7) // 8 for count in counts)

    def spot(p):
        return (p % 2) * 2 * CHIPS + p // 2

    def partner(group, j):
        return lists_ref[group // 16, (group % 16) * 8 + j]

    def fetch(group, carry):
        for j in range(8):
            pltpu.make_async_copy(
                table_hbm.at[spot(partner(group, j))], blocks_ref.at[group * 8 + j], sem.at[group]
            ).start()
        return carry

    def mine(l):
        return pltpu.make_async_copy(table_hbm.at[spot(first_ref[0] + l)], own_ref.at[l], own_sem.at[l])

    mine(0).start()
    lax.fori_loop(0, total, fetch, 0)
    for l in range(1, LOCALS):
        mine(l).start()
    rows = lax.broadcasted_iota(jnp.int32, (CROP, CROP), 0)
    columns = lax.broadcasted_iota(jnp.int32, (1, CROP), 1)
    done = 0
    for l in range(LOCALS):
        me = first_ref[0] + l
        row_bias = jnp.where(rows < len_ref[me], 0.0, -1e30)
        count = counts[l]
        mine(l).wait()
        own = own_ref[l].astype(jnp.float32)
        kp = own[:HDIM].T.astype(jnp.bfloat16)
        vp = own[HDIM : 2 * HDIM].T.astype(jnp.bfloat16)
        gp = own[2 * HDIM :].T.astype(jnp.bfloat16)
        out_acc[...] = jnp.zeros_like(out_acc)
        dk_acc[...] = jnp.zeros_like(dk_acc)
        dv_acc[...] = jnp.zeros_like(dv_acc)

        def step(base, group, at):
            pltpu.make_async_copy(
                table_hbm.at[pl.ds(0, 8)], blocks_ref.at[pl.ds(at * 8, 8)], sem.at[at]
            ).wait()
            blocks, lens, live = [], [], []
            for j in range(group):
                blocks.append(blocks_ref[at * 8 + j])
                lens.append(len_ref[partner(at, j)])
                live.append(jnp.where(base + j < count, 1.0, 0.0))
            many = jnp.concatenate(blocks, axis=1)
            kq, vq, gq = many[:HDIM], many[HDIM : 2 * HDIM], many[2 * HDIM :]
            scores = jnp.dot(kp, kq, preferred_element_type=jnp.float32)
            d_rows = jnp.dot(gp, vq, preferred_element_type=jnp.float32)
            d_cols = jnp.dot(vp, gq, preferred_element_type=jnp.float32)
            a_parts, b_parts, ds_parts = [], [], []
            for j in range(group):
                part = slice(j * CROP, (j + 1) * CROP)
                s = scores[:, part] * SCALE
                sa = s + jnp.where(columns < lens[j], 0.0, -1e30)
                ea = jnp.exp2(sa - jnp.max(sa, axis=1, keepdims=True))
                a = ea * (live[j] / jnp.sum(ea, axis=1, keepdims=True))
                sb = s + row_bias
                eb = jnp.exp2(sb - jnp.max(sb, axis=0, keepdims=True))
                b = eb * (live[j] / jnp.sum(eb, axis=0, keepdims=True))
                ta = a * d_rows[:, part]
                tb = b * d_cols[:, part]
                ds = (ta - a * jnp.sum(ta, axis=1, keepdims=True)) + (
                    tb - b * jnp.sum(tb, axis=0, keepdims=True)
                )
                a_parts.append(a.astype(jnp.bfloat16))
                b_parts.append(b.astype(jnp.bfloat16))
                ds_parts.append(ds.astype(jnp.bfloat16))
            for acc, parts, other in ((out_acc, a_parts, vq), (dv_acc, b_parts, gq), (dk_acc, ds_parts, kq)):
                acc[...] += lax.dot_general(
                    jnp.concatenate(parts, axis=1), other, NT, preferred_element_type=jnp.float32
                )

        def eight(i, carry):
            step(i * 8, 8, done + i)
            return carry

        def four(i, carry):
            step(big * 8, 4, done + big)
            return carry

        big = (count + 3) // 8
        lax.fori_loop(0, big, eight, 0)
        lax.fori_loop(0, jnp.where(count > big * 8, 1, 0), four, 0)
        done = done + (count + 7) // 8
        ok = rows[:, :HDIM] < len_ref[me]
        hid_ref[l // 2, :, (l % 2) * HDIM : (l % 2 + 1) * HDIM] = jnp.where(ok, out_acc[...], 0.0).astype(
            jnp.bfloat16
        )
        turned = jnp.concatenate([dk_acc[...] * HDIM**-0.5, dv_acc[...]], axis=1).T
        for core in range(2):
            eights = []
            for xd in range(NX):
                at = (xd * 2 + core) * 8
                eights += [turned[at : at + 8], turned[HDIM + at : HDIM + at + 8]]
            grad_ref[core, :, l * CROP : (l + 1) * CROP] = jnp.concatenate(eights, axis=0).astype(jnp.bfloat16)


def pair_call(lists, lengths, first, table):
    smem = pl.BlockSpec(memory_space=pltpu.SMEM)
    vmem = pl.BlockSpec(memory_space=pltpu.VMEM)
    hbm = pl.BlockSpec(memory_space=pl.ANY)
    return pl.pallas_call(
        pair_kernel,
        out_shape=(
            jax.ShapeDtypeStruct((2, CROP, 2 * HDIM), jnp.bfloat16),
            jax.ShapeDtypeStruct((2, HDIM, LOCALS * CROP), jnp.bfloat16),
        ),
        in_specs=[smem, smem, smem, hbm],
        out_specs=(vmem, vmem),
        scratch_shapes=[
            pltpu.VMEM((8 * GROUPS, 3 * HDIM, CROP), jnp.bfloat16),
            pltpu.VMEM((LOCALS, 3 * HDIM, CROP), jnp.bfloat16),
            pltpu.VMEM((CROP, HDIM), jnp.float32),
            pltpu.VMEM((CROP, HDIM), jnp.float32),
            pltpu.VMEM((CROP, HDIM), jnp.float32),
            pltpu.SemaphoreType.DMA((GROUPS,)),
            pltpu.SemaphoreType.DMA((LOCALS,)),
        ],
        compiler_params=pltpu.CompilerParams(vmem_limit_bytes=VMEM_LIMIT),
    )(lists, lengths, first, table)


def ring_sum(n, term, plus, minus, send, recv, ssem, rsem, done):
    steps = n // 2
    half = send.shape[-1] // 2
    sent = []
    for s in range(steps):
        d = steps - s
        for way, to in ((0, plus), (1, minus)):
            own = slice(way * half, (way + 1) * half)
            rest = slice((1 - way) * half, (2 - way) * half)
            value = term(d if way == 0 else n - d)
            if s > 0:
                landing = recv.at[way, s - 1, :, own] if s == 1 else recv.at[way, s - 1]
                remote(landing, landing, ssem.at[way, s - 1], rsem.at[way, s - 1], to).wait_recv()
            send[way, s, :, own] = (
                value[:, own] if s == 0 else value[:, own] + recv[way, s - 1, :, own].astype(jnp.float32)
            ).astype(jnp.bfloat16)
            if s == 1:
                send[way, s, :, rest] = value[:, rest].astype(jnp.bfloat16)
            elif s > 1:
                send[way, s, :, rest] = (
                    value[:, rest] + recv[way, s - 1, :, rest].astype(jnp.float32)
                ).astype(jnp.bfloat16)
            spot = own if s == 0 else slice(None)
            copy = remote(
                send.at[way, s, :, spot], recv.at[way, s, :, spot], ssem.at[way, s], rsem.at[way, s], to
            )
            copy.start()
            sent.append(copy)
        yield
    total = term(0)
    for way, to in ((0, plus), (1, minus)):
        landing = recv.at[way, steps - 1]
        remote(landing, landing, ssem.at[way, steps - 1], rsem.at[way, steps - 1], to).wait_recv()
        total = total + recv[way, steps - 1].astype(jnp.float32)
    done(total)
    for copy in sent:
        copy.wait_send()
    yield


def line_sum(term, ways, send, recv, ssem, rsem, done):
    half = send.shape[-1] // 2
    whole = slice(None)
    sent = []

    def copy(way, s, spot, to):
        return remote(send.at[way, s, :, spot], recv.at[way, s, :, spot], ssem.at[way, s], rsem.at[way, s], to)

    def go(way, s, spot, to):
        sent.append(copy(way, s, spot, to))
        sent[-1].start()

    def got(way, s, spot):
        copy(way, s, spot, ways[way][0]).wait_recv()
        return recv[way, s, :, spot].astype(jnp.float32)

    for way, (one, two) in enumerate(ways):
        own = slice(way * half, (way + 1) * half)
        send[way, 0, :, own] = term(4)[:, own].astype(jnp.bfloat16)
        go(way, 0, own, two)
        send[way, 1] = term(3 if way == 0 else 5).astype(jnp.bfloat16)
        go(way, 1, whole, one)
    yield
    for way, (one, two) in enumerate(ways):
        own = slice(way * half, (way + 1) * half)
        rest = slice((1 - way) * half, (2 - way) * half)
        value = term(2 if way == 0 else 6) + got(way, 1, whole)
        send[way, 2, :, rest] = value[:, rest].astype(jnp.bfloat16)
        send[way, 2, :, own] = (value[:, own] + got(way, 0, own)).astype(jnp.bfloat16)
        go(way, 2, whole, one)
    yield
    for way, (one, two) in enumerate(ways):
        send[way, 3] = (term(1 if way == 0 else 7) + got(way, 2, whole)).astype(jnp.bfloat16)
        go(way, 3, whole, one)
    yield
    done(term(0) + got(0, 3, whole) + got(1, 3, whole))
    for one in sent:
        one.wait_send()
    yield


def together(*rings):
    live = list(rings)
    while live:
        for one in list(live):
            if next(one, 1) == 1:
                live.remove(one)


def finish_kernel(
    hid_ref, grad_ref, emb_hbm, sib_hbm, wo_hbm, att_hbm, qk_ref, value_ref,
    emb, sib, wo, hidden, att, hid_recv, g_recv, terms, z_send, z_recv, x_send, x_recv, line, last_send, last_recv,
    lsem, h_ssem, h_rsem, g_ssem, g_rsem, zs_sem, zr_sem, xs_sem, xr_sem, ls_sem, lr_sem,
):
    z, x, c, y = place()
    col = column_of(x, c)
    kept = c == x // 2
    mine = 2 * y + x // 2
    loads = [pltpu.make_async_copy(emb_hbm, emb, lsem.at[0]), pltpu.make_async_copy(sib_hbm, sib, lsem.at[1])]
    fetch = pltpu.make_async_copy(wo_hbm, wo, lsem.at[2])
    store = pltpu.make_async_copy(att, att_hbm, lsem.at[3])
    for load in loads:
        load.start()
    fetch.start()
    sibling = device(z, x, 1 - c, y)
    up, down = device((z + 1) % NZ, x, c, y), device((z + NZ - 1) % NZ, x, c, y)
    east, west = device(z, (x + 1) % NX, c, y), device(z, (x + NX - 1) % NX, c, y)
    near = [device(z, x, cd, (y + d) % NY) for d in (1, 2, 3) for cd in (0, 1)] + [sibling]
    near += [device(z, NX - 1 - x, cd, (y + d) % NY) for d in range(NY) for cd in (0, 1)]
    near += [device(z, (x + d) % NX, c, y) for d in range(1, NX)]
    near += [device((z + d) % NZ, x, c, y) for d in range(1, NZ)]
    greet(near)

    ways = [(d, cd) for d in (2, 1, 3, 0) for cd in (0, 1)]

    def outgoing(d, cd, kind):
        yd = (y + d) % NY
        slot = yd * 2 + cd
        to = device(z, col, cd, yd)
        if kind == 0:
            return remote(grad_ref.at[cd], g_recv.at[mine], g_ssem.at[slot], g_rsem.at[mine], to)
        return remote(hid_ref.at[cd], hid_recv.at[mine], h_ssem.at[slot], h_rsem.at[mine], to)

    def away(d, cd):
        return jnp.logical_not(kept & (cd == c)) if d == 0 else None

    def launch(kind):
        for d, cd in ways:
            if d:
                outgoing(d, cd, kind).start()
            else:

                @pl.when(away(d, cd))
                def _():
                    outgoing(d, cd, kind).start()

    launch(0)

    @pl.when(kept)
    def _():
        g_recv[mine] = grad_ref[c]
        hid_recv[mine] = hid_ref[c]

    def arrive(ref, ss, rs):
        def one(slot, carry):
            @pl.when(jnp.logical_not(kept & (slot == mine)))
            def _():
                remote(ref.at[slot], ref.at[slot], ss.at[slot], rs.at[slot], sibling).wait_recv()

            return carry

        lax.fori_loop(0, HEADS, one, 0)

    for load in loads:
        load.wait()
    arrive(g_recv, g_ssem, g_rsem)
    launch(1)
    width = emb.shape[-1]
    all_g = g_recv[...].reshape(HEADS * HDIM, LOCALS * CROP)
    own = jnp.where(c == 0, all_g[:, : 2 * CROP], all_g[:, 2 * CROP :])
    theirs = jnp.where(c == 0, all_g[:, 2 * CROP :], all_g[:, : 2 * CROP])
    terms[...] = (
        jnp.dot(own, emb[...], preferred_element_type=jnp.float32)
        + jnp.dot(theirs, sib[...], preferred_element_type=jnp.float32)
    ).reshape(terms.shape)

    def heads():
        arrive(hid_recv, h_ssem, h_rsem)
        low = lax.broadcasted_iota(jnp.int32, (CROP, 2 * HDIM), 1) < HDIM
        for yy in range(NY):
            even = hid_recv[2 * yy].astype(jnp.float32)
            odd = hid_recv[2 * yy + 1].astype(jnp.float32)
            at = slice(yy * 2 * HDIM, (yy + 1) * 2 * HDIM)
            hidden[:CROP, at] = jnp.where(low, even, pltpu.roll(odd, HDIM, 1)).astype(jnp.bfloat16)
            hidden[CROP:, at] = jnp.where(low, pltpu.roll(even, HDIM, 1), odd).astype(jnp.bfloat16)
        fetch.wait()
        att[...] = jnp.dot(hidden[...], wo[...], preferred_element_type=jnp.float32).astype(jnp.bfloat16)
        store.start()

    def finish(n, term, to):
        sends = []
        for d in sorted(range(1, n), key=lambda d: -min(d, n - d)):
            last_send[d] = term(d).astype(jnp.bfloat16)
            copy = remote(last_send.at[d], last_recv.at[d], ls_sem.at[d], lr_sem.at[d], to(d))
            copy.start()
            sends.append(copy)
        heads()
        total = term(0)
        for copy in sends:
            copy.wait_recv()
        for d in range(1, n):
            total = total + last_recv[d].astype(jnp.float32)
        qk_ref[...] = total[:8]
        value_ref[...] = total[8:]
        for copy in sends:
            copy.wait_send()

    @pl.when(c == 0)
    def _():
        def ring(i):
            def done(total):
                line[i] = total

            return line_sum(
                lambda d: terms[(z + d) % NZ, i],
                ((up, device((z + 2) % NZ, x, c, y)), (down, device((z + NZ - 2) % NZ, x, c, y))), z_send.at[i], z_recv.at[i], zs_sem.at[i], zr_sem.at[i], done,
            )

        together(*[ring(i) for i in range(NX)])
        finish(NX, lambda d: line[(x + d) % NX], lambda d: device(z, (x + d) % NX, c, y))

    @pl.when(c == 1)
    def _():
        def ring(i):
            def done(total):
                line[4 * i : 4 * i + 4] = total.reshape(4, 16, width)

            return ring_sum(
                NX,
                lambda d: terms[4 * i : 4 * i + 4, (x + d) % NX].reshape(64, width),
                east, west, x_send.at[i], x_recv.at[i], xs_sem.at[i], xr_sem.at[i], done,
            )

        together(ring(0), ring(1))
        finish(NZ, lambda d: line[(z + d) % NZ], lambda d: device((z + d) % NZ, x, c, y))

    store.wait()
    for d, cd in ways:
        for kind in (0, 1):
            if d:
                outgoing(d, cd, kind).wait_send()
            else:

                @pl.when(away(d, cd))
                def _():
                    outgoing(d, cd, kind).wait_send()


def finish_call(hid, grads, emb, sib, w_out):
    rows, width = emb.shape
    vmem = pl.BlockSpec(memory_space=pltpu.VMEM)
    hbm = pl.BlockSpec(memory_space=pl.ANY)
    dma = pltpu.SemaphoreType.DMA
    bf = jnp.bfloat16
    return pl.pallas_call(
        finish_kernel,
        out_shape=(
            jax.ShapeDtypeStruct((rows, width), bf),
            jax.ShapeDtypeStruct((8, width), jnp.float32),
            jax.ShapeDtypeStruct((8, width), jnp.float32),
        ),
        in_specs=[vmem, vmem, hbm, hbm, hbm],
        out_specs=(hbm, vmem, vmem),
        scratch_shapes=[
            pltpu.VMEM((rows, width), bf),
            pltpu.VMEM((rows, width), bf),
            pltpu.VMEM(w_out.shape, bf),
            pltpu.VMEM((rows, w_out.shape[0]), bf),
            pltpu.VMEM((rows, width), bf),
            pltpu.VMEM((HEADS, CROP, 2 * HDIM), bf),
            pltpu.VMEM((HEADS, HDIM, LOCALS * CROP), bf),
            pltpu.VMEM((NZ, NX, 16, width), jnp.float32),
            pltpu.VMEM((NX, 2, NZ // 2, 16, width), bf),
            pltpu.VMEM((NX, 2, NZ // 2, 16, width), bf),
            pltpu.VMEM((2, 2, NX // 2, 64, width), bf),
            pltpu.VMEM((2, 2, NX // 2, 64, width), bf),
            pltpu.VMEM((NZ, 16, width), jnp.float32),
            pltpu.VMEM((NZ, 16, width), bf),
            pltpu.VMEM((NZ, 16, width), bf),
            dma((4,)),
            dma((HEADS,)),
            dma((HEADS,)),
            dma((HEADS,)),
            dma((HEADS,)),
            dma((NX, 2, NZ // 2)),
            dma((NX, 2, NZ // 2)),
            dma((2, 2, NX // 2)),
            dma((2, 2, NX // 2)),
            dma((NZ,)),
            dma((NZ,)),
        ],
        compiler_params=pltpu.CompilerParams(
            collective_id=1, has_side_effects=True, vmem_limit_bytes=VMEM_LIMIT
        ),
    )(hid, grads, emb, sib, w_out)


def output_kernel(att_ref, qk_ref, value_ref, out_att_ref, out_qk_ref, out_value_ref, att, qk, value, sem):
    rows = att.shape[0] // PIECES
    moves = [(qk_ref, qk, out_qk_ref), (value_ref, value, out_value_ref)]
    for i in range(PIECES):
        part = pl.ds(i * rows, rows)
        moves.append((att_ref.at[part], att.at[part], out_att_ref.at[part]))
    come = [pltpu.make_async_copy(src, mid, sem.at[0, i]) for i, (src, mid, dst) in enumerate(moves)]
    go = [pltpu.make_async_copy(mid, dst, sem.at[1, i]) for i, (src, mid, dst) in enumerate(moves)]
    for copy in come:
        copy.start()
    for first, then in zip(come, go):
        first.wait()
        then.start()
    for copy in go:
        copy.wait()


def output_call(*results):
    hbm = pl.BlockSpec(memory_space=pl.ANY)
    return pl.pallas_call(
        output_kernel,
        out_shape=tuple(jax.ShapeDtypeStruct(v.shape, v.dtype) for v in results),
        in_specs=[hbm] * 3,
        out_specs=(hbm,) * 3,
        scratch_shapes=[pltpu.VMEM(v.shape, v.dtype) for v in results]
        + [pltpu.SemaphoreType.DMA((2, PIECES + 2))],
        compiler_params=pltpu.CompilerParams(vmem_limit_bytes=VMEM_LIMIT),
    )(*results)


def on_device(embeddings, cotangent, w_qk, w_value, w_out, lengths, pair_list):
    owned, crop, width = embeddings.shape
    rows = owned * crop
    emb = embeddings.reshape(rows, width)
    z, x, c, _ = place()
    first = LOCALS * (z * NX + column_of(x, c))
    table, sib, lists = gather_call(
        lengths, pair_list.T, emb, cotangent.reshape(rows, width), w_qk, w_value, w_out
    )
    hid, grads = pair_call(lists, lengths, first.reshape(1), table)
    attended, grad_qk, grad_value = output_call(*finish_call(hid, grads, emb, sib, w_out))
    return (attended.reshape(embeddings.shape), grad_qk.T, grad_value.T)


def solution(mesh):
    in_specs = (
        P("pairs", None, "mp"),
        P("pairs", None, "mp"),
        P("mp", None),
        P("mp", None),
        P(None, "mp"),
        P(),
        P(),
    )
    out_specs = (P("pairs", None, "mp"), P("mp", "pairs"), P("mp", "pairs"))
    return jax.shard_map(on_device, mesh=mesh, in_specs=in_specs, out_specs=out_specs, check_vma=False)
```

```python
import math

import jax
import jax.numpy as jnp
from jax import lax
from jax.experimental import pallas as pl
from jax.experimental.pallas import tpu as pltpu
from jax.sharding import PartitionSpec as P

HDIM = 64
CROP = 128
SCALE = HDIM**-0.5 * math.log2(math.e)
NT = (((1,), (1,)), ((), ()))
NZ, NX, NY = 8, 4, 4
CHIPS = NZ * NX
LOCALS = 4
HEADS = 2 * NY
GROUPS = 20
PIECES = 2
MESH = pl.DeviceIdType.MESH
VMEM_LIMIT = 56 * 1024 * 1024
SCHEDULE = (0, 1, None, 2, 3)


def place():
    me = lax.axis_index("pairs")
    chip = me // 2
    return chip // NX, chip % NX, me % 2, lax.axis_index("mp")


def device(z, x, c, y):
    return ((z * NX + x) * 2 + c, y)


def column_of(x, c):
    return jnp.where(c == x // 2, x, NX - 1 - x)


def mate_of(x):
    return x + 1 - 2 * (x % 2)


def remote(src, dst, send, recv, to):
    return pltpu.make_async_remote_copy(
        src_ref=src, dst_ref=dst, send_sem=send, recv_sem=recv, device_id=to, device_id_type=MESH
    )


def greet(others):
    barrier = pltpu.get_barrier_semaphore()
    for other in others:
        pl.semaphore_signal(barrier, inc=1, device_id=other, device_id_type=MESH)
    pl.semaphore_wait(barrier, len(others))


def gather_kernel(
    len_ref, pairs_ref, emb_hbm, cot_hbm, wq_hbm, wv_hbm, wo_hbm, table_ref, sib_ref, codes_ref,
    emb, cot, wq, wv, wo, k_send, k_recv, vg_send, vg_recv, seed,
    lsem, k_ssem, k_rsem, vg_ssem, vg_rsem, bsem, ssem, rsem,
):
    z, x, c, y = place()
    mine = y * 2 + c
    sibling = device(z, x, 1 - c, y)
    above, below = (z + 1) % NZ, (z + NZ - 1) % NZ
    mate = device(z, mate_of(x), c, y)
    up, down = device(above, x, c, y), device(below, x, c, y)
    mate_up, mate_down = device(above, mate_of(x), c, y), device(below, mate_of(x), c, y)
    col, mate_col = column_of(x, c), column_of(mate_of(x), c)
    sib_col, sib_mate_col = column_of(x, 1 - c), column_of(mate_of(x), 1 - c)
    kept = c == x // 2

    loads = [
        pltpu.make_async_copy(src, dst, lsem.at[i])
        for i, (src, dst) in enumerate(
            ((emb_hbm, emb), (wq_hbm, wq), (wv_hbm, wv), (cot_hbm, cot), (wo_hbm, wo))
        )
    ]
    for load in loads:
        load.start()
    greet(
        [device(z, x, cd, (y + d) % NY) for d in (1, 2, 3) for cd in (0, 1)]
        + [device(z, NX - 1 - x, cd, (y + d) % NY) for d in range(NY) for cd in (0, 1)]
        + [sibling, mate, up, down, mate_up, mate_down]
    )
    for load in loads:
        load.wait()

    def copies(j, slot, to):
        return (
            remote(k_send.at[j, slot], k_recv.at[j, mine], k_ssem.at[j, slot], k_rsem.at[j, mine], to),
            remote(vg_send.at[j, slot], vg_recv.at[j, mine], vg_ssem.at[j, slot], vg_rsem.at[j, mine], to),
        )

    def project(j):
        rows = slice(j * CROP, (j + 1) * CROP)

        def away(step, carry):
            d = jnp.where(step == 0, 2, jnp.where(step == 1, 1, jnp.where(step == 2, 3, 0)))
            yd = (y + d) % NY
            at = pl.ds(pl.multiple_of(yd * 2 * HDIM, 2 * HDIM), 2 * HDIM)
            k = jnp.dot(emb[rows], wq[:, at], preferred_element_type=jnp.float32).T
            v = jnp.dot(emb[rows], wv[:, at], preferred_element_type=jnp.float32).T.astype(jnp.bfloat16)
            g = lax.dot_general(cot[rows], wo[at, :], NT, preferred_element_type=jnp.float32).T.astype(jnp.bfloat16)
            for h in (0, 1):
                slot = yd * 2 + h
                part = slice(h * HDIM, (h + 1) * HDIM)
                here = kept & (slot == mine)

                @pl.when(here)
                def _():
                    k_recv[j, mine] = k[part]
                    vg_recv[j, mine, :HDIM] = v[part]
                    vg_recv[j, mine, HDIM:] = g[part]

                @pl.when(jnp.logical_not(here))
                def _():
                    k_send[j, slot] = k[part]
                    vg_send[j, slot, :HDIM] = v[part]
                    vg_send[j, slot, HDIM:] = g[part]
                    to = device(z, jnp.where(x // 2 == h, x, NX - 1 - x), x // 2, yd)
                    for copy in copies(j, slot, to):
                        copy.start()

            return carry

        lax.fori_loop(0, NY, away, 0)

    def settle(j):
        def arrive(slot, carry):
            @pl.when(jnp.logical_not(kept & (slot == mine)))
            def _():
                for ref, ss, rs in ((k_recv, k_ssem, k_rsem), (vg_recv, vg_ssem, vg_rsem)):
                    remote(ref.at[j, slot], ref.at[j, slot], ss.at[j, slot], rs.at[j, slot], sibling).wait_recv()

            return carry

        lax.fori_loop(0, HEADS, arrive, 0)
        lanes = lax.broadcasted_iota(jnp.int32, (HDIM, CROP), 1)
        for cs in (0, 1):
            k = (k_recv[j, cs] + k_recv[j, 2 + cs]) + (k_recv[j, 4 + cs] + k_recv[j, 6 + cs])
            vg = [vg_recv[j, 2 * yy + cs].astype(jnp.float32) for yy in range(NY)]
            vg = (vg[0] + vg[1]) + (vg[2] + vg[3])
            ok = lanes < len_ref[(z * NX + col) * LOCALS + 2 * cs + j]
            seed[j, cs, :HDIM] = k.astype(jnp.bfloat16)
            seed[j, cs, HDIM : 2 * HDIM] = vg[:HDIM].astype(jnp.bfloat16)
            seed[j, cs, 2 * HDIM :] = jnp.where(ok, vg[HDIM:], 0.0).astype(jnp.bfloat16)
        keep(j).start()

    def keep(j):
        at = pl.ds(j * 2 * CHIPS + (z * NX + col) * 2, 2)
        return pltpu.make_async_copy(seed.at[j], table_ref.at[at], bsem.at[j])

    def spread(j, cs, sent, first):
        lane = 2 * j + cs

        def part(bz, bx, half):
            at = j * 2 * CHIPS + (bz * NX + bx) * 2 + cs
            if half is None:
                return table_ref.at[at]
            return table_ref.at[at, pl.ds(half * 3 * HDIM // 2, 3 * HDIM // 2)]

        def signal(bz, bx, half):
            return rsem.at[lane, CHIPS + jnp.where(bx == col, 0, 1) if half == 1 else bz * NX + bx]

        def landed(bz, bx, half=None):
            ref = part(bz, bx, half)
            remote(ref, ref, ssem.at[0], signal(bz, bx, half), sibling).wait_recv()

        def push(bz, bx, to, half=None, src=None, far=None):
            dst = part(bz, bx, half)
            sem = signal(bz, bx, half) if far is None else rsem.at[lane, far]
            copy = remote(dst if src is None else src, dst, ssem.at[len(sent)], sem, to)
            copy.start()
            sent.append(copy)

        def hop(s, bx, extra):
            for bz, to, half in (((z + NZ - s) % NZ, up, 0), ((z + s) % NZ, down, 1)):
                landed(bz, bx)
                push(bz, bx, to, half if s == NZ // 2 - 1 else None)
                for other in extra:
                    push(bz, bx, other)

        def meet(bx, extra):
            bz = (z + NZ // 2) % NZ
            landed(bz, bx, 0)
            landed(bz, bx, 1)
            for other in extra:
                push(bz, bx, other)

        def relay(bz):
            landed(bz, mate_col)
            push(bz, mate_col, sibling)

        own = seed.at[j, cs]
        if first == "z":
            for to in (up, down, mate, sibling):
                push(z, col, to, src=own)
            ready = [z]
            yield
            for s in range(1, NZ // 2):
                hop(s, col, (mate, sibling))
                yield
                for bz in ready:
                    relay(bz)
                ready = [(z + NZ - s) % NZ, (z + s) % NZ]
                yield
            meet(col, (mate, sibling))
            for bz in ready:
                relay(bz)
            yield
            relay((z + NZ // 2) % NZ)
            yield
        else:
            for to in (up, down, mate_up, mate_down, mate, sibling):
                push(z, col, to, src=own)
            yield
            for s in range(1, NZ // 2):
                for bx in (col, mate_col):
                    hop(s, bx, (sibling,))
                if s == 1:
                    relay(z)
                yield
            for bx in (col, mate_col):
                meet(bx, (sibling,))
            yield
        for bz in range(NZ):
            landed(bz, sib_col)
            landed(bz, sib_mate_col)
        yield

    def whole(first):
        sent = []
        flows = [spread(j, cs, sent, first) for j in (0, 1) for cs in (0, 1)]
        for what in SCHEDULE:
            if what is None:
                settle(1)
            else:
                next(flows[what])
        live = list(flows)
        while live:
            for one in list(live):
                if next(one, 1) == 1:
                    live.remove(one)
        for copy in sent:
            copy.wait_send()

    project(0)
    project(1)
    share = remote(emb, sib_ref, lsem.at[5], lsem.at[6], sibling)
    share.start()
    first = (z * NX + col) * LOCALS
    a, b = pairs_ref[0:1], pairs_ref[1:2]
    owners = lax.broadcasted_iota(jnp.int32, (8, 1), 0) + first // 2
    codes = jnp.where(a // 2 == owners, 1 + (a - first) * CROP + b, 0) + jnp.where(
        b // 2 == owners, 1 + (b - first) * CROP + a, 0
    )
    count = pairs_ref.shape[1]
    each = count // (2 * CHIPS)
    segment = (
        lax.broadcasted_iota(jnp.int32, (count, CROP), 0) // each
        == lax.broadcasted_iota(jnp.int32, (count, CROP), 1)
    ).astype(jnp.float32)
    codes = jnp.dot(
        codes.astype(jnp.float32), segment, precision=lax.Precision.HIGHEST, preferred_element_type=jnp.float32
    )
    index = lax.broadcasted_iota(jnp.int32, (8, CROP), 0)
    named = jnp.where(index < 2, codes[0:1], codes[1:2])
    base = (index * CROP).astype(jnp.float32)
    member = (named > base) & (named <= base + CROP) & (index < LOCALS)
    member = member.astype(jnp.float32)
    before = lax.broadcasted_iota(jnp.int32, (CROP, CROP), 0) < lax.broadcasted_iota(jnp.int32, (CROP, CROP), 1)
    rank = jnp.dot(member, before.astype(jnp.float32), preferred_element_type=jnp.float32)
    many = jnp.broadcast_to(jnp.sum(member, axis=1, keepdims=True), (8, CROP))
    groups = jnp.floor((many + 7.0) * 0.125)
    start, starts = jnp.zeros((1, CROP), jnp.float32), []
    for l in range(LOCALS):
        starts.append(start)
        start = start + 8.0 * groups[l : l + 1]
    starts = jnp.concatenate(starts + [start] * 4, axis=0)
    spot = jnp.where(member > 0, rank + starts, -1.0).T
    partner = (named - base - 1.0).astype(jnp.bfloat16)
    across = lax.broadcasted_iota(jnp.int32, (CROP, 2 * CROP), 1).astype(jnp.float32)
    flat = jnp.zeros((1, 2 * CROP), jnp.float32)
    for l in range(LOCALS):
        hot = (spot[:, l : l + 1] == across).astype(jnp.bfloat16)
        flat = flat + jnp.dot(partner[l : l + 1], hot, preferred_element_type=jnp.float32)
    zero = jnp.zeros((2, CROP), jnp.float32)
    codes_ref[...] = jnp.concatenate(
        [flat[:, :CROP], flat[:, CROP:], zero, many[:LOCALS]], axis=0
    ).astype(jnp.int32)
    settle(0)

    @pl.when(c == 0)
    def _():
        whole("z")

    @pl.when(c == 1)
    def _():
        whole("x")

    for j in (0, 1):

        def leave(slot, carry):
            @pl.when(jnp.logical_not(kept & (slot == mine)))
            def _():
                for copy in copies(j, slot, sibling):
                    copy.wait_send()

            return carry

        lax.fori_loop(0, HEADS, leave, 0)
        keep(j).wait()
    share.wait()


def gather_call(lengths, pairs, emb, cot, w_qk, w_value, w_out):
    rows, width = emb.shape
    smem = pl.BlockSpec(memory_space=pltpu.SMEM)
    vmem = pl.BlockSpec(memory_space=pltpu.VMEM)
    hbm = pl.BlockSpec(memory_space=pl.ANY)
    dma = pltpu.SemaphoreType.DMA
    bf = jnp.bfloat16
    return pl.pallas_call(
        gather_kernel,
        out_shape=(
            jax.ShapeDtypeStruct((CHIPS * LOCALS, 3 * HDIM, CROP), bf),
            jax.ShapeDtypeStruct((rows, width), bf),
            jax.ShapeDtypeStruct((8, CROP), jnp.int32),
        ),
        in_specs=[smem, vmem] + [hbm] * 5,
        out_specs=(hbm, hbm, vmem),
        scratch_shapes=[pltpu.VMEM(v.shape, bf) for v in (emb, cot, w_qk, w_value, w_out)]
        + [
            pltpu.VMEM((2, HEADS, HDIM, CROP), jnp.float32),
            pltpu.VMEM((2, HEADS, HDIM, CROP), jnp.float32),
            pltpu.VMEM((2, HEADS, 2 * HDIM, CROP), bf),
            pltpu.VMEM((2, HEADS, 2 * HDIM, CROP), bf),
            pltpu.VMEM((2, 2, 3 * HDIM, CROP), bf),
            dma((7,)),
            dma((2, HEADS)),
            dma((2, HEADS)),
            dma((2, HEADS)),
            dma((2, HEADS)),
            dma((2,)),
            dma((144,)),
            dma((LOCALS, CHIPS + 2)),
        ],
        compiler_params=pltpu.CompilerParams(
            collective_id=0, has_side_effects=True, vmem_limit_bytes=VMEM_LIMIT
        ),
    )(lengths, pairs, emb, cot, w_qk, w_value, w_out)


def pair_kernel(
    lists_ref, len_ref, first_ref, table_hbm, hid_ref, grad_ref, blocks_ref, own_ref, out_acc, dk_acc, dv_acc, sem, own_sem
):
    counts = [lists_ref[LOCALS + l, 0] for l in range(LOCALS)]
    total = sum((count + 7) // 8 for count in counts)

    def spot(p):
        return (p % 2) * 2 * CHIPS + p // 2

    def partner(group, j):
        return lists_ref[group // 16, (group % 16) * 8 + j]

    def fetch(group, carry):
        for j in range(8):
            pltpu.make_async_copy(
                table_hbm.at[spot(partner(group, j))], blocks_ref.at[group * 8 + j], sem.at[group]
            ).start()
        return carry

    def mine(l):
        return pltpu.make_async_copy(table_hbm.at[spot(first_ref[0] + l)], own_ref.at[l], own_sem.at[l])

    mine(0).start()
    lax.fori_loop(0, total, fetch, 0)
    for l in range(1, LOCALS):
        mine(l).start()
    rows = lax.broadcasted_iota(jnp.int32, (CROP, CROP), 0)
    columns = lax.broadcasted_iota(jnp.int32, (1, CROP), 1)
    done = 0
    for l in range(LOCALS):
        me = first_ref[0] + l
        row_bias = jnp.where(rows < len_ref[me], 0.0, -1e30)
        count = counts[l]
        mine(l).wait()
        own = own_ref[l].astype(jnp.float32)
        kp = own[:HDIM].T.astype(jnp.bfloat16)
        vp = own[HDIM : 2 * HDIM].T.astype(jnp.bfloat16)
        gp = own[2 * HDIM :].T.astype(jnp.bfloat16)
        out_acc[...] = jnp.zeros_like(out_acc)
        dk_acc[...] = jnp.zeros_like(dk_acc)
        dv_acc[...] = jnp.zeros_like(dv_acc)

        def step(base, group, at):
            pltpu.make_async_copy(
                table_hbm.at[pl.ds(0, 8)], blocks_ref.at[pl.ds(at * 8, 8)], sem.at[at]
            ).wait()
            blocks, lens, live = [], [], []
            for j in range(group):
                blocks.append(blocks_ref[at * 8 + j])
                lens.append(len_ref[partner(at, j)])
                live.append(jnp.where(base + j < count, 1.0, 0.0))
            many = jnp.concatenate(blocks, axis=1)
            kq, vq, gq = many[:HDIM], many[HDIM : 2 * HDIM], many[2 * HDIM :]
            scores = jnp.dot(kp, kq, preferred_element_type=jnp.float32)
            d_rows = jnp.dot(gp, vq, preferred_element_type=jnp.float32)
            d_cols = jnp.dot(vp, gq, preferred_element_type=jnp.float32)
            a_parts, b_parts, ds_parts = [], [], []
            for j in range(group):
                part = slice(j * CROP, (j + 1) * CROP)
                s = scores[:, part] * SCALE
                sa = s + jnp.where(columns < lens[j], 0.0, -1e30)
                ea = jnp.exp2(sa - jnp.max(sa, axis=1, keepdims=True))
                a = ea * (live[j] / jnp.sum(ea, axis=1, keepdims=True))
                sb = s + row_bias
                eb = jnp.exp2(sb - jnp.max(sb, axis=0, keepdims=True))
                b = eb * (live[j] / jnp.sum(eb, axis=0, keepdims=True))
                ta = a * d_rows[:, part]
                tb = b * d_cols[:, part]
                ds = (ta - a * jnp.sum(ta, axis=1, keepdims=True)) + (
                    tb - b * jnp.sum(tb, axis=0, keepdims=True)
                )
                a_parts.append(a.astype(jnp.bfloat16))
                b_parts.append(b.astype(jnp.bfloat16))
                ds_parts.append(ds.astype(jnp.bfloat16))
            for acc, parts, other in ((out_acc, a_parts, vq), (dv_acc, b_parts, gq), (dk_acc, ds_parts, kq)):
                acc[...] += lax.dot_general(
                    jnp.concatenate(parts, axis=1), other, NT, preferred_element_type=jnp.float32
                )

        def eight(i, carry):
            step(i * 8, 8, done + i)
            return carry

        def four(i, carry):
            step(big * 8, 4, done + big)
            return carry

        big = (count + 3) // 8
        lax.fori_loop(0, big, eight, 0)
        lax.fori_loop(0, jnp.where(count > big * 8, 1, 0), four, 0)
        done = done + (count + 7) // 8
        ok = rows[:, :HDIM] < len_ref[me]
        hid_ref[l // 2, :, (l % 2) * HDIM : (l % 2 + 1) * HDIM] = jnp.where(ok, out_acc[...], 0.0).astype(
            jnp.bfloat16
        )
        turned = jnp.concatenate([dk_acc[...] * HDIM**-0.5, dv_acc[...]], axis=1).T
        for core in range(2):
            eights = []
            for xd in range(NX):
                at = (xd * 2 + core) * 8
                eights += [turned[at : at + 8], turned[HDIM + at : HDIM + at + 8]]
            grad_ref[core, :, l * CROP : (l + 1) * CROP] = jnp.concatenate(eights, axis=0).astype(jnp.bfloat16)


def pair_call(lists, lengths, first, table):
    smem = pl.BlockSpec(memory_space=pltpu.SMEM)
    vmem = pl.BlockSpec(memory_space=pltpu.VMEM)
    hbm = pl.BlockSpec(memory_space=pl.ANY)
    return pl.pallas_call(
        pair_kernel,
        out_shape=(
            jax.ShapeDtypeStruct((2, CROP, 2 * HDIM), jnp.bfloat16),
            jax.ShapeDtypeStruct((2, HDIM, LOCALS * CROP), jnp.bfloat16),
        ),
        in_specs=[smem, smem, smem, hbm],
        out_specs=(vmem, vmem),
        scratch_shapes=[
            pltpu.VMEM((8 * GROUPS, 3 * HDIM, CROP), jnp.bfloat16),
            pltpu.VMEM((LOCALS, 3 * HDIM, CROP), jnp.bfloat16),
            pltpu.VMEM((CROP, HDIM), jnp.float32),
            pltpu.VMEM((CROP, HDIM), jnp.float32),
            pltpu.VMEM((CROP, HDIM), jnp.float32),
            pltpu.SemaphoreType.DMA((GROUPS,)),
            pltpu.SemaphoreType.DMA((LOCALS,)),
        ],
        compiler_params=pltpu.CompilerParams(vmem_limit_bytes=VMEM_LIMIT),
    )(lists, lengths, first, table)


def ring_sum(n, term, plus, minus, send, recv, ssem, rsem, done):
    steps = n // 2
    half = send.shape[-1] // 2
    sent = []
    for s in range(steps):
        d = steps - s
        for way, to in ((0, plus), (1, minus)):
            own = slice(way * half, (way + 1) * half)
            rest = slice((1 - way) * half, (2 - way) * half)
            value = term(d if way == 0 else n - d)
            if s > 0:
                landing = recv.at[way, s - 1, :, own] if s == 1 else recv.at[way, s - 1]
                remote(landing, landing, ssem.at[way, s - 1], rsem.at[way, s - 1], to).wait_recv()
            send[way, s, :, own] = (
                value[:, own] if s == 0 else value[:, own] + recv[way, s - 1, :, own].astype(jnp.float32)
            ).astype(jnp.bfloat16)
            if s == 1:
                send[way, s, :, rest] = value[:, rest].astype(jnp.bfloat16)
            elif s > 1:
                send[way, s, :, rest] = (
                    value[:, rest] + recv[way, s - 1, :, rest].astype(jnp.float32)
                ).astype(jnp.bfloat16)
            spot = own if s == 0 else slice(None)
            copy = remote(
                send.at[way, s, :, spot], recv.at[way, s, :, spot], ssem.at[way, s], rsem.at[way, s], to
            )
            copy.start()
            sent.append(copy)
        yield
    total = term(0)
    for way, to in ((0, plus), (1, minus)):
        landing = recv.at[way, steps - 1]
        remote(landing, landing, ssem.at[way, steps - 1], rsem.at[way, steps - 1], to).wait_recv()
        total = total + recv[way, steps - 1].astype(jnp.float32)
    done(total)
    for copy in sent:
        copy.wait_send()
    yield


def line_sum(term, ways, send, recv, ssem, rsem, done):
    half = send.shape[-1] // 2
    whole = slice(None)
    sent = []

    def copy(way, s, spot, to):
        return remote(send.at[way, s, :, spot], recv.at[way, s, :, spot], ssem.at[way, s], rsem.at[way, s], to)

    def go(way, s, spot, to):
        sent.append(copy(way, s, spot, to))
        sent[-1].start()

    def got(way, s, spot):
        copy(way, s, spot, ways[way][0]).wait_recv()
        return recv[way, s, :, spot].astype(jnp.float32)

    for way, (one, two) in enumerate(ways):
        own = slice(way * half, (way + 1) * half)
        send[way, 0, :, own] = term(4)[:, own].astype(jnp.bfloat16)
        go(way, 0, own, two)
        send[way, 1] = term(3 if way == 0 else 5).astype(jnp.bfloat16)
        go(way, 1, whole, one)
    yield
    for way, (one, two) in enumerate(ways):
        own = slice(way * half, (way + 1) * half)
        rest = slice((1 - way) * half, (2 - way) * half)
        value = term(2 if way == 0 else 6) + got(way, 1, whole)
        send[way, 2, :, rest] = value[:, rest].astype(jnp.bfloat16)
        send[way, 2, :, own] = (value[:, own] + got(way, 0, own)).astype(jnp.bfloat16)
        go(way, 2, whole, one)
    yield
    for way, (one, two) in enumerate(ways):
        send[way, 3] = (term(1 if way == 0 else 7) + got(way, 2, whole)).astype(jnp.bfloat16)
        go(way, 3, whole, one)
    yield
    done(term(0) + got(0, 3, whole) + got(1, 3, whole))
    for one in sent:
        one.wait_send()
    yield


def together(*rings):
    live = list(rings)
    while live:
        for one in list(live):
            if next(one, 1) == 1:
                live.remove(one)


def finish_kernel(
    hid_ref, grad_ref, emb_hbm, sib_hbm, wo_hbm, att_hbm, qk_ref, value_ref,
    emb, sib, wo, hidden, att, hid_recv, g_recv, terms, z_send, z_recv, x_send, x_recv, line, last_send, last_recv,
    lsem, h_ssem, h_rsem, g_ssem, g_rsem, zs_sem, zr_sem, xs_sem, xr_sem, ls_sem, lr_sem,
):
    z, x, c, y = place()
    col = column_of(x, c)
    kept = c == x // 2
    mine = 2 * y + x // 2
    loads = [pltpu.make_async_copy(emb_hbm, emb, lsem.at[0]), pltpu.make_async_copy(sib_hbm, sib, lsem.at[1])]
    fetch = pltpu.make_async_copy(wo_hbm, wo, lsem.at[2])
    store = pltpu.make_async_copy(att, att_hbm, lsem.at[3])
    for load in loads:
        load.start()
    fetch.start()
    sibling = device(z, x, 1 - c, y)
    up, down = device((z + 1) % NZ, x, c, y), device((z + NZ - 1) % NZ, x, c, y)
    east, west = device(z, (x + 1) % NX, c, y), device(z, (x + NX - 1) % NX, c, y)
    near = [device(z, x, cd, (y + d) % NY) for d in (1, 2, 3) for cd in (0, 1)] + [sibling]
    near += [device(z, NX - 1 - x, cd, (y + d) % NY) for d in range(NY) for cd in (0, 1)]
    near += [device(z, (x + d) % NX, c, y) for d in range(1, NX)]
    near += [device((z + d) % NZ, x, c, y) for d in range(1, NZ)]
    greet(near)

    ways = [(d, cd) for d in (2, 1, 3, 0) for cd in (0, 1)]

    def outgoing(d, cd, kind):
        yd = (y + d) % NY
        slot = yd * 2 + cd
        to = device(z, col, cd, yd)
        if kind == 0:
            return remote(grad_ref.at[cd], g_recv.at[mine], g_ssem.at[slot], g_rsem.at[mine], to)
        return remote(hid_ref.at[cd], hid_recv.at[mine], h_ssem.at[slot], h_rsem.at[mine], to)

    def away(d, cd):
        return jnp.logical_not(kept & (cd == c)) if d == 0 else None

    def launch(kind):
        for d, cd in ways:
            if d:
                outgoing(d, cd, kind).start()
            else:

                @pl.when(away(d, cd))
                def _():
                    outgoing(d, cd, kind).start()

    launch(0)

    @pl.when(kept)
    def _():
        g_recv[mine] = grad_ref[c]
        hid_recv[mine] = hid_ref[c]

    def arrive(ref, ss, rs):
        def one(slot, carry):
            @pl.when(jnp.logical_not(kept & (slot == mine)))
            def _():
                remote(ref.at[slot], ref.at[slot], ss.at[slot], rs.at[slot], sibling).wait_recv()

            return carry

        lax.fori_loop(0, HEADS, one, 0)

    for load in loads:
        load.wait()
    arrive(g_recv, g_ssem, g_rsem)
    launch(1)
    width = emb.shape[-1]
    all_g = g_recv[...].reshape(HEADS * HDIM, LOCALS * CROP)
    own = jnp.where(c == 0, all_g[:, : 2 * CROP], all_g[:, 2 * CROP :])
    theirs = jnp.where(c == 0, all_g[:, 2 * CROP :], all_g[:, : 2 * CROP])
    terms[...] = (
        jnp.dot(own, emb[...], preferred_element_type=jnp.float32)
        + jnp.dot(theirs, sib[...], preferred_element_type=jnp.float32)
    ).reshape(terms.shape)

    def heads():
        arrive(hid_recv, h_ssem, h_rsem)
        low = lax.broadcasted_iota(jnp.int32, (CROP, 2 * HDIM), 1) < HDIM
        for yy in range(NY):
            even = hid_recv[2 * yy].astype(jnp.float32)
            odd = hid_recv[2 * yy + 1].astype(jnp.float32)
            at = slice(yy * 2 * HDIM, (yy + 1) * 2 * HDIM)
            hidden[:CROP, at] = jnp.where(low, even, pltpu.roll(odd, HDIM, 1)).astype(jnp.bfloat16)
            hidden[CROP:, at] = jnp.where(low, pltpu.roll(even, HDIM, 1), odd).astype(jnp.bfloat16)
        fetch.wait()
        att[...] = jnp.dot(hidden[...], wo[...], preferred_element_type=jnp.float32).astype(jnp.bfloat16)
        store.start()

    def last(d, to):
        return remote(last_send.at[d], last_recv.at[d], ls_sem.at[d], lr_sem.at[d], to)

    def finish(n, term, to, sent=False):
        sends = []
        for d in sorted(range(1, n), key=lambda d: -min(d, n - d)):
            copy = last(d, to(d))
            if not sent:
                last_send[d] = term(d).astype(jnp.bfloat16)
                copy.start()
            sends.append(copy)
        heads()
        total = term(0)
        for copy in sends:
            copy.wait_recv()
        for d in range(1, n):
            total = total + last_recv[d].astype(jnp.float32)
        qk_ref[...] = total[:8]
        value_ref[...] = total[8:]
        for copy in sends:
            copy.wait_send()

    @pl.when(c == 0)
    def _():
        def ring(i):
            def done(total):
                line[i] = total
                d = (i + NX - x) % NX

                @pl.when(d != 0)
                def _():
                    last_send[d] = total.astype(jnp.bfloat16)
                    last(d, device(z, i, c, y)).start()

            return line_sum(
                lambda d: terms[(z + d) % NZ, i],
                ((up, device((z + 2) % NZ, x, c, y)), (down, device((z + NZ - 2) % NZ, x, c, y))), z_send.at[i], z_recv.at[i], zs_sem.at[i], zr_sem.at[i], done,
            )

        together(*[ring(i) for i in range(NX)])
        finish(NX, lambda d: line[(x + d) % NX], lambda d: device(z, (x + d) % NX, c, y), sent=True)

    @pl.when(c == 1)
    def _():
        def ring(i):
            def done(total):
                line[4 * i : 4 * i + 4] = total.reshape(4, 16, width)

            return ring_sum(
                NX,
                lambda d: terms[4 * i : 4 * i + 4, (x + d) % NX].reshape(64, width),
                east, west, x_send.at[i], x_recv.at[i], xs_sem.at[i], xr_sem.at[i], done,
            )

        together(ring(0), ring(1))
        finish(NZ, lambda d: line[(z + d) % NZ], lambda d: device((z + d) % NZ, x, c, y))

    store.wait()
    for d, cd in ways:
        for kind in (0, 1):
            if d:
                outgoing(d, cd, kind).wait_send()
            else:

                @pl.when(away(d, cd))
                def _():
                    outgoing(d, cd, kind).wait_send()


def finish_call(hid, grads, emb, sib, w_out):
    rows, width = emb.shape
    vmem = pl.BlockSpec(memory_space=pltpu.VMEM)
    hbm = pl.BlockSpec(memory_space=pl.ANY)
    dma = pltpu.SemaphoreType.DMA
    bf = jnp.bfloat16
    return pl.pallas_call(
        finish_kernel,
        out_shape=(
            jax.ShapeDtypeStruct((rows, width), bf),
            jax.ShapeDtypeStruct((8, width), jnp.float32),
            jax.ShapeDtypeStruct((8, width), jnp.float32),
        ),
        in_specs=[vmem, vmem, hbm, hbm, hbm],
        out_specs=(hbm, vmem, vmem),
        scratch_shapes=[
            pltpu.VMEM((rows, width), bf),
            pltpu.VMEM((rows, width), bf),
            pltpu.VMEM(w_out.shape, bf),
            pltpu.VMEM((rows, w_out.shape[0]), bf),
            pltpu.VMEM((rows, width), bf),
            pltpu.VMEM((HEADS, CROP, 2 * HDIM), bf),
            pltpu.VMEM((HEADS, HDIM, LOCALS * CROP), bf),
            pltpu.VMEM((NZ, NX, 16, width), jnp.float32),
            pltpu.VMEM((NX, 2, NZ // 2, 16, width), bf),
            pltpu.VMEM((NX, 2, NZ // 2, 16, width), bf),
            pltpu.VMEM((2, 2, NX // 2, 64, width), bf),
            pltpu.VMEM((2, 2, NX // 2, 64, width), bf),
            pltpu.VMEM((NZ, 16, width), jnp.float32),
            pltpu.VMEM((NZ, 16, width), bf),
            pltpu.VMEM((NZ, 16, width), bf),
            dma((4,)),
            dma((HEADS,)),
            dma((HEADS,)),
            dma((HEADS,)),
            dma((HEADS,)),
            dma((NX, 2, NZ // 2)),
            dma((NX, 2, NZ // 2)),
            dma((2, 2, NX // 2)),
            dma((2, 2, NX // 2)),
            dma((NZ,)),
            dma((NZ,)),
        ],
        compiler_params=pltpu.CompilerParams(
            collective_id=1, has_side_effects=True, vmem_limit_bytes=VMEM_LIMIT
        ),
    )(hid, grads, emb, sib, w_out)


def output_kernel(att_ref, qk_ref, value_ref, out_att_ref, out_qk_ref, out_value_ref, att, qk, value, sem):
    rows = att.shape[0] // PIECES
    moves = [(qk_ref, qk, out_qk_ref), (value_ref, value, out_value_ref)]
    for i in range(PIECES):
        part = pl.ds(i * rows, rows)
        moves.append((att_ref.at[part], att.at[part], out_att_ref.at[part]))
    come = [pltpu.make_async_copy(src, mid, sem.at[0, i]) for i, (src, mid, dst) in enumerate(moves)]
    go = [pltpu.make_async_copy(mid, dst, sem.at[1, i]) for i, (src, mid, dst) in enumerate(moves)]
    for copy in come:
        copy.start()
    for first, then in zip(come, go):
        first.wait()
        then.start()
    for copy in go:
        copy.wait()


def output_call(*results):
    hbm = pl.BlockSpec(memory_space=pl.ANY)
    return pl.pallas_call(
        output_kernel,
        out_shape=tuple(jax.ShapeDtypeStruct(v.shape, v.dtype) for v in results),
        in_specs=[hbm] * 3,
        out_specs=(hbm,) * 3,
        scratch_shapes=[pltpu.VMEM(v.shape, v.dtype) for v in results]
        + [pltpu.SemaphoreType.DMA((2, PIECES + 2))],
        compiler_params=pltpu.CompilerParams(vmem_limit_bytes=VMEM_LIMIT),
    )(*results)


def on_device(embeddings, cotangent, w_qk, w_value, w_out, lengths, pair_list):
    owned, crop, width = embeddings.shape
    rows = owned * crop
    emb = embeddings.reshape(rows, width)
    z, x, c, _ = place()
    first = LOCALS * (z * NX + column_of(x, c))
    table, sib, lists = gather_call(
        lengths, pair_list.T, emb, cotangent.reshape(rows, width), w_qk, w_value, w_out
    )
    hid, grads = pair_call(lists, lengths, first.reshape(1), table)
    attended, grad_qk, grad_value = output_call(*finish_call(hid, grads, emb, sib, w_out))
    return (attended.reshape(embeddings.shape), grad_qk.T, grad_value.T)


def solution(mesh):
    in_specs = (
        P("pairs", None, "mp"),
        P("pairs", None, "mp"),
        P("mp", None),
        P("mp", None),
        P(None, "mp"),
        P(),
        P(),
    )
    out_specs = (P("pairs", None, "mp"), P("mp", "pairs"), P("mp", "pairs"))
    return jax.shard_map(on_device, mesh=mesh, in_specs=in_specs, out_specs=out_specs, check_vma=False)
```

```python
import math

import jax
import jax.numpy as jnp
from jax import lax
from jax.experimental import pallas as pl
from jax.experimental.pallas import tpu as pltpu
from jax.sharding import PartitionSpec as P

HDIM = 64
CROP = 128
SCALE = HDIM**-0.5 * math.log2(math.e)
NT = (((1,), (1,)), ((), ()))
NZ, NX, NY = 8, 4, 4
CHIPS = NZ * NX
LOCALS = 4
HEADS = 2 * NY
GROUPS = 20
PIECES = 2
MESH = pl.DeviceIdType.MESH
VMEM_LIMIT = 56 * 1024 * 1024


def place():
    me = lax.axis_index("pairs")
    chip = me // 2
    return chip // NX, chip % NX, me % 2, lax.axis_index("mp")


def device(z, x, c, y):
    return ((z * NX + x) * 2 + c, y)


def column_of(x, c):
    return jnp.where(c == x // 2, x, NX - 1 - x)


def mate_of(x):
    return x + 1 - 2 * (x % 2)


def remote(src, dst, send, recv, to):
    return pltpu.make_async_remote_copy(
        src_ref=src, dst_ref=dst, send_sem=send, recv_sem=recv, device_id=to, device_id_type=MESH
    )


def greet(others):
    barrier = pltpu.get_barrier_semaphore()
    for other in others:
        pl.semaphore_signal(barrier, inc=1, device_id=other, device_id_type=MESH)
    pl.semaphore_wait(barrier, len(others))


def gather_kernel(
    len_ref, pairs_ref, emb_hbm, cot_hbm, wq_hbm, wv_hbm, wo_hbm, table_ref, sib_ref, codes_ref,
    emb, cot, wq, wv, wo, k_send, k_recv, vg_send, vg_recv, seed,
    lsem, k_ssem, k_rsem, vg_ssem, vg_rsem, bsem, ssem, rsem,
):
    z, x, c, y = place()
    mine = y * 2 + c
    sibling = device(z, x, 1 - c, y)
    above, below = (z + 1) % NZ, (z + NZ - 1) % NZ
    mate = device(z, mate_of(x), c, y)
    up, down = device(above, x, c, y), device(below, x, c, y)
    mate_up, mate_down = device(above, mate_of(x), c, y), device(below, mate_of(x), c, y)
    col, mate_col = column_of(x, c), column_of(mate_of(x), c)
    sib_col, sib_mate_col = column_of(x, 1 - c), column_of(mate_of(x), 1 - c)
    kept = c == x // 2

    loads = [
        pltpu.make_async_copy(src, dst, lsem.at[i])
        for i, (src, dst) in enumerate(
            ((emb_hbm, emb), (wq_hbm, wq), (wv_hbm, wv), (cot_hbm, cot), (wo_hbm, wo))
        )
    ]
    for load in loads:
        load.start()
    greet(
        [device(z, x, cd, (y + d) % NY) for d in (1, 2, 3) for cd in (0, 1)]
        + [device(z, NX - 1 - x, cd, (y + d) % NY) for d in range(NY) for cd in (0, 1)]
        + [sibling, mate, up, down, mate_up, mate_down]
    )
    for load in loads:
        load.wait()

    def copies(j, slot, to):
        return (
            remote(k_send.at[j, slot], k_recv.at[j, mine], k_ssem.at[j, slot], k_rsem.at[j, mine], to),
            remote(vg_send.at[j, slot], vg_recv.at[j, mine], vg_ssem.at[j, slot], vg_rsem.at[j, mine], to),
        )

    def project(j):
        rows = slice(j * CROP, (j + 1) * CROP)

        def away(step, carry):
            d = jnp.where(step == 0, 2, jnp.where(step == 1, 1, jnp.where(step == 2, 3, 0)))
            yd = (y + d) % NY
            at = pl.ds(pl.multiple_of(yd * 2 * HDIM, 2 * HDIM), 2 * HDIM)
            k = jnp.dot(emb[rows], wq[:, at], preferred_element_type=jnp.float32).T
            v = jnp.dot(emb[rows], wv[:, at], preferred_element_type=jnp.float32).T.astype(jnp.bfloat16)
            g = lax.dot_general(cot[rows], wo[at, :], NT, preferred_element_type=jnp.float32).T.astype(jnp.bfloat16)
            for h in (0, 1):
                slot = yd * 2 + h
                part = slice(h * HDIM, (h + 1) * HDIM)
                here = kept & (slot == mine)

                @pl.when(here)
                def _():
                    k_recv[j, mine] = k[part]
                    vg_recv[j, mine, :HDIM] = v[part]
                    vg_recv[j, mine, HDIM:] = g[part]

                @pl.when(jnp.logical_not(here))
                def _():
                    k_send[j, slot] = k[part]
                    vg_send[j, slot, :HDIM] = v[part]
                    vg_send[j, slot, HDIM:] = g[part]
                    to = device(z, jnp.where(x // 2 == h, x, NX - 1 - x), x // 2, yd)
                    for copy in copies(j, slot, to):
                        copy.start()

            return carry

        lax.fori_loop(0, NY, away, 0)

    def settle(j, cs):
        def arrive(yy, carry):
            slot = 2 * yy + cs

            @pl.when(jnp.logical_not(kept & (slot == mine)))
            def _():
                for ref, ss, rs in ((k_recv, k_ssem, k_rsem), (vg_recv, vg_ssem, vg_rsem)):
                    remote(ref.at[j, slot], ref.at[j, slot], ss.at[j, slot], rs.at[j, slot], sibling).wait_recv()

            return carry

        lax.fori_loop(0, NY, arrive, 0)
        lanes = lax.broadcasted_iota(jnp.int32, (HDIM, CROP), 1)
        k = (k_recv[j, cs] + k_recv[j, 2 + cs]) + (k_recv[j, 4 + cs] + k_recv[j, 6 + cs])
        vg = [vg_recv[j, 2 * yy + cs].astype(jnp.float32) for yy in range(NY)]
        vg = (vg[0] + vg[1]) + (vg[2] + vg[3])
        ok = lanes < len_ref[(z * NX + col) * LOCALS + 2 * cs + j]
        seed[j, cs, :HDIM] = k.astype(jnp.bfloat16)
        seed[j, cs, HDIM : 2 * HDIM] = vg[:HDIM].astype(jnp.bfloat16)
        seed[j, cs, 2 * HDIM :] = jnp.where(ok, vg[HDIM:], 0.0).astype(jnp.bfloat16)
        if cs == 1:
            keep(j).start()

    def keep(j):
        at = pl.ds(j * 2 * CHIPS + (z * NX + col) * 2, 2)
        return pltpu.make_async_copy(seed.at[j], table_ref.at[at], bsem.at[j])

    def spread(j, cs, sent, first):
        lane = 2 * j + cs

        def part(bz, bx, half):
            at = j * 2 * CHIPS + (bz * NX + bx) * 2 + cs
            if half is None:
                return table_ref.at[at]
            return table_ref.at[at, pl.ds(half * 3 * HDIM // 2, 3 * HDIM // 2)]

        def signal(bz, bx, half):
            return rsem.at[lane, CHIPS + jnp.where(bx == col, 0, 1) if half == 1 else bz * NX + bx]

        def landed(bz, bx, half=None):
            ref = part(bz, bx, half)
            remote(ref, ref, ssem.at[0], signal(bz, bx, half), sibling).wait_recv()

        def push(bz, bx, to, half=None, src=None, far=None):
            dst = part(bz, bx, half)
            sem = signal(bz, bx, half) if far is None else rsem.at[lane, far]
            copy = remote(dst if src is None else src, dst, ssem.at[len(sent)], sem, to)
            copy.start()
            sent.append(copy)

        def hop(s, bx, extra):
            for bz, to, half in (((z + NZ - s) % NZ, up, 0), ((z + s) % NZ, down, 1)):
                landed(bz, bx)
                push(bz, bx, to, half if s == NZ // 2 - 1 else None)
                for other in extra:
                    push(bz, bx, other)

        def meet(bx, extra):
            bz = (z + NZ // 2) % NZ
            landed(bz, bx, 0)
            landed(bz, bx, 1)
            for other in extra:
                push(bz, bx, other)

        def relay(bz):
            landed(bz, mate_col)
            push(bz, mate_col, sibling)

        own = seed.at[j, cs]
        if first == "z":
            for to in (up, down, mate, sibling):
                push(z, col, to, src=own)
            ready = [z]
            yield
            for s in range(1, NZ // 2):
                hop(s, col, (mate, sibling))
                yield
                for bz in ready:
                    relay(bz)
                ready = [(z + NZ - s) % NZ, (z + s) % NZ]
                yield
            meet(col, (mate, sibling))
            for bz in ready:
                relay(bz)
            yield
            relay((z + NZ // 2) % NZ)
            yield
        else:
            for to in (up, down, mate_up, mate_down, mate, sibling):
                push(z, col, to, src=own)
            yield
            for s in range(1, NZ // 2):
                for bx in (col, mate_col):
                    hop(s, bx, (sibling,))
                if s == 1:
                    relay(z)
                yield
            for bx in (col, mate_col):
                meet(bx, (sibling,))
            yield
        for bz in range(NZ):
            landed(bz, sib_col)
            landed(bz, sib_mate_col)
        yield

    def whole(first):
        sent = []
        flows = [spread(j, cs, sent, first) for j in (0, 1) for cs in (0, 1)]
        for j in (0, 1):
            for cs in (0, 1):
                if j or cs:
                    settle(j, cs)
                next(flows[2 * j + cs])
        live = list(flows)
        while live:
            for one in list(live):
                if next(one, 1) == 1:
                    live.remove(one)
        for copy in sent:
            copy.wait_send()

    project(0)
    project(1)
    share = remote(emb, sib_ref, lsem.at[5], lsem.at[6], sibling)
    share.start()
    first = (z * NX + col) * LOCALS
    a, b = pairs_ref[0:1], pairs_ref[1:2]
    owners = lax.broadcasted_iota(jnp.int32, (8, 1), 0) + first // 2
    codes = jnp.where(a // 2 == owners, 1 + (a - first) * CROP + b, 0) + jnp.where(
        b // 2 == owners, 1 + (b - first) * CROP + a, 0
    )
    count = pairs_ref.shape[1]
    each = count // (2 * CHIPS)
    segment = (
        lax.broadcasted_iota(jnp.int32, (count, CROP), 0) // each
        == lax.broadcasted_iota(jnp.int32, (count, CROP), 1)
    ).astype(jnp.float32)
    codes = jnp.dot(
        codes.astype(jnp.float32), segment, precision=lax.Precision.HIGHEST, preferred_element_type=jnp.float32
    )
    index = lax.broadcasted_iota(jnp.int32, (8, CROP), 0)
    named = jnp.where(index < 2, codes[0:1], codes[1:2])
    base = (index * CROP).astype(jnp.float32)
    member = (named > base) & (named <= base + CROP) & (index < LOCALS)
    member = member.astype(jnp.float32)
    before = lax.broadcasted_iota(jnp.int32, (CROP, CROP), 0) < lax.broadcasted_iota(jnp.int32, (CROP, CROP), 1)
    rank = jnp.dot(member, before.astype(jnp.float32), preferred_element_type=jnp.float32)
    many = jnp.broadcast_to(jnp.sum(member, axis=1, keepdims=True), (8, CROP))
    groups = jnp.floor((many + 7.0) * 0.125)
    start, starts = jnp.zeros((1, CROP), jnp.float32), []
    for l in range(LOCALS):
        starts.append(start)
        start = start + 8.0 * groups[l : l + 1]
    starts = jnp.concatenate(starts + [start] * 4, axis=0)
    spot = jnp.where(member > 0, rank + starts, -1.0).T
    partner = (named - base - 1.0).astype(jnp.bfloat16)
    across = lax.broadcasted_iota(jnp.int32, (CROP, 2 * CROP), 1).astype(jnp.float32)
    flat = jnp.zeros((1, 2 * CROP), jnp.float32)
    for l in range(LOCALS):
        hot = (spot[:, l : l + 1] == across).astype(jnp.bfloat16)
        flat = flat + jnp.dot(partner[l : l + 1], hot, preferred_element_type=jnp.float32)
    zero = jnp.zeros((2, CROP), jnp.float32)
    codes_ref[...] = jnp.concatenate(
        [flat[:, :CROP], flat[:, CROP:], zero, many[:LOCALS]], axis=0
    ).astype(jnp.int32)
    settle(0, 0)

    @pl.when(c == 0)
    def _():
        whole("z")

    @pl.when(c == 1)
    def _():
        whole("x")

    for j in (0, 1):

        def leave(slot, carry):
            @pl.when(jnp.logical_not(kept & (slot == mine)))
            def _():
                for copy in copies(j, slot, sibling):
                    copy.wait_send()

            return carry

        lax.fori_loop(0, HEADS, leave, 0)
        keep(j).wait()
    share.wait()


def gather_call(lengths, pairs, emb, cot, w_qk, w_value, w_out):
    rows, width = emb.shape
    smem = pl.BlockSpec(memory_space=pltpu.SMEM)
    vmem = pl.BlockSpec(memory_space=pltpu.VMEM)
    hbm = pl.BlockSpec(memory_space=pl.ANY)
    dma = pltpu.SemaphoreType.DMA
    bf = jnp.bfloat16
    return pl.pallas_call(
        gather_kernel,
        out_shape=(
            jax.ShapeDtypeStruct((CHIPS * LOCALS, 3 * HDIM, CROP), bf),
            jax.ShapeDtypeStruct((rows, width), bf),
            jax.ShapeDtypeStruct((8, CROP), jnp.int32),
        ),
        in_specs=[smem, vmem] + [hbm] * 5,
        out_specs=(hbm, hbm, vmem),
        scratch_shapes=[pltpu.VMEM(v.shape, bf) for v in (emb, cot, w_qk, w_value, w_out)]
        + [
            pltpu.VMEM((2, HEADS, HDIM, CROP), jnp.float32),
            pltpu.VMEM((2, HEADS, HDIM, CROP), jnp.float32),
            pltpu.VMEM((2, HEADS, 2 * HDIM, CROP), bf),
            pltpu.VMEM((2, HEADS, 2 * HDIM, CROP), bf),
            pltpu.VMEM((2, 2, 3 * HDIM, CROP), bf),
            dma((7,)),
            dma((2, HEADS)),
            dma((2, HEADS)),
            dma((2, HEADS)),
            dma((2, HEADS)),
            dma((2,)),
            dma((144,)),
            dma((LOCALS, CHIPS + 2)),
        ],
        compiler_params=pltpu.CompilerParams(
            collective_id=0, has_side_effects=True, vmem_limit_bytes=VMEM_LIMIT
        ),
    )(lengths, pairs, emb, cot, w_qk, w_value, w_out)


def pair_kernel(
    lists_ref, len_ref, first_ref, table_hbm, hid_ref, grad_ref, blocks_ref, own_ref, out_acc, dk_acc, dv_acc, sem, own_sem
):
    counts = [lists_ref[LOCALS + l, 0] for l in range(LOCALS)]
    total = sum((count + 7) // 8 for count in counts)

    def spot(p):
        return (p % 2) * 2 * CHIPS + p // 2

    def partner(group, j):
        return lists_ref[group // 16, (group % 16) * 8 + j]

    def fetch(group, carry):
        for j in range(8):
            pltpu.make_async_copy(
                table_hbm.at[spot(partner(group, j))], blocks_ref.at[group * 8 + j], sem.at[group]
            ).start()
        return carry

    def mine(l):
        return pltpu.make_async_copy(table_hbm.at[spot(first_ref[0] + l)], own_ref.at[l], own_sem.at[l])

    mine(0).start()
    lax.fori_loop(0, total, fetch, 0)
    for l in range(1, LOCALS):
        mine(l).start()
    rows = lax.broadcasted_iota(jnp.int32, (CROP, CROP), 0)
    columns = lax.broadcasted_iota(jnp.int32, (1, CROP), 1)
    done = 0
    for l in range(LOCALS):
        me = first_ref[0] + l
        row_bias = jnp.where(rows < len_ref[me], 0.0, -1e30)
        count = counts[l]
        mine(l).wait()
        own = own_ref[l].astype(jnp.float32)
        kp = own[:HDIM].T.astype(jnp.bfloat16)
        vp = own[HDIM : 2 * HDIM].T.astype(jnp.bfloat16)
        gp = own[2 * HDIM :].T.astype(jnp.bfloat16)
        out_acc[...] = jnp.zeros_like(out_acc)
        dk_acc[...] = jnp.zeros_like(dk_acc)
        dv_acc[...] = jnp.zeros_like(dv_acc)

        def step(base, group, at):
            pltpu.make_async_copy(
                table_hbm.at[pl.ds(0, 8)], blocks_ref.at[pl.ds(at * 8, 8)], sem.at[at]
            ).wait()
            blocks, lens, live = [], [], []
            for j in range(group):
                blocks.append(blocks_ref[at * 8 + j])
                lens.append(len_ref[partner(at, j)])
                live.append(jnp.where(base + j < count, 1.0, 0.0))
            many = jnp.concatenate(blocks, axis=1)
            kq, vq, gq = many[:HDIM], many[HDIM : 2 * HDIM], many[2 * HDIM :]
            scores = jnp.dot(kp, kq, preferred_element_type=jnp.float32)
            d_rows = jnp.dot(gp, vq, preferred_element_type=jnp.float32)
            d_cols = jnp.dot(vp, gq, preferred_element_type=jnp.float32)
            a_parts, b_parts, ds_parts = [], [], []
            for j in range(group):
                part = slice(j * CROP, (j + 1) * CROP)
                s = scores[:, part] * SCALE
                sa = s + jnp.where(columns < lens[j], 0.0, -1e30)
                ea = jnp.exp2(sa - jnp.max(sa, axis=1, keepdims=True))
                a = ea * (live[j] / jnp.sum(ea, axis=1, keepdims=True))
                sb = s + row_bias
                eb = jnp.exp2(sb - jnp.max(sb, axis=0, keepdims=True))
                b = eb * (live[j] / jnp.sum(eb, axis=0, keepdims=True))
                ta = a * d_rows[:, part]
                tb = b * d_cols[:, part]
                ds = (ta - a * jnp.sum(ta, axis=1, keepdims=True)) + (
                    tb - b * jnp.sum(tb, axis=0, keepdims=True)
                )
                a_parts.append(a.astype(jnp.bfloat16))
                b_parts.append(b.astype(jnp.bfloat16))
                ds_parts.append(ds.astype(jnp.bfloat16))
            for acc, parts, other in ((out_acc, a_parts, vq), (dv_acc, b_parts, gq), (dk_acc, ds_parts, kq)):
                acc[...] += lax.dot_general(
                    jnp.concatenate(parts, axis=1), other, NT, preferred_element_type=jnp.float32
                )

        def eight(i, carry):
            step(i * 8, 8, done + i)
            return carry

        def four(i, carry):
            step(big * 8, 4, done + big)
            return carry

        big = (count + 3) // 8
        lax.fori_loop(0, big, eight, 0)
        lax.fori_loop(0, jnp.where(count > big * 8, 1, 0), four, 0)
        done = done + (count + 7) // 8
        ok = rows[:, :HDIM] < len_ref[me]
        hid_ref[l // 2, :, (l % 2) * HDIM : (l % 2 + 1) * HDIM] = jnp.where(ok, out_acc[...], 0.0).astype(
            jnp.bfloat16
        )
        turned = jnp.concatenate([dk_acc[...] * HDIM**-0.5, dv_acc[...]], axis=1).T
        for core in range(2):
            eights = []
            for xd in range(NX):
                at = (xd * 2 + core) * 8
                eights += [turned[at : at + 8], turned[HDIM + at : HDIM + at + 8]]
            grad_ref[core, :, l * CROP : (l + 1) * CROP] = jnp.concatenate(eights, axis=0).astype(jnp.bfloat16)


def pair_call(lists, lengths, first, table):
    smem = pl.BlockSpec(memory_space=pltpu.SMEM)
    vmem = pl.BlockSpec(memory_space=pltpu.VMEM)
    hbm = pl.BlockSpec(memory_space=pl.ANY)
    return pl.pallas_call(
        pair_kernel,
        out_shape=(
            jax.ShapeDtypeStruct((2, CROP, 2 * HDIM), jnp.bfloat16),
            jax.ShapeDtypeStruct((2, HDIM, LOCALS * CROP), jnp.bfloat16),
        ),
        in_specs=[smem, smem, smem, hbm],
        out_specs=(vmem, vmem),
        scratch_shapes=[
            pltpu.VMEM((8 * GROUPS, 3 * HDIM, CROP), jnp.bfloat16),
            pltpu.VMEM((LOCALS, 3 * HDIM, CROP), jnp.bfloat16),
            pltpu.VMEM((CROP, HDIM), jnp.float32),
            pltpu.VMEM((CROP, HDIM), jnp.float32),
            pltpu.VMEM((CROP, HDIM), jnp.float32),
            pltpu.SemaphoreType.DMA((GROUPS,)),
            pltpu.SemaphoreType.DMA((LOCALS,)),
        ],
        compiler_params=pltpu.CompilerParams(vmem_limit_bytes=VMEM_LIMIT),
    )(lists, lengths, first, table)


def ring_sum(n, term, plus, minus, send, recv, ssem, rsem, done):
    steps = n // 2
    half = send.shape[-1] // 2
    sent = []
    for s in range(steps):
        d = steps - s
        for way, to in ((0, plus), (1, minus)):
            own = slice(way * half, (way + 1) * half)
            rest = slice((1 - way) * half, (2 - way) * half)
            value = term(d if way == 0 else n - d)
            if s > 0:
                landing = recv.at[way, s - 1, :, own] if s == 1 else recv.at[way, s - 1]
                remote(landing, landing, ssem.at[way, s - 1], rsem.at[way, s - 1], to).wait_recv()
            send[way, s, :, own] = (
                value[:, own] if s == 0 else value[:, own] + recv[way, s - 1, :, own].astype(jnp.float32)
            ).astype(jnp.bfloat16)
            if s == 1:
                send[way, s, :, rest] = value[:, rest].astype(jnp.bfloat16)
            elif s > 1:
                send[way, s, :, rest] = (
                    value[:, rest] + recv[way, s - 1, :, rest].astype(jnp.float32)
                ).astype(jnp.bfloat16)
            spot = own if s == 0 else slice(None)
            copy = remote(
                send.at[way, s, :, spot], recv.at[way, s, :, spot], ssem.at[way, s], rsem.at[way, s], to
            )
            copy.start()
            sent.append(copy)
        yield
    total = term(0)
    for way, to in ((0, plus), (1, minus)):
        landing = recv.at[way, steps - 1]
        remote(landing, landing, ssem.at[way, steps - 1], rsem.at[way, steps - 1], to).wait_recv()
        total = total + recv[way, steps - 1].astype(jnp.float32)
    done(total)
    for copy in sent:
        copy.wait_send()
    yield


def line_sum(term, ways, send, recv, ssem, rsem, done):
    half = send.shape[-1] // 2
    whole = slice(None)
    sent = []

    def copy(way, s, spot, to):
        return remote(send.at[way, s, :, spot], recv.at[way, s, :, spot], ssem.at[way, s], rsem.at[way, s], to)

    def go(way, s, spot, to):
        sent.append(copy(way, s, spot, to))
        sent[-1].start()

    def got(way, s, spot):
        copy(way, s, spot, ways[way][0]).wait_recv()
        return recv[way, s, :, spot].astype(jnp.float32)

    for way, (one, two) in enumerate(ways):
        own = slice(way * half, (way + 1) * half)
        send[way, 0, :, own] = term(4)[:, own].astype(jnp.bfloat16)
        go(way, 0, own, two)
        send[way, 1] = term(3 if way == 0 else 5).astype(jnp.bfloat16)
        go(way, 1, whole, one)
    yield
    for way, (one, two) in enumerate(ways):
        own = slice(way * half, (way + 1) * half)
        rest = slice((1 - way) * half, (2 - way) * half)
        value = term(2 if way == 0 else 6) + got(way, 1, whole)
        send[way, 2, :, rest] = value[:, rest].astype(jnp.bfloat16)
        send[way, 2, :, own] = (value[:, own] + got(way, 0, own)).astype(jnp.bfloat16)
        go(way, 2, whole, one)
    yield
    for way, (one, two) in enumerate(ways):
        send[way, 3] = (term(1 if way == 0 else 7) + got(way, 2, whole)).astype(jnp.bfloat16)
        go(way, 3, whole, one)
    yield
    done(term(0) + got(0, 3, whole) + got(1, 3, whole))
    for one in sent:
        one.wait_send()
    yield


def together(*rings):
    live = list(rings)
    while live:
        for one in list(live):
            if next(one, 1) == 1:
                live.remove(one)


def finish_kernel(
    hid_ref, grad_ref, emb_hbm, sib_hbm, wo_hbm, att_hbm, qk_ref, value_ref,
    emb, sib, wo, hidden, att, hid_recv, g_recv, terms, z_send, z_recv, x_send, x_recv, line, last_send, last_recv,
    lsem, h_ssem, h_rsem, g_ssem, g_rsem, zs_sem, zr_sem, xs_sem, xr_sem, ls_sem, lr_sem,
):
    z, x, c, y = place()
    col = column_of(x, c)
    kept = c == x // 2
    mine = 2 * y + x // 2
    loads = [pltpu.make_async_copy(emb_hbm, emb, lsem.at[0]), pltpu.make_async_copy(sib_hbm, sib, lsem.at[1])]
    fetch = pltpu.make_async_copy(wo_hbm, wo, lsem.at[2])
    store = pltpu.make_async_copy(att, att_hbm, lsem.at[3])
    for load in loads:
        load.start()
    fetch.start()
    sibling = device(z, x, 1 - c, y)
    up, down = device((z + 1) % NZ, x, c, y), device((z + NZ - 1) % NZ, x, c, y)
    east, west = device(z, (x + 1) % NX, c, y), device(z, (x + NX - 1) % NX, c, y)
    near = [device(z, x, cd, (y + d) % NY) for d in (1, 2, 3) for cd in (0, 1)] + [sibling]
    near += [device(z, NX - 1 - x, cd, (y + d) % NY) for d in range(NY) for cd in (0, 1)]
    near += [device(z, (x + d) % NX, c, y) for d in range(1, NX)]
    near += [device((z + d) % NZ, x, c, y) for d in range(1, NZ)]
    greet(near)

    ways = [(d, cd) for d in (2, 1, 3, 0) for cd in (0, 1)]

    def outgoing(d, cd, kind):
        yd = (y + d) % NY
        slot = yd * 2 + cd
        to = device(z, col, cd, yd)
        if kind == 0:
            return remote(grad_ref.at[cd], g_recv.at[mine], g_ssem.at[slot], g_rsem.at[mine], to)
        return remote(hid_ref.at[cd], hid_recv.at[mine], h_ssem.at[slot], h_rsem.at[mine], to)

    def away(d, cd):
        return jnp.logical_not(kept & (cd == c)) if d == 0 else None

    def launch(kind):
        for d, cd in ways:
            if d:
                outgoing(d, cd, kind).start()
            else:

                @pl.when(away(d, cd))
                def _():
                    outgoing(d, cd, kind).start()

    launch(0)

    @pl.when(kept)
    def _():
        g_recv[mine] = grad_ref[c]
        hid_recv[mine] = hid_ref[c]

    def arrive(ref, ss, rs):
        def one(slot, carry):
            @pl.when(jnp.logical_not(kept & (slot == mine)))
            def _():
                remote(ref.at[slot], ref.at[slot], ss.at[slot], rs.at[slot], sibling).wait_recv()

            return carry

        lax.fori_loop(0, HEADS, one, 0)

    for load in loads:
        load.wait()
    arrive(g_recv, g_ssem, g_rsem)
    launch(1)
    width = emb.shape[-1]
    all_g = g_recv[...].reshape(HEADS * HDIM, LOCALS * CROP)
    own = jnp.where(c == 0, all_g[:, : 2 * CROP], all_g[:, 2 * CROP :])
    theirs = jnp.where(c == 0, all_g[:, 2 * CROP :], all_g[:, : 2 * CROP])
    terms[...] = (
        jnp.dot(own, emb[...], preferred_element_type=jnp.float32)
        + jnp.dot(theirs, sib[...], preferred_element_type=jnp.float32)
    ).reshape(terms.shape)

    def heads():
        arrive(hid_recv, h_ssem, h_rsem)
        low = lax.broadcasted_iota(jnp.int32, (CROP, 2 * HDIM), 1) < HDIM
        for yy in range(NY):
            even = hid_recv[2 * yy].astype(jnp.float32)
            odd = hid_recv[2 * yy + 1].astype(jnp.float32)
            at = slice(yy * 2 * HDIM, (yy + 1) * 2 * HDIM)
            hidden[:CROP, at] = jnp.where(low, even, pltpu.roll(odd, HDIM, 1)).astype(jnp.bfloat16)
            hidden[CROP:, at] = jnp.where(low, pltpu.roll(even, HDIM, 1), odd).astype(jnp.bfloat16)
        fetch.wait()
        att[...] = jnp.dot(hidden[...], wo[...], preferred_element_type=jnp.float32).astype(jnp.bfloat16)
        store.start()

    def last(d, to):
        return remote(last_send.at[d], last_recv.at[d], ls_sem.at[d], lr_sem.at[d], to)

    def finish(n, term, to, sent=False):
        sends = []
        for d in sorted(range(1, n), key=lambda d: -min(d, n - d)):
            copy = last(d, to(d))
            if not sent:
                last_send[d] = term(d).astype(jnp.bfloat16)
                copy.start()
            sends.append(copy)
        heads()
        total = term(0)
        for copy in sends:
            copy.wait_recv()
        for d in range(1, n):
            total = total + last_recv[d].astype(jnp.float32)
        qk_ref[...] = total[:8]
        value_ref[...] = total[8:]
        for copy in sends:
            copy.wait_send()

    @pl.when(c == 0)
    def _():
        def ring(i):
            def done(total):
                line[i] = total
                d = (i + NX - x) % NX

                @pl.when(d != 0)
                def _():
                    last_send[d] = total.astype(jnp.bfloat16)
                    last(d, device(z, i, c, y)).start()

            return line_sum(
                lambda d: terms[(z + d) % NZ, i],
                ((up, device((z + 2) % NZ, x, c, y)), (down, device((z + NZ - 2) % NZ, x, c, y))), z_send.at[i], z_recv.at[i], zs_sem.at[i], zr_sem.at[i], done,
            )

        together(*[ring(i) for i in range(NX)])
        finish(NX, lambda d: line[(x + d) % NX], lambda d: device(z, (x + d) % NX, c, y), sent=True)

    @pl.when(c == 1)
    def _():
        def ring(i):
            def done(total):
                line[4 * i : 4 * i + 4] = total.reshape(4, 16, width)

            return ring_sum(
                NX,
                lambda d: terms[4 * i : 4 * i + 4, (x + d) % NX].reshape(64, width),
                east, west, x_send.at[i], x_recv.at[i], xs_sem.at[i], xr_sem.at[i], done,
            )

        together(ring(0), ring(1))
        finish(NZ, lambda d: line[(z + d) % NZ], lambda d: device((z + d) % NZ, x, c, y))

    store.wait()
    for d, cd in ways:
        for kind in (0, 1):
            if d:
                outgoing(d, cd, kind).wait_send()
            else:

                @pl.when(away(d, cd))
                def _():
                    outgoing(d, cd, kind).wait_send()


def finish_call(hid, grads, emb, sib, w_out):
    rows, width = emb.shape
    vmem = pl.BlockSpec(memory_space=pltpu.VMEM)
    hbm = pl.BlockSpec(memory_space=pl.ANY)
    dma = pltpu.SemaphoreType.DMA
    bf = jnp.bfloat16
    return pl.pallas_call(
        finish_kernel,
        out_shape=(
            jax.ShapeDtypeStruct((rows, width), bf),
            jax.ShapeDtypeStruct((8, width), jnp.float32),
            jax.ShapeDtypeStruct((8, width), jnp.float32),
        ),
        in_specs=[vmem, vmem, hbm, hbm, hbm],
        out_specs=(hbm, vmem, vmem),
        scratch_shapes=[
            pltpu.VMEM((rows, width), bf),
            pltpu.VMEM((rows, width), bf),
            pltpu.VMEM(w_out.shape, bf),
            pltpu.VMEM((rows, w_out.shape[0]), bf),
            pltpu.VMEM((rows, width), bf),
            pltpu.VMEM((HEADS, CROP, 2 * HDIM), bf),
            pltpu.VMEM((HEADS, HDIM, LOCALS * CROP), bf),
            pltpu.VMEM((NZ, NX, 16, width), jnp.float32),
            pltpu.VMEM((NX, 2, NZ // 2, 16, width), bf),
            pltpu.VMEM((NX, 2, NZ // 2, 16, width), bf),
            pltpu.VMEM((2, 2, NX // 2, 64, width), bf),
            pltpu.VMEM((2, 2, NX // 2, 64, width), bf),
            pltpu.VMEM((NZ, 16, width), jnp.float32),
            pltpu.VMEM((NZ, 16, width), bf),
            pltpu.VMEM((NZ, 16, width), bf),
            dma((4,)),
            dma((HEADS,)),
            dma((HEADS,)),
            dma((HEADS,)),
            dma((HEADS,)),
            dma((NX, 2, NZ // 2)),
            dma((NX, 2, NZ // 2)),
            dma((2, 2, NX // 2)),
            dma((2, 2, NX // 2)),
            dma((NZ,)),
            dma((NZ,)),
        ],
        compiler_params=pltpu.CompilerParams(
            collective_id=1, has_side_effects=True, vmem_limit_bytes=VMEM_LIMIT
        ),
    )(hid, grads, emb, sib, w_out)


def output_kernel(att_ref, qk_ref, value_ref, out_att_ref, out_qk_ref, out_value_ref, att, qk, value, sem):
    rows = att.shape[0] // PIECES
    moves = [(qk_ref, qk, out_qk_ref), (value_ref, value, out_value_ref)]
    for i in range(PIECES):
        part = pl.ds(i * rows, rows)
        moves.append((att_ref.at[part], att.at[part], out_att_ref.at[part]))
    come = [pltpu.make_async_copy(src, mid, sem.at[0, i]) for i, (src, mid, dst) in enumerate(moves)]
    go = [pltpu.make_async_copy(mid, dst, sem.at[1, i]) for i, (src, mid, dst) in enumerate(moves)]
    for copy in come:
        copy.start()
    for first, then in zip(come, go):
        first.wait()
        then.start()
    for copy in go:
        copy.wait()


def output_call(*results):
    hbm = pl.BlockSpec(memory_space=pl.ANY)
    return pl.pallas_call(
        output_kernel,
        out_shape=tuple(jax.ShapeDtypeStruct(v.shape, v.dtype) for v in results),
        in_specs=[hbm] * 3,
        out_specs=(hbm,) * 3,
        scratch_shapes=[pltpu.VMEM(v.shape, v.dtype) for v in results]
        + [pltpu.SemaphoreType.DMA((2, PIECES + 2))],
        compiler_params=pltpu.CompilerParams(vmem_limit_bytes=VMEM_LIMIT),
    )(*results)


def on_device(embeddings, cotangent, w_qk, w_value, w_out, lengths, pair_list):
    owned, crop, width = embeddings.shape
    rows = owned * crop
    emb = embeddings.reshape(rows, width)
    z, x, c, _ = place()
    first = LOCALS * (z * NX + column_of(x, c))
    table, sib, lists = gather_call(
        lengths, pair_list.T, emb, cotangent.reshape(rows, width), w_qk, w_value, w_out
    )
    hid, grads = pair_call(lists, lengths, first.reshape(1), table)
    attended, grad_qk, grad_value = output_call(*finish_call(hid, grads, emb, sib, w_out))
    return (attended.reshape(embeddings.shape), grad_qk.T, grad_value.T)


def solution(mesh):
    in_specs = (
        P("pairs", None, "mp"),
        P("pairs", None, "mp"),
        P("mp", None),
        P("mp", None),
        P(None, "mp"),
        P(),
        P(),
    )
    out_specs = (P("pairs", None, "mp"), P("mp", "pairs"), P("mp", "pairs"))
    return jax.shard_map(on_device, mesh=mesh, in_specs=in_specs, out_specs=out_specs, check_vma=False)
```
